32 devices in a mesh: row: 8 (over y, x, core), col: 4 (over z).
Axes of the slice: x: 2, y: 2, z: 4, core: 2. Of those that a mesh axis runs over, the one named last changes fastest.
Arguments:
- a_blocks: bfloat16 [64, 16, 128, 128], P('row', 'col'), may hold values from -0.125 to 0.125
- a_mask: int32 [64, 16], P('row', 'col'), may hold values 0 or 1
- b_blocks: bfloat16 [32, 32, 128, 128], P('row', 'col'), may hold values from -6 to 6
- b_mask: int32 [32, 32], P('row', 'col'), may hold values 0 or 1
- c_mask: int32 [64, 32], P('row', 'col'), may hold values 0 or 1
Outputs:
- product: bfloat16 [64, 32, 128, 128], P('row', 'col')
The draws below stay inside these ranges and needn't reach their ends.
All inputs are finite; a program needn't handle non-finite values. No bound on the sum of `a_mask` or of `b_mask` or of `c_mask` on one device may be relied on, other than what follows from the above.
Results may differ from the reference program's by a relative error of at most 0.001.
Values may be sent and summed in bfloat16 or wider, within the bound.
No kernel may reach another device: no remote copies, remote signals or barrier semaphores. Data moves between devices by JAX's collectives and lax.ppermute only.
A program may use at most 64 MiB of HBM per device.

```python
import jax
import jax.numpy as jnp
from jax import lax

BLK = 128
BR = 8
KB = 4
BC = 8
STEPS = 4
ROWS_BLK = 64
COLS_BLK = 32
KA_BLK = 16
KBR_BLK = 32
N_ROW = 8
N_COL = 4


def touch_ends(result, rng, smallest, largest):
    longest = result.shape.index(max(result.shape))
    spots = []
    for shift in (0, 1):
        where = [jax.random.randint(jax.random.fold_in(rng, axis), (), 0, length) for axis, length in enumerate(result.shape)]
        where[longest] = (where[longest] + shift) % result.shape[longest]
        spots.append(tuple(where))
    return result.at[spots[0]].set(smallest).at[spots[1]].set(largest)


def block_levels(key, dims, shards, low, top_value):
    def one(dim, shards_of):
        draws = jax.random.uniform(jax.random.fold_in(jax.random.fold_in(key, 6), dim), (shards_of,), jnp.float32, low / len(shards), top_value / len(shards))
        return jnp.repeat(jnp.exp(draws), dims[dim] // shards_of).reshape((-1,) + (1,) * (len(dims) - dim - 1))

    gain = one(*shards[0])
    for cut in shards[1:]:
        gain = gain * one(*cut)
    return gain


def bell_draw(own_key, extent, deviation, most, pieces=(), held_as=jnp.bfloat16):
    result = jax.random.normal(own_key, extent, jnp.float32) * deviation
    if len(pieces) > 0:
        result = block_levels(own_key, extent, pieces, -0.22, 0.18) * result
    return jnp.clip(result, min=-most, max=most).astype(held_as)


def setup_inputs(seed: int = 0) -> dict:
    key_list = jax.random.split(jax.random.key(seed), 6)
    return {
        "a_blocks": bell_draw(key_list[0], (ROWS_BLK, KA_BLK, BLK, BLK), (STEPS * KB * BLK) ** -0.5, 0.125, ((0, 8), (1, 4))),
        "a_mask": touch_ends((jax.random.randint(key_list[1], (ROWS_BLK, KA_BLK), 0, 5) < 3).astype(jnp.int32), jax.random.fold_in(key_list[1], 1), 0, 1),
        "b_blocks": bell_draw(key_list[2], (KBR_BLK, COLS_BLK, BLK, BLK), 1.0, 6.0, ((0, 8), (1, 4))),
        "b_mask": touch_ends((jax.random.randint(key_list[3], (KBR_BLK, COLS_BLK), 0, 5) < 3).astype(jnp.int32), jax.random.fold_in(key_list[3], 1), 0, 1),
        "c_mask": touch_ends((jax.random.randint(key_list[4], (ROWS_BLK, COLS_BLK), 0, 5) < 4).astype(jnp.int32), jax.random.fold_in(key_list[4], 1), 0, 1),
    }


def reference(a_blocks, a_mask, b_blocks, b_mask, c_mask):
    a_live = a_blocks * a_mask[:, :, None, None].astype(jnp.bfloat16)
    b_live = b_blocks * b_mask[:, :, None, None].astype(jnp.bfloat16)
    a_five = a_live.reshape(N_ROW, BR, N_COL, KB, BLK, BLK)
    b_five = b_live.reshape(N_ROW, KB, N_COL, BC, BLK, BLK)

    def one_panel(panel):
        a_row = a_five[panel].astype(jnp.float32)
        total = jnp.zeros((BR, N_COL, BC, BLK, BLK), jnp.float32)
        for step in range(STEPS):
            a_step = jnp.roll(a_row, -step, axis=1)
            b_step = b_five[(panel + step) % N_ROW].astype(jnp.float32)
            total = total + jnp.einsum("ickxy,kcjyz->icjxz", a_step, b_step, precision=lax.Precision.HIGHEST)
        return total

    total = lax.map(one_panel, jnp.arange(N_ROW, dtype=jnp.int32))
    total = total.reshape(N_ROW * BR, N_COL * BC, BLK, BLK)
    keep = c_mask[:, :, None, None].astype(jnp.float32)
    return (total * keep).astype(jnp.bfloat16)
```

```python
import functools

import jax
import jax.numpy as jnp
from jax import lax
from jax.experimental import pallas as pl
from jax.experimental.pallas import tpu as pltpu
from jax.sharding import PartitionSpec as P

STEPS = 4
HALVES = 2


def from_behind(array, axis, by):
    size = lax.axis_size(axis)
    return lax.ppermute(array, axis, [(i, (i + by) % size) for i in range(size)])


def wide(a_refs, rows):
    kb = a_refs[0].shape[1]
    blk = a_refs[0].shape[-1]
    columns = []
    for k in range(kb):
        columns.append(jnp.concatenate([a[:, k].reshape(-1, blk) for a in a_refs], axis=0))
    return jnp.concatenate(columns, axis=1)


def tall(b_ref):
    kb, bc = b_ref.shape[:2]
    return jnp.concatenate(
        [jnp.concatenate([b_ref[k, j] for j in range(bc)], axis=1) for k in range(kb)], axis=0
    )


def first_kernel(steps, *refs):
    a_refs, b_refs, acc_ref = refs[: HALVES * steps], refs[HALVES * steps : -1], refs[-1]
    total = None
    for t in range(steps):
        part = jnp.dot(
            wide(a_refs[HALVES * t : HALVES * (t + 1)], None), tall(b_refs[t]), preferred_element_type=jnp.float32
        )
        total = part if total is None else total + part
    acc_ref[...] = total


def last_kernel(c_ref, acc_ref, *refs):
    a_refs, b_ref, out_ref = refs[:HALVES], refs[HALVES], refs[-1]
    blk = out_ref.shape[-1]
    total = acc_ref[...] + jnp.dot(wide(a_refs, None), tall(b_ref), preferred_element_type=jnp.float32)
    j0 = pl.program_id(0) * out_ref.shape[1]
    for i in range(out_ref.shape[0]):
        for j in range(out_ref.shape[1]):
            keep = c_ref[i, j0 + j].astype(jnp.float32)
            out_ref[i, j] = (total[i * blk : (i + 1) * blk, j * blk : (j + 1) * blk] * keep).astype(out_ref.dtype)


def on_device(a_blocks, a_mask, b_blocks, b_mask, c_mask):
    br, kb, blk, _ = a_blocks.shape
    bc = b_blocks.shape[1]
    a_live = a_blocks * a_mask[:, :, None, None].astype(jnp.bfloat16)
    b_live = b_blocks * b_mask[:, :, None, None].astype(jnp.bfloat16)
    size = br // HALVES
    left = [[a_live[h * size : (h + 1) * size] for h in range(HALVES)]]
    right = [b_live]
    for step in range(1, STEPS):
        left.append([from_behind(part, "col", -1) for part in left[-1]])
        right.append(from_behind(right[-1], "row", -1))

    wide_j = 2
    grid = (bc // wide_j,)
    a_spec = pl.BlockSpec((size, kb, blk, blk), lambda g: (0, 0, 0, 0))
    b_spec = pl.BlockSpec((kb, wide_j, blk, blk), lambda g: (0, g, 0, 0))
    acc_spec = pl.BlockSpec((br * blk, wide_j * blk), lambda g: (0, g))
    done = STEPS - 1
    acc = pl.pallas_call(
        functools.partial(first_kernel, done),
        grid=grid,
        in_specs=[a_spec] * (HALVES * done) + [b_spec] * done,
        out_specs=acc_spec,
        out_shape=jax.ShapeDtypeStruct((br * blk, bc * blk), jnp.float32),
        compiler_params=pltpu.CompilerParams(vmem_limit_bytes=40 * 1024 * 1024),
        cost_estimate=pl.CostEstimate(flops=2 * br * blk * bc * blk * kb * blk * done, bytes_accessed=10 << 20, transcendentals=0),
    )(*[part for parts in left[:done] for part in parts], *right[:done])
    return pl.pallas_call(
        last_kernel,
        grid=grid,
        in_specs=[pl.BlockSpec(memory_space=pltpu.SMEM), acc_spec] + [a_spec] * HALVES + [b_spec],
        out_specs=pl.BlockSpec((br, wide_j, blk, blk), lambda g: (0, g, 0, 0)),
        out_shape=jax.ShapeDtypeStruct((br, bc, blk, blk), jnp.bfloat16),
        compiler_params=pltpu.CompilerParams(vmem_limit_bytes=40 * 1024 * 1024),
        cost_estimate=pl.CostEstimate(flops=2 * br * blk * bc * blk * kb * blk, bytes_accessed=8 << 20, transcendentals=0),
    )(c_mask, acc, *left[done], right[done])


def solution(mesh):
    return jax.shard_map(
        on_device,
        mesh=mesh,
        in_specs=(
            P("row", "col", None, None),
            P("row", "col"),
            P("row", "col", None, None),
            P("row", "col"),
            P("row", "col"),
        ),
        out_specs=P("row", "col", None, None),
        check_vma=False,
    )
```

```python
import functools

import jax
import jax.numpy as jnp
from jax import lax
from jax.experimental import pallas as pl
from jax.experimental.pallas import tpu as pltpu
from jax.sharding import PartitionSpec as P

STEPS = 4
END_CHUNKS = 9
MID_CHUNKS = 7
VMEM = 48 * 1024 * 1024


def from_behind(array, axis, by):
    size = lax.axis_size(axis)
    return lax.ppermute(array, axis, [(i, (i + by) % size) for i in range(size)])


def smem():
    return pl.BlockSpec(memory_space=pltpu.SMEM)


def whole():
    return pl.BlockSpec(memory_space=pltpu.VMEM)


def params():
    return pltpu.CompilerParams(vmem_limit_bytes=VMEM)


def cost(flops, nbytes):
    return pl.CostEstimate(flops=int(flops), bytes_accessed=int(nbytes), transcendentals=0)


def wide(a_ref):
    kb, blk = a_ref.shape[1], a_ref.shape[-1]
    return jnp.concatenate([a_ref[:, k].reshape(-1, blk) for k in range(kb)], axis=1)


def tall(b_ref):
    kb, bc = b_ref.shape[:2]
    return jnp.concatenate(
        [jnp.concatenate([b_ref[k, j] for j in range(bc)], axis=1) for k in range(kb)], axis=0
    )


def dense_kernel(c_ref, *refs):
    a_refs, b_refs, out_ref = refs[:STEPS], refs[STEPS:-1], refs[-1]
    total = None
    for a_ref, b_ref in zip(a_refs, b_refs):
        part = jnp.dot(wide(a_ref), tall(b_ref), preferred_element_type=jnp.float32)
        total = part if total is None else total + part
    blk = out_ref.shape[-1]
    j0 = pl.program_id(0) * out_ref.shape[1]
    for i in range(out_ref.shape[0]):
        for j in range(out_ref.shape[1]):
            keep = c_ref[i, j0 + j].astype(jnp.float32)
            out_ref[i, j] = (total[i * blk : (i + 1) * blk, j * blk : (j + 1) * blk] * keep).astype(out_ref.dtype)


def dense_product(a_live, right, c_mask):
    br, kb, blk, _ = a_live.shape
    bc = right[0].shape[1]
    left = [a_live]
    for _ in range(1, STEPS):
        left.append(from_behind(left[-1], "col", -1))
    wide_j = 2 if bc % 2 == 0 else 1
    return pl.pallas_call(
        dense_kernel,
        grid=(bc // wide_j,),
        in_specs=[smem()]
        + [pl.BlockSpec((br, kb, blk, blk), lambda g: (0, 0, 0, 0))] * STEPS
        + [pl.BlockSpec((kb, wide_j, blk, blk), lambda g: (0, g, 0, 0))] * STEPS,
        out_specs=pl.BlockSpec((br, wide_j, blk, blk), lambda g: (0, g, 0, 0)),
        out_shape=jax.ShapeDtypeStruct((br, bc, blk, blk), jnp.bfloat16),
        compiler_params=params(),
        cost_estimate=cost(2 * STEPS * br * bc * kb * blk**3, 10 << 20),
    )(c_mask, *left, *right)


def compact_kernel(mask_ref, a_ref, head0_ref, head1_ref, tail_ref, n_ref, list_ref):
    br, kb = a_ref.shape[:2]
    quarter = br * kb // 4
    count = jnp.int32(0)
    for k in range(kb):
        for i in range(br):
            list_ref[count] = a_ref[i, k]
            count = count + mask_ref[i, k]
    head0_ref[...] = list_ref[0:quarter]
    head1_ref[...] = list_ref[quarter : 2 * quarter]
    tail_ref[...] = list_ref[2 * quarter : 4 * quarter]
    n_ref[0] = jnp.maximum(count, 2 * quarter)


def relay_own_kernel(chunk, sides, n_ref, tail_ref, *refs):
    ins, outs, line = refs[: sides * (chunk - 1)], refs[sides * (chunk - 1) : -1], refs[-1]
    quarter = outs[0].shape[0]
    at = n_ref[0] - 2 * quarter
    for side, out_ref in enumerate(outs):
        line[0 : 2 * quarter] = tail_ref[...]
        for c, ref in enumerate(ins[side * (chunk - 1) : (side + 1) * (chunk - 1)]):
            line[pl.ds(at + c * quarter, quarter)] = ref[...]
        out_ref[...] = line[(chunk - 2) * quarter : (chunk - 1) * quarter]


def relay_kernel(sides, n_ref, *refs):
    ins, outs, line = refs[: 3 * sides], refs[3 * sides : -1], refs[-1]
    quarter = outs[0].shape[0]
    at = 4 * quarter - n_ref[0]
    for side, out_ref in enumerate(outs):
        for c in range(3):
            line[c * quarter : (c + 1) * quarter] = ins[3 * side + c][...]
        out_ref[...] = line[pl.ds(at, quarter)]


def table_kernel(where_ref, mask_ref, end_ref, mid_ref, over_ref):
    blocks = mask_ref.shape[1]
    none = STEPS * blocks
    z = where_ref[0]
    at_end = jnp.logical_or(z == 0, z == 3)
    near = 1 + 2 * (z % 2)

    def clear(ref):
        def body(p, carry):
            ref[p] = none
            return carry

        lax.fori_loop(0, ref.shape[0], body, 0)

    def fill(ref, base, step, there):
        def body(b, count):
            ref[count] = step * blocks + b
            return count + mask_ref[step, b]

        count = lax.fori_loop(0, jnp.where(there, blocks, 0), body, base)
        ref[count] = none
        return jnp.where(there, jnp.maximum(count, base + blocks // 2), base)

    clear(end_ref)
    clear(mid_ref)
    base = fill(end_ref, jnp.int32(0), near, True)
    base = fill(end_ref, base, 2, at_end)
    fill(end_ref, base, 4 - near, at_end)
    base = fill(mid_ref, jnp.int32(0), 4 - near, jnp.logical_not(at_end))
    fill(mid_ref, base, 2, jnp.logical_not(at_end))

    def count_of(slab):
        step = (slab - z + 4) % 4
        total = lax.fori_loop(0, blocks, lambda b, total: total + mask_ref[step, b], jnp.int32(0))
        return jnp.maximum(total, blocks // 2)

    n = [count_of(slab) for slab in range(4)]
    end = n[0] + n[1] + n[2] + n[3] - jnp.minimum(n[0], n[3])
    mid = jnp.maximum(n[0] + n[1], n[2] + n[3])
    quarter = blocks // 4
    over = jnp.logical_or(end > END_CHUNKS * quarter, mid > MID_CHUNKS * quarter)
    over_ref[0] = jnp.where(over, 1, 0).astype(jnp.int32)


def early_kernel(n_end, n_mid, mask_ref, end_ref, mid_ref, a_ref, *refs):
    ends, refs = refs[:n_end], refs[n_end:]
    mids, refs = refs[:n_mid], refs[n_mid:]
    b_refs, acc_ref, left_ref = refs[:STEPS], refs[STEPS], refs[STEPS + 1]
    br, kb, blk, _ = a_ref.shape
    quarter = ends[0].shape[0]

    @pl.when(pl.program_id(0) == 0)
    def _():
        for k in range(kb):
            for i in range(br):
                left_ref[i * blk : (i + 1) * blk, k * blk : (k + 1) * blk] = a_ref[i, k] * mask_ref[i, k].astype(
                    jnp.float32
                ).astype(jnp.bfloat16)
        left_ref[:, kb * blk :] = jnp.zeros((br * blk, left_ref.shape[1] - kb * blk), jnp.bfloat16)
        for table, chunks in ((end_ref, ends), (mid_ref, mids)):
            for c, chunk in enumerate(chunks):
                for b in range(quarter):
                    place = table[c * quarter + b]
                    row = pl.multiple_of((place % br) * blk, blk)
                    column = pl.multiple_of((place // br) * blk, blk)
                    left_ref[pl.ds(row, blk), pl.ds(column, blk)] = chunk[b]

    total = None
    for t in range(STEPS):
        part = jnp.dot(
            left_ref[:, t * kb * blk : (t + 1) * kb * blk], tall(b_refs[t]), preferred_element_type=jnp.float32
        )
        total = part if total is None else total + part
    acc_ref[...] = total


def late_kernel(first, where_ref, c_ref, end_ref, late_ref, acc_ref, b1_ref, b3_ref, out_ref, b_ref, sum_ref, sem):
    i = pl.program_id(0)
    bc, blk = out_ref.shape[1], out_ref.shape[-1]
    kb = b_ref.shape[0]
    br = pl.num_programs(0)
    z = where_ref[0]

    @pl.when(i == 0)
    def _():
        @pl.when(z < 2)
        def _():
            copy = pltpu.make_async_copy(b3_ref, b_ref, sem)
            copy.start()
            copy.wait()

        @pl.when(z >= 2)
        def _():
            copy = pltpu.make_async_copy(b1_ref, b_ref, sem)
            copy.start()
            copy.wait()

    sum_ref[...] = acc_ref[...]
    for b in range(late_ref.shape[0]):
        place = end_ref[first + b]

        @pl.when(jnp.logical_and(place < STEPS * kb * br, place % br == i))
        def _():
            k = (place // br) % kb
            row = jnp.concatenate([b_ref[k, j] for j in range(bc)], axis=1)
            sum_ref[...] += jnp.dot(late_ref[b], row, preferred_element_type=jnp.float32)

    for j in range(bc):
        keep = c_ref[i, j].astype(jnp.float32)
        out_ref[0, j] = (sum_ref[:, j * blk : (j + 1) * blk] * keep).astype(out_ref.dtype)


def sparse_product(a_blocks, a_mask, right, c_mask):
    br, kb, blk, _ = a_blocks.shape
    bc = right[0].shape[1]
    blocks = br * kb
    quarter = blocks // 4
    z = lax.axis_index("col").astype(jnp.int32).reshape(1)
    chunk_shape = jax.ShapeDtypeStruct((quarter, blk, blk), a_blocks.dtype)
    chunk_bytes = quarter * blk * blk * 2

    def end_swap(x):
        return lax.ppermute(x, "col", [(0, 1), (1, 0), (2, 3), (3, 2)])

    def mid_swap(x):
        return lax.ppermute(x, "col", [(1, 2), (2, 1)])

    head0, head1, tail, n = pl.pallas_call(
        compact_kernel,
        in_specs=[smem(), whole()],
        out_specs=[whole(), whole(), whole(), smem()],
        out_shape=[
            chunk_shape,
            chunk_shape,
            jax.ShapeDtypeStruct((2 * quarter, blk, blk), a_blocks.dtype),
            jax.ShapeDtypeStruct((1,), jnp.int32),
        ],
        scratch_shapes=[pltpu.VMEM((blocks, blk, blk), a_blocks.dtype)],
        compiler_params=params(),
        cost_estimate=cost(0, 8 * chunk_bytes),
        name="compact",
    )(a_mask, a_blocks)

    ends = [end_swap(head0)]
    mids = [mid_swap(head0)]
    ends.append(end_swap(head1))
    mids.append(mid_swap(head1))

    masks = [a_mask] + [from_behind(a_mask, "col", -t) for t in range(1, STEPS)]
    by_column = jnp.stack([m.T.reshape(blocks) for m in masks])
    end_table, mid_table, over = pl.pallas_call(
        table_kernel,
        in_specs=[smem(), smem()],
        out_specs=[smem(), smem(), smem()],
        out_shape=[
            jax.ShapeDtypeStruct((3 * blocks + 8,), jnp.int32),
            jax.ShapeDtypeStruct((2 * blocks + 8,), jnp.int32),
            jax.ShapeDtypeStruct((1,), jnp.int32),
        ],
        compiler_params=params(),
        name="table",
    )(z, by_column)
    rows = lax.axis_size("row")
    bit = 1
    while bit < rows:
        over = jnp.maximum(over, lax.ppermute(over, "row", [(i, i ^ bit) for i in range(rows)]))
        bit *= 2

    for chunk in range(2, END_CHUNKS):
        to_mid = chunk < MID_CHUNKS
        sides = 2 if to_mid else 1
        if chunk < 4:
            kernel = functools.partial(relay_own_kernel, chunk, sides)
            ins = [tail] + mids[: chunk - 1] + (ends[: chunk - 1] if to_mid else [])
            length = 2 + chunk - 1
        else:
            kernel = functools.partial(relay_kernel, sides)
            ins = mids[chunk - 4 : chunk - 1] + (ends[chunk - 4 : chunk - 1] if to_mid else [])
            length = 3
        outs = pl.pallas_call(
            kernel,
            in_specs=[smem()] + [whole()] * len(ins),
            out_specs=[whole()] * sides,
            out_shape=[chunk_shape] * sides,
            scratch_shapes=[pltpu.VMEM((length * quarter, blk, blk), a_blocks.dtype)],
            compiler_params=params(),
            cost_estimate=cost(0, (len(ins) + sides) * chunk_bytes),
            name=f"relay{chunk}",
        )(n, *ins)
        ends.append(end_swap(outs[0]))
        if to_mid:
            mids.append(mid_swap(outs[1]))

    wide_j = 2 if bc % 2 == 0 else 1
    chunk_spec = pl.BlockSpec(chunk_shape.shape, lambda g: (0, 0, 0))
    acc = pl.pallas_call(
        functools.partial(early_kernel, END_CHUNKS - 1, MID_CHUNKS),
        grid=(bc // wide_j,),
        in_specs=[smem(), smem(), smem(), pl.BlockSpec(a_blocks.shape, lambda g: (0, 0, 0, 0))]
        + [chunk_spec] * (END_CHUNKS - 1 + MID_CHUNKS)
        + [pl.BlockSpec((kb, wide_j, blk, blk), lambda g: (0, g, 0, 0))] * STEPS,
        out_specs=pl.BlockSpec((br * blk, wide_j * blk), lambda g: (0, g)),
        out_shape=jax.ShapeDtypeStruct((br * blk, bc * blk), jnp.float32),
        scratch_shapes=[pltpu.VMEM((br * blk, (STEPS * kb + 1) * blk), a_blocks.dtype)],
        compiler_params=params(),
        cost_estimate=cost(2 * STEPS * br * bc * kb * blk**3, 14 << 20),
        name="early",
    )(a_mask, end_table, mid_table, a_blocks, *ends[:-1], *mids, *right)

    def rest(late, acc, right):
        return pl.pallas_call(
            functools.partial(late_kernel, (END_CHUNKS - 1) * quarter),
            grid=(br,),
            in_specs=[
                smem(),
                smem(),
                smem(),
                pl.BlockSpec(late.shape, lambda g: (0, 0, 0)),
                pl.BlockSpec((blk, bc * blk), lambda g: (g, 0)),
                pl.BlockSpec(memory_space=pl.ANY),
                pl.BlockSpec(memory_space=pl.ANY),
            ],
            out_specs=pl.BlockSpec((1, bc, blk, blk), lambda g: (g, 0, 0, 0)),
            out_shape=jax.ShapeDtypeStruct((br, bc, blk, blk), jnp.bfloat16),
            scratch_shapes=[
                pltpu.VMEM((kb, bc, blk, blk), jnp.bfloat16),
                pltpu.VMEM((blk, bc * blk), jnp.float32),
                pltpu.SemaphoreType.DMA,
            ],
            compiler_params=params(),
            cost_estimate=cost(0, 8 << 20),
            name="late",
        )(z, c_mask, end_table, late, acc, right[1], right[3])

    def everything(late, acc, right):
        a_live = a_blocks * a_mask[:, :, None, None].astype(a_blocks.dtype)
        return dense_product(a_live, right, c_mask)

    return lax.cond(over[0] > 0, everything, rest, ends[-1], acc, right)


def on_device(a_blocks, a_mask, b_blocks, b_mask, c_mask):
    b_live = b_blocks * b_mask[:, :, None, None].astype(jnp.bfloat16)
    right = [b_live]
    for _ in range(1, STEPS):
        right.append(from_behind(right[-1], "row", -1))
    blocks = a_blocks.shape[0] * a_blocks.shape[1]
    rows = lax.axis_size("row")
    if lax.axis_size("col") == STEPS and blocks % 4 == 0 and rows & (rows - 1) == 0:
        return sparse_product(a_blocks, a_mask, right, c_mask)
    a_live = a_blocks * a_mask[:, :, None, None].astype(jnp.bfloat16)
    return dense_product(a_live, right, c_mask)


def solution(mesh):
    return jax.shard_map(
        on_device,
        mesh=mesh,
        in_specs=(
            P("row", "col", None, None),
            P("row", "col"),
            P("row", "col", None, None),
            P("row", "col"),
            P("row", "col"),
        ),
        out_specs=P("row", "col", None, None),
        check_vma=False,
    )
```

```python
import functools

import jax
import jax.numpy as jnp
from jax import lax
from jax.experimental import pallas as pl
from jax.experimental.pallas import tpu as pltpu
from jax.sharding import PartitionSpec as P

STEPS = 4
T_SECOND, T_RIGHT = 5, 0
NOTE = 16
MIB = 1024 * 1024


def slots(blocks):
    return blocks // 2, 3 * blocks // 4, 3 * blocks // 8, 9 * blocks // 16


def from_behind(array, axis, by):
    size = lax.axis_size(axis)
    return lax.ppermute(array, axis, [(i, (i + by) % size) for i in range(size)])


def smem():
    return pl.BlockSpec(memory_space=pltpu.SMEM)


def whole():
    return pl.BlockSpec(memory_space=pltpu.VMEM)


def anywhere():
    return pl.BlockSpec(memory_space=pl.ANY)


def in_hbm():
    return pl.BlockSpec(memory_space=pltpu.HBM)


def params(mib=8):
    return pltpu.CompilerParams(vmem_limit_bytes=mib * MIB)


def cost(flops, nbytes):
    return pl.CostEstimate(flops=int(flops), bytes_accessed=int(nbytes), transcendentals=0)


def wide(a_ref):
    kb, blk = a_ref.shape[1], a_ref.shape[-1]
    return jnp.concatenate([a_ref[:, k].reshape(-1, blk) for k in range(kb)], axis=1)


def tall(b_ref):
    kb, bc = b_ref.shape[:2]
    return jnp.concatenate(
        [jnp.concatenate([b_ref[k, j] for j in range(bc)], axis=1) for k in range(kb)], axis=0
    )


def filtered(c_ref, i, j, block):
    return (block * c_ref[i, j].astype(jnp.float32)).astype(jnp.bfloat16)


def token_kernel(*refs):
    refs[-1][...] = jnp.zeros_like(refs[-1])


def token(seen, us):
    return pl.pallas_call(
        token_kernel,
        in_specs=[anywhere()] * len(seen),
        out_specs=whole(),
        out_shape=jax.ShapeDtypeStruct((8, 128), jnp.float32),
        compiler_params=params(),
        cost_estimate=cost(us * 1.1e9, 0),
        name="token",
    )(*seen)


def passed(x, seen):
    return pl.pallas_call(
        lambda *refs: None,
        in_specs=[anywhere()] * (1 + len(seen)),
        out_specs=anywhere(),
        out_shape=jax.ShapeDtypeStruct(x.shape, x.dtype),
        input_output_aliases={0: 0},
        compiler_params=params(),
        cost_estimate=cost(0, 0),
        name="passed",
    )(x, *seen)


def live_kernel(by_column, mask_ref, x_ref, *refs):
    out_ref = refs[-1]
    i = pl.program_id(0)
    for j in range(x_ref.shape[1]):
        keep = mask_ref[j, i] if by_column else mask_ref[i, j]
        out_ref[0, j] = x_ref[0, j] * keep.astype(jnp.float32).astype(x_ref.dtype)


def live(blocks, mask, by_column=False, after=()):
    shape = (1,) + blocks.shape[1:]
    return pl.pallas_call(
        functools.partial(live_kernel, by_column),
        grid=(blocks.shape[0],),
        in_specs=[smem(), pl.BlockSpec(shape, lambda g: (g, 0, 0, 0))] + [anywhere()] * len(after),
        out_specs=pl.BlockSpec(shape, lambda g: (g, 0, 0, 0)),
        out_shape=jax.ShapeDtypeStruct(blocks.shape, blocks.dtype),
        compiler_params=params(),
        cost_estimate=cost(0, 4 * blocks.size),
        name="live",
    )(mask, blocks, *after)


def dense_kernel(*refs):
    a_refs, b_refs, acc_ref = refs[:STEPS], refs[STEPS:-1], refs[-1]
    total = None
    for a_ref, b_ref in zip(a_refs, b_refs):
        part = jnp.dot(wide(a_ref), tall(b_ref), preferred_element_type=jnp.float32)
        total = part if total is None else total + part
    acc_ref[...] = total


def dense_sum(left, right):
    br, kb, blk, _ = left[0].shape
    bc = right[0].shape[1]
    wide_j = 2 if bc % 2 == 0 else 1
    return pl.pallas_call(
        dense_kernel,
        grid=(bc // wide_j,),
        in_specs=[pl.BlockSpec((br, kb, blk, blk), lambda g: (0, 0, 0, 0))] * STEPS
        + [pl.BlockSpec((kb, wide_j, blk, blk), lambda g: (0, g, 0, 0))] * STEPS,
        out_specs=pl.BlockSpec((br * blk, wide_j * blk), lambda g: (0, g)),
        out_shape=jax.ShapeDtypeStruct((br * blk, bc * blk), jnp.float32),
        compiler_params=params(32),
        cost_estimate=cost(2 * STEPS * br * bc * kb * blk**3, 12 << 20),
        name="dense",
    )(*left, *right)


def filter_kernel(c_ref, acc_ref, out_ref):
    blk = out_ref.shape[-1]
    for j in range(out_ref.shape[1]):
        out_ref[0, j] = filtered(c_ref, pl.program_id(0), j, acc_ref[:, j * blk : (j + 1) * blk])


def filter_sum(total, c_mask, blk):
    br, bc = c_mask.shape
    return pl.pallas_call(
        filter_kernel,
        grid=(br,),
        in_specs=[smem(), pl.BlockSpec((blk, bc * blk), lambda g: (g, 0))],
        out_specs=pl.BlockSpec((1, bc, blk, blk), lambda g: (g, 0, 0, 0)),
        out_shape=jax.ShapeDtypeStruct((br, bc, blk, blk), jnp.bfloat16),
        compiler_params=params(),
        name="filter",
    )(c_mask, total)


def dense_product(a_blocks, a_mask, b_blocks, b_mask, c_mask):
    left = [live(a_blocks, a_mask.T, by_column=True)]
    right = [live(b_blocks, b_mask)]
    for _ in range(1, STEPS):
        left.append(from_behind(left[-1], "col", -1))
        right.append(from_behind(right[-1], "row", -1))
    return filter_sum(dense_sum(left, right), c_mask, a_blocks.shape[-1])


def compact_kernel(mask_ref, a_ref, lead_ref, head_ref, inner_ref, tail_ref, n_ref, list_ref):
    br, kb, blk = a_ref.shape[:3]
    head, lead, inner, _ = slots(br * kb)
    lanes = lax.broadcasted_iota(jnp.int32, (NOTE, blk), 1)
    note = jnp.zeros((NOTE, blk), jnp.int32)
    count = jnp.int32(0)
    for k in range(kb):
        for i in range(br):
            list_ref[pl.ds(pl.multiple_of(count * blk, blk), blk), :] = a_ref[i, k]
            note = jnp.where(lanes == k * br + i, mask_ref[k, i], note)
            count = count + mask_ref[k, i]
    note = note.astype(jnp.float32).astype(jnp.bfloat16)
    lead_ref[0 : lead * blk, :] = list_ref[0 : lead * blk, :]
    lead_ref[lead * blk :, :] = note
    head_ref[0 : head * blk, :] = list_ref[0 : head * blk, :]
    head_ref[head * blk :, :] = note
    inner_ref[...] = list_ref[head * blk : (head + inner) * blk, :]
    tail_ref[...] = list_ref[head * blk :, :]
    n_ref[0] = count


def pool_kernel(skip, n_ref, tail_ref, more_ref, *refs):
    out_ref, line = refs[-2:]
    blk = out_ref.shape[1]
    first = skip * blk - tail_ref.shape[0]
    own = tail_ref.shape[0] - first
    line[0:own, :] = tail_ref[first:, :]
    at = pl.multiple_of(jnp.maximum(n_ref[0] - skip, 0) * blk, blk)
    line[pl.ds(at, more_ref.shape[0]), :] = more_ref[...]
    out_ref[...] = line[0 : out_ref.shape[0], :]


def table_kernel(blocks, where_ref, own_ref, *refs):
    notes, (table_ref, over_ref, note_ref, wide_ref, mask_ref, sems, sem) = refs[:6], refs[6:]
    copies = [
        pltpu.make_async_copy(
            ref.at[pl.ds(ref.shape[0] - NOTE, NOTE), :], note_ref.at[pl.ds(m * NOTE, NOTE), :], sems.at[m]
        )
        for m, ref in enumerate(notes)
    ]
    for copy in copies:
        copy.start()
    for copy in copies:
        copy.wait()
    wide_ref[...] = note_ref[...].astype(jnp.float32).astype(jnp.int32)
    down = pltpu.make_async_copy(wide_ref, mask_ref, sem)
    down.start()
    down.wait()

    none, apart = STEPS * blocks, blocks + 8
    head, lead, inner, pool = slots(blocks)
    z = where_ref[0]
    at_end = jnp.logical_or(z == 0, z == 3)
    near = 1 + 2 * (z % 2)
    flip = where_ref[1] % 2 == 1

    def place_of(step):
        return jnp.where(flip, 4 - step, step)

    def fill(base, place, m):
        count = jnp.int32(base)
        for b in range(blocks):
            table_ref[count] = place * blocks + b
            count = count + mask_ref[m * NOTE, b]

        def pad(p, carry):
            table_ref[p] = none
            return carry

        lax.fori_loop(count, base + blocks, pad, 0)
        return count - base

    first = fill(0, place_of(near), jnp.where(at_end, 0, 3))
    second = fill(apart, jnp.where(at_end, 2, place_of(4 - near)), jnp.where(at_end, 1, 4))
    third = fill(2 * apart, jnp.where(at_end, place_of(4 - near), 2), jnp.where(at_end, 2, 5))

    def append(base, begin, length, at):
        def body(p, at):
            table_ref[at] = table_ref[base + p]
            return at + 1

        return lax.fori_loop(begin, length, body, at)

    at = append(0, jnp.where(at_end, lead, blocks), first, jnp.int32(3 * apart))
    at = append(apart, head, second, at)
    at = append(2 * apart, head, third, at)

    def pad(p, carry):
        table_ref[p] = none
        return carry

    lax.fori_loop(at, 3 * apart + pool, pad, 0)

    own = jnp.int32(0)
    for k in range(own_ref.shape[0]):
        for i in range(own_ref.shape[1]):
            own = own + own_ref[k, i]

    def past(n, by):
        return jnp.maximum(n - by, 0)

    def overflows(next_one, middle, far):
        pooled = past(next_one, lead) + past(middle, head) + past(far, head)
        return jnp.logical_or(pooled > pool, far > head + inner)

    ends_view = jnp.logical_or(overflows(first, second, third), overflows(second, first, own))
    middles_view = jnp.logical_or(overflows(own, second, third), overflows(second, own, first))
    over_ref[0] = jnp.where(jnp.where(at_end, ends_view, middles_view), 1, 0).astype(jnp.int32)


def masked_tall(mask_ref, b_ref, j0):
    kb, bc = b_ref.shape[:2]

    def block(k, j):
        return b_ref[k, j] * mask_ref[k, j0 + j].astype(jnp.float32).astype(b_ref.dtype)

    return jnp.concatenate([jnp.concatenate([block(k, j) for j in range(bc)], axis=1) for k in range(kb)], axis=0)


def early_kernel(where_ref, mask_ref, c_ref, table_ref, *refs):
    b_masks, a_ref, refs = refs[:STEPS], refs[STEPS], refs[STEPS + 1 :]
    outs, mids, b_refs, (acc_ref, out_ref, left_ref) = refs[:3], refs[3:8], refs[8:12], refs[12:]
    br, kb, blk, _ = a_ref.shape
    blocks = br * kb
    apart = blocks + 8
    head, lead, inner, pool = slots(blocks)
    z = where_ref[0]
    at_end = jnp.logical_or(z == 0, z == 3)

    def scatter(ref, first, length):
        for b in range(length):
            place = table_ref[first + b]
            row = pl.multiple_of((place % br) * blk, blk)
            column = pl.multiple_of((place // br) * blk, blk)
            left_ref[pl.ds(row, blk), pl.ds(column, blk)] = ref[b * blk : (b + 1) * blk, :]

    @pl.when(pl.program_id(0) == 0)
    def _():
        for k in range(kb):
            for i in range(br):
                left_ref[i * blk : (i + 1) * blk, k * blk : (k + 1) * blk] = a_ref[i, k] * mask_ref[k, i].astype(
                    jnp.float32
                ).astype(jnp.bfloat16)
        left_ref[:, kb * blk :] = jnp.zeros((br * blk, left_ref.shape[1] - kb * blk), jnp.bfloat16)

        @pl.when(at_end)
        def _():
            scatter(outs[0], 0, lead)
            scatter(outs[1], apart, head)
            scatter(outs[2], 2 * apart, head)

        @pl.when(jnp.logical_not(at_end))
        def _():
            scatter(mids[0], 0, head)
            scatter(mids[1], head, inner)
            scatter(mids[2], apart, head)
            scatter(mids[3], 2 * apart, head)
            scatter(mids[4], 3 * apart, pool)

    j0 = pl.program_id(0) * out_ref.shape[1]
    total = None
    for t in range(STEPS):
        part = jnp.dot(
            left_ref[:, t * kb * blk : (t + 1) * kb * blk],
            masked_tall(b_masks[t], b_refs[t], j0),
            preferred_element_type=jnp.float32,
        )
        total = part if total is None else total + part
    acc_ref[...] = total
    for i in range(br):
        for j in range(out_ref.shape[1]):
            out_ref[i, j] = filtered(c_ref, i, j0 + j, total[i * blk : (i + 1) * blk, j * blk : (j + 1) * blk])


def late_kernel(where_ref, c_ref, table_ref, *refs):
    b_masks, refs = refs[: STEPS - 1], refs[STEPS - 1 :]
    late_ref, acc_ref, b_refs, refs = refs[0], refs[1], refs[2 : 1 + STEPS], refs[2 + STEPS :]
    out_ref, row_ref, sems = refs
    br, bc, blk, _ = out_ref.shape
    kb = b_refs[0].shape[0]
    none = STEPS * kb * br
    _, _, _, pool = slots(kb * br)
    first = 3 * (kb * br + 8)
    at_end = jnp.logical_or(where_ref[0] == 0, where_ref[0] == 3)
    places = [jnp.where(at_end, table_ref[first + b], none) for b in range(pool)]

    for b, place in enumerate(places):
        for slab, (b_ref, mask_ref) in enumerate(zip(b_refs, b_masks)):

            @pl.when(place // (kb * br) == slab + 1)
            def _():
                row, k = pl.multiple_of((place % br) * blk, blk), (place // br) % kb
                keep = [mask_ref[k, j].astype(jnp.float32).astype(jnp.bfloat16) for j in range(bc)]
                columns = jnp.concatenate([b_ref[k, j] * keep[j] for j in range(bc)], axis=1)
                acc_ref[pl.ds(row, blk), :] += jnp.dot(
                    late_ref[b * blk : (b + 1) * blk, :], columns, preferred_element_type=jnp.float32
                )

    go = [pltpu.make_async_copy(row_ref.at[i], out_ref.at[i], sems.at[i]) for i in range(br)]
    touched = [
        functools.reduce(jnp.logical_or, [jnp.logical_and(p < none, p % br == i) for p in places]) for i in range(br)
    ]
    for i in range(br):

        @pl.when(touched[i])
        def _():
            for j in range(bc):
                row_ref[i, j] = filtered(c_ref, i, j, acc_ref[i * blk : (i + 1) * blk, j * blk : (j + 1) * blk])
            go[i].start()

    for i in range(br):

        @pl.when(touched[i])
        def _():
            go[i].wait()


def sparse_product(a_blocks, a_mask, b_blocks, b_mask, c_mask):
    br, kb, blk, _ = a_blocks.shape
    bc = b_blocks.shape[1]
    blocks = br * kb
    head, lead, inner, pool = slots(blocks)
    rows = lax.axis_size("row")
    where = jnp.stack([lax.axis_index("col"), lax.axis_index("row")]).astype(jnp.int32)
    by_column = a_mask.T

    def outward(x):
        return lax.ppermute(x, "col", [(1, 0), (2, 3)])

    def inward(x):
        return lax.ppermute(x, "col", [(0, 1), (3, 2)])

    def over_middle(x):
        return lax.ppermute(x, "col", [(1, 2), (2, 1)])

    def two_up(x):
        return from_behind(x, "row", -2)

    def odd_up(x):
        return lax.ppermute(x, "row", [((r + 1 + 2 * (r % 2)) % rows, r) for r in range(rows)])

    def core_swap(x):
        return lax.ppermute(x, "row", [(r, r ^ 1) for r in range(rows)])

    def listed(slot_count, note=0):
        return jax.ShapeDtypeStruct((slot_count * blk + note, blk), a_blocks.dtype)

    with jax.named_scope("right_two_up"):
        second = two_up(b_blocks)
    with jax.named_scope("right_odd_up"):
        odd_one = odd_up(b_blocks)
    with jax.named_scope("right_masks"):
        second_mask, odd_mask = two_up(b_mask), odd_up(b_mask)
        b_masks = [b_mask, odd_mask, second_mask, core_swap(second_mask)]

    own_lead, own_head, own_inner, own_tail, n = pl.pallas_call(
        compact_kernel,
        in_specs=[smem(), whole()],
        out_specs=[whole(), whole(), whole(), whole(), smem()],
        out_shape=[
            listed(lead, NOTE),
            listed(head, NOTE),
            listed(inner),
            listed(blocks - head),
            jax.ShapeDtypeStruct((1,), jnp.int32),
        ],
        scratch_shapes=[pltpu.VMEM((blocks * blk, blk), a_blocks.dtype)],
        compiler_params=params(),
        cost_estimate=cost(0, 6 * blocks * blk * blk),
        name="compact",
    )(by_column, a_blocks)

    def pooled(skip, more, gate, seen):
        own = blocks - skip
        outs = pl.pallas_call(
            functools.partial(pool_kernel, skip),
            in_specs=[smem(), whole(), whole()] + [anywhere()] * (len(gate) + len(seen)),
            out_specs=[anywhere()] * len(gate) + [whole()],
            out_shape=[jax.ShapeDtypeStruct(g.shape, g.dtype) for g in gate] + [listed(pool)],
            scratch_shapes=[pltpu.VMEM((own * blk + more.shape[0], blk), a_blocks.dtype)],
            input_output_aliases={3 + g: g for g in range(len(gate))},
            compiler_params=params(),
            cost_estimate=cost(0, 6 * pool * blk * blk),
            name="pool",
        )(n, own_tail, more, *gate, *seen)
        return outs[-1], outs[:-1]

    with jax.named_scope("lead_outward"):
        near_lead = outward(own_lead)
    with jax.named_scope("head_inward"):
        near_head = inward(own_head)
    with jax.named_scope("head_over_middle"):
        mid_head = over_middle(own_head)
    with jax.named_scope("second_head_outward"):
        mid_head = passed(mid_head, [near_lead])
        second_head = outward(mid_head)
    with jax.named_scope("tail_inward"):
        near_tail = inward(passed(own_inner, [near_lead]))
    with jax.named_scope("end_head_over_middle"):
        end_head = over_middle(near_head)
    with jax.named_scope("third_head_outward"):
        third_head = outward(end_head)
    mid_pool, _ = pooled(head, near_tail, [], [end_head])
    with jax.named_scope("pool_over_middle"):
        mid_pool = over_middle(mid_pool)
    slabs_here = token([second, odd_one], T_RIGHT)
    out_pool, (second, odd_one) = pooled(
        lead, mid_pool, [second, odd_one], [token([second_head], T_SECOND), slabs_here, third_head] + b_masks[1:]
    )
    with jax.named_scope("pool_outward"):
        out_pool = outward(out_pool)
    with jax.named_scope("right_core_swap"):
        right = [b_blocks, odd_one, second, core_swap(second)]

    table, over = pl.pallas_call(
        functools.partial(table_kernel, blocks),
        in_specs=[smem(), smem()] + [anywhere()] * 6,
        out_specs=[smem(), smem()],
        out_shape=[jax.ShapeDtypeStruct((5 * (blocks + 8),), jnp.int32), jax.ShapeDtypeStruct((1,), jnp.int32)],
        scratch_shapes=[
            pltpu.VMEM((6 * NOTE, blk), jnp.bfloat16),
            pltpu.VMEM((6 * NOTE, blk), jnp.int32),
            pltpu.SMEM((6 * NOTE, blk), jnp.int32),
            pltpu.SemaphoreType.DMA((6,)),
            pltpu.SemaphoreType.DMA,
        ],
        compiler_params=params(),
        name="table",
    )(where, by_column, near_lead, second_head, third_head, near_head, mid_head, end_head)

    def fixed(x):
        return pl.BlockSpec(x.shape, lambda g: (0,) * x.ndim)

    wide_j = 2 if bc % 2 == 0 else 1
    arrived = [near_lead, second_head, third_head, near_head, near_tail, mid_head, end_head, mid_pool]
    acc, out = pl.pallas_call(
        early_kernel,
        grid=(bc // wide_j,),
        in_specs=[smem()] * (4 + STEPS)
        + [fixed(x) for x in [a_blocks] + arrived]
        + [pl.BlockSpec((kb, wide_j, blk, blk), lambda g: (0, g, 0, 0))] * STEPS,
        out_specs=[
            pl.BlockSpec((br * blk, wide_j * blk), lambda g: (0, g)),
            pl.BlockSpec((br, wide_j, blk, blk), lambda g: (0, g, 0, 0)),
        ],
        out_shape=[
            jax.ShapeDtypeStruct((br * blk, bc * blk), jnp.float32),
            jax.ShapeDtypeStruct((br, bc, blk, blk), jnp.bfloat16),
        ],
        scratch_shapes=[pltpu.VMEM((br * blk, (STEPS * kb + 1) * blk), a_blocks.dtype)],
        compiler_params=params(32),
        cost_estimate=cost(2 * STEPS * br * bc * kb * blk**3, 14 << 20),
        name="early",
    )(where, by_column, c_mask, table, *b_masks, a_blocks, *arrived, *right)

    out = pl.pallas_call(
        late_kernel,
        in_specs=[smem()] * (3 + STEPS - 1) + [whole()] * (1 + STEPS) + [in_hbm()],
        out_specs=in_hbm(),
        out_shape=jax.ShapeDtypeStruct((br, bc, blk, blk), jnp.bfloat16),
        scratch_shapes=[pltpu.VMEM((br, bc, blk, blk), jnp.bfloat16), pltpu.SemaphoreType.DMA((br,))],
        input_output_aliases={3 + STEPS - 1 + 1 + STEPS: 0},
        compiler_params=params(24),
        cost_estimate=cost(0, 4 << 20),
        name="late",
    )(where, c_mask, table, *b_masks[1:], out_pool, acc, *right[1:], out)

    def again(state):
        before, trips = state
        left = [live(a_blocks, by_column, by_column=True, after=(before,))]
        for _ in range(1, STEPS):
            left.append(from_behind(left[-1], "col", -1))
        odd = lax.axis_index("row") % 2 == 1
        held = [live(slab, mask, after=(before,)) for slab, mask in zip(right, b_masks)]
        ordered = [held[0], jnp.where(odd, held[3], held[1]), held[2], jnp.where(odd, held[1], held[3])]
        return filter_sum(dense_sum(left, ordered), c_mask, blk), trips - 1

    out, _ = lax.while_loop(lambda state: state[1] > 0, again, (out, over[0]))
    return out


def on_device(a_blocks, a_mask, b_blocks, b_mask, c_mask):
    blocks = a_blocks.shape[0] * a_blocks.shape[1]
    fits = blocks % 16 == 0 and blocks <= a_blocks.shape[-1]
    if lax.axis_size("col") == STEPS and lax.axis_size("row") % 2 == 0 and fits:
        return sparse_product(a_blocks, a_mask, b_blocks, b_mask, c_mask)
    return dense_product(a_blocks, a_mask, b_blocks, b_mask, c_mask)


def solution(mesh):
    return jax.shard_map(
        on_device,
        mesh=mesh,
        in_specs=(
            P("row", "col", None, None),
            P("row", "col"),
            P("row", "col", None, None),
            P("row", "col"),
            P("row", "col"),
        ),
        out_specs=P("row", "col", None, None),
        check_vma=False,
    )
```

```python
import functools

import jax
import jax.numpy as jnp
from jax import lax
from jax.experimental import pallas as pl
from jax.experimental.pallas import tpu as pltpu
from jax.sharding import PartitionSpec as P

STEPS = 4
T_TAIL, T_SECOND, T_RIGHT = 7, 5, 2
NOTE = 16
MIB = 1024 * 1024


def slots(blocks):
    return blocks // 2, 3 * blocks // 4, 3 * blocks // 8, 9 * blocks // 16


def from_behind(array, axis, by):
    size = lax.axis_size(axis)
    return lax.ppermute(array, axis, [(i, (i + by) % size) for i in range(size)])


def smem():
    return pl.BlockSpec(memory_space=pltpu.SMEM)


def whole():
    return pl.BlockSpec(memory_space=pltpu.VMEM)


def anywhere():
    return pl.BlockSpec(memory_space=pl.ANY)


def params(mib=8):
    return pltpu.CompilerParams(vmem_limit_bytes=mib * MIB)


def cost(flops, nbytes):
    return pl.CostEstimate(flops=int(flops), bytes_accessed=int(nbytes), transcendentals=0)


def wide(a_ref):
    kb, blk = a_ref.shape[1], a_ref.shape[-1]
    return jnp.concatenate([a_ref[:, k].reshape(-1, blk) for k in range(kb)], axis=1)


def tall(b_ref):
    kb, bc = b_ref.shape[:2]
    return jnp.concatenate(
        [jnp.concatenate([b_ref[k, j] for j in range(bc)], axis=1) for k in range(kb)], axis=0
    )


def filtered(c_ref, i, j, block):
    return (block * c_ref[i, j].astype(jnp.float32)).astype(jnp.bfloat16)


def token_kernel(*refs):
    refs[-1][...] = jnp.zeros_like(refs[-1])


def token(seen, us):
    return pl.pallas_call(
        token_kernel,
        in_specs=[anywhere()] * len(seen),
        out_specs=whole(),
        out_shape=jax.ShapeDtypeStruct((8, 128), jnp.float32),
        compiler_params=params(),
        cost_estimate=cost(us * 1.1e9, 0),
        name="token",
    )(*seen)


def passed(arrays, seen=()):
    return pl.pallas_call(
        lambda *refs: None,
        in_specs=[anywhere()] * (len(arrays) + len(seen)),
        out_specs=[anywhere()] * len(arrays),
        out_shape=[jax.ShapeDtypeStruct(x.shape, x.dtype) for x in arrays],
        input_output_aliases={x: x for x in range(len(arrays))},
        compiler_params=params(),
        cost_estimate=cost(0, 0),
        name="passed",
    )(*arrays, *seen)


def live_kernel(by_column, mask_ref, x_ref, *refs):
    out_ref = refs[-1]
    i = pl.program_id(0)
    for j in range(x_ref.shape[1]):
        keep = mask_ref[j, i] if by_column else mask_ref[i, j]
        out_ref[0, j] = x_ref[0, j] * keep.astype(jnp.float32).astype(x_ref.dtype)


def live(blocks, mask, by_column=False, after=()):
    shape = (1,) + blocks.shape[1:]
    return pl.pallas_call(
        functools.partial(live_kernel, by_column),
        grid=(blocks.shape[0],),
        in_specs=[smem(), pl.BlockSpec(shape, lambda g: (g, 0, 0, 0))] + [anywhere()] * len(after),
        out_specs=pl.BlockSpec(shape, lambda g: (g, 0, 0, 0)),
        out_shape=jax.ShapeDtypeStruct(blocks.shape, blocks.dtype),
        compiler_params=params(),
        cost_estimate=cost(0, 4 * blocks.size),
        name="live",
    )(mask, blocks, *after)


def dense_kernel(*refs):
    a_refs, b_refs, acc_ref = refs[:STEPS], refs[STEPS:-1], refs[-1]
    total = None
    for a_ref, b_ref in zip(a_refs, b_refs):
        part = jnp.dot(wide(a_ref), tall(b_ref), preferred_element_type=jnp.float32)
        total = part if total is None else total + part
    acc_ref[...] = total


def dense_sum(left, right):
    br, kb, blk, _ = left[0].shape
    bc = right[0].shape[1]
    wide_j = 2 if bc % 2 == 0 else 1
    return pl.pallas_call(
        dense_kernel,
        grid=(bc // wide_j,),
        in_specs=[pl.BlockSpec((br, kb, blk, blk), lambda g: (0, 0, 0, 0))] * STEPS
        + [pl.BlockSpec((kb, wide_j, blk, blk), lambda g: (0, g, 0, 0))] * STEPS,
        out_specs=pl.BlockSpec((br * blk, wide_j * blk), lambda g: (0, g)),
        out_shape=jax.ShapeDtypeStruct((br * blk, bc * blk), jnp.float32),
        compiler_params=params(20),
        cost_estimate=cost(2 * STEPS * br * bc * kb * blk**3, 12 << 20),
        name="dense",
    )(*left, *right)


def filter_kernel(c_ref, acc_ref, *refs):
    out_ref = refs[-1]
    blk = out_ref.shape[-1]
    for j in range(out_ref.shape[1]):
        out_ref[0, j] = filtered(c_ref, pl.program_id(0), j, acc_ref[:, j * blk : (j + 1) * blk])


def filter_sum(total, c_mask, blk, *into):
    br, bc = c_mask.shape
    return pl.pallas_call(
        filter_kernel,
        grid=(br,),
        in_specs=[smem(), pl.BlockSpec((blk, bc * blk), lambda g: (g, 0))] + [anywhere()] * len(into),
        out_specs=pl.BlockSpec((1, bc, blk, blk), lambda g: (g, 0, 0, 0)),
        out_shape=jax.ShapeDtypeStruct((br, bc, blk, blk), jnp.bfloat16),
        input_output_aliases={2: 0} if into else {},
        compiler_params=params(),
        name="filter",
    )(c_mask, total, *into)


def dense_product(a_blocks, a_mask, b_blocks, b_mask, c_mask):
    left = [live(a_blocks, a_mask.T, by_column=True)]
    right = [live(b_blocks, b_mask)]
    for _ in range(1, STEPS):
        left.append(from_behind(left[-1], "col", -1))
        right.append(from_behind(right[-1], "row", -1))
    return filter_sum(dense_sum(left, right), c_mask, a_blocks.shape[-1])


def compact_kernel(mask_ref, a_ref, head_ref, inner_ref, tail_ref, n_ref, list_ref):
    br, kb, blk = a_ref.shape[:3]
    head, lead, inner, _ = slots(br * kb)
    lanes = lax.broadcasted_iota(jnp.int32, (NOTE, blk), 1)
    note = jnp.zeros((NOTE, blk), jnp.int32)
    count = jnp.int32(0)
    for k in range(kb):
        for i in range(br):
            list_ref[pl.ds(pl.multiple_of(count * blk, blk), blk), :] = a_ref[i, k]
            note = jnp.where(lanes == k * br + i, mask_ref[k, i], note)
            count = count + mask_ref[k, i]
    note = note.astype(jnp.float32).astype(jnp.bfloat16)
    head_ref[0 : head * blk, :] = list_ref[0 : head * blk, :]
    head_ref[head * blk :, :] = note
    inner_ref[...] = list_ref[head * blk : (head + inner) * blk, :]
    tail_ref[...] = list_ref[head * blk :, :]
    n_ref[0] = count


def extend_kernel(head_ref, tail_ref, out_ref):
    size = head_ref.shape[0] - NOTE
    more = out_ref.shape[0] - head_ref.shape[0]
    out_ref[0:size, :] = head_ref[0:size, :]
    out_ref[size : size + more, :] = tail_ref[0:more, :]
    out_ref[size + more :, :] = head_ref[size:, :]


def pool_kernel(skip, n_ref, tail_ref, more_ref, *refs):
    out_ref, line = refs[-2:]
    blk = out_ref.shape[1]
    first = skip * blk - tail_ref.shape[0]
    own = tail_ref.shape[0] - first
    line[0:own, :] = tail_ref[first:, :]
    at = pl.multiple_of(jnp.maximum(n_ref[0] - skip, 0) * blk, blk)
    line[pl.ds(at, more_ref.shape[0]), :] = more_ref[...]
    out_ref[...] = line[0 : out_ref.shape[0], :]


def table_kernel(blocks, where_ref, own_ref, *refs):
    notes, (table_ref, over_ref, note_ref, wide_ref, mask_ref, sems, sem) = refs[:5], refs[5:]
    copies = [
        pltpu.make_async_copy(
            ref.at[pl.ds(ref.shape[0] - NOTE, NOTE), :], note_ref.at[pl.ds(m * NOTE, NOTE), :], sems.at[m]
        )
        for m, ref in enumerate(notes)
    ]
    for copy in copies:
        copy.start()
    for copy in copies:
        copy.wait()
    wide_ref[...] = note_ref[...].astype(jnp.float32).astype(jnp.int32)
    down = pltpu.make_async_copy(wide_ref, mask_ref, sem)
    down.start()
    down.wait()

    none, apart = STEPS * blocks, blocks + 8
    head, lead, inner, pool = slots(blocks)
    z = where_ref[0]
    at_end = jnp.logical_or(z == 0, z == 3)
    near = 1 + 2 * (z % 2)
    flip = where_ref[1] % 2 == 1

    def place_of(step):
        return jnp.where(flip, 4 - step, step)

    def fill(base, place, m):
        def body(b, count):
            table_ref[count] = place * blocks + b
            return count + mask_ref[m * NOTE, b]

        count = lax.fori_loop(0, blocks, body, jnp.int32(base), unroll=8)

        def pad(p, carry):
            table_ref[p] = none
            return carry

        lax.fori_loop(count, base + blocks, pad, 0)
        return count - base

    first = fill(0, place_of(near), 0)
    second = fill(apart, jnp.where(at_end, 2, place_of(4 - near)), jnp.where(at_end, 1, 3))
    third = fill(2 * apart, jnp.where(at_end, place_of(4 - near), 2), jnp.where(at_end, 2, 4))

    def append(base, begin, length, at):
        def body(p, at):
            table_ref[at] = table_ref[base + p]
            return at + 1

        return lax.fori_loop(begin, length, body, at)

    at = append(0, jnp.where(at_end, lead, blocks), first, jnp.int32(3 * apart))
    at = append(apart, head, second, at)
    at = append(2 * apart, head, third, at)

    def pad(p, carry):
        table_ref[p] = none
        return carry

    lax.fori_loop(at, 3 * apart + pool, pad, 0)

    own = jnp.int32(0)
    for k in range(own_ref.shape[0]):
        for i in range(own_ref.shape[1]):
            own = own + own_ref[k, i]

    def past(n, by):
        return jnp.maximum(n - by, 0)

    def overflows(next_one, middle, far):
        pooled = past(next_one, lead) + past(middle, head) + past(far, head)
        return jnp.logical_or(pooled > pool, far > head + inner)

    ends_view = jnp.logical_or(overflows(first, second, third), overflows(second, first, own))
    middles_view = jnp.logical_or(overflows(own, second, third), overflows(second, own, first))
    over_ref[0] = jnp.where(jnp.where(at_end, ends_view, middles_view), 1, 0).astype(jnp.int32)


def masked_tall(mask_ref, b_ref, j0):
    kb, bc = b_ref.shape[:2]

    def block(k, j):
        return b_ref[k, j] * mask_ref[k, j0 + j].astype(jnp.float32).astype(b_ref.dtype)

    return jnp.concatenate([jnp.concatenate([block(k, j) for j in range(bc)], axis=1) for k in range(kb)], axis=0)


def early_kernel(where_ref, mask_ref, c_ref, table_ref, *refs):
    b_masks, a_ref, refs = refs[:STEPS], refs[STEPS], refs[STEPS + 1 :]
    near_ref, outs, mids, refs = refs[0], refs[1:3], refs[3:7], refs[7:]
    b_refs, (acc_ref, out_ref, left_ref) = refs[:STEPS], refs[STEPS:]
    br, kb, blk, _ = a_ref.shape
    blocks = br * kb
    apart = blocks + 8
    head, lead, inner, pool = slots(blocks)
    z = where_ref[0]
    at_end = jnp.logical_or(z == 0, z == 3)

    def scatter(ref, first, length, at=0):
        def body(b, carry):
            place = table_ref[first + b]
            row = pl.multiple_of((place % br) * blk, blk)
            column = pl.multiple_of((place // br) * blk, blk)
            left_ref[pl.ds(row, blk), pl.ds(column, blk)] = ref[pl.ds(pl.multiple_of((at + b) * blk, blk), blk), :]
            return carry

        lax.fori_loop(0, length, body, 0, unroll=2)

    @pl.when(pl.program_id(0) == 0)
    def _():
        for k in range(kb):
            for i in range(br):
                left_ref[i * blk : (i + 1) * blk, k * blk : (k + 1) * blk] = a_ref[i, k] * mask_ref[k, i].astype(
                    jnp.float32
                ).astype(jnp.bfloat16)
        left_ref[:, kb * blk :] = jnp.zeros((br * blk, left_ref.shape[1] - kb * blk), jnp.bfloat16)
        scatter(near_ref, 0, head)

        @pl.when(at_end)
        def _():
            scatter(outs[0], apart, head)
            scatter(outs[0], head, lead - head, head)
            scatter(outs[1], 2 * apart, head)

        @pl.when(jnp.logical_not(at_end))
        def _():
            scatter(mids[0], head, inner)
            scatter(mids[1], apart, head)
            scatter(mids[2], 2 * apart, head)
            scatter(mids[3], 3 * apart, pool)

    j0 = pl.program_id(0) * out_ref.shape[1]
    total = None
    for t in range(STEPS):
        part = jnp.dot(
            left_ref[:, t * kb * blk : (t + 1) * kb * blk],
            masked_tall(b_masks[t], b_refs[t], j0),
            preferred_element_type=jnp.float32,
        )
        total = part if total is None else total + part
    acc_ref[...] = total
    for i in range(br):
        for j in range(out_ref.shape[1]):
            out_ref[i, j] = filtered(c_ref, i, j0 + j, total[i * blk : (i + 1) * blk, j * blk : (j + 1) * blk])


def late_kernel(where_ref, c_ref, table_ref, *refs):
    b_masks, refs = refs[: STEPS - 1], refs[STEPS - 1 :]
    late_ref, acc_ref, b_refs, refs = refs[0], refs[1], refs[2 : 1 + STEPS], refs[2 + STEPS :]
    out_ref, row_ref, touched_ref, sems = refs
    br, bc, blk, _ = out_ref.shape
    kb = b_refs[0].shape[0]
    _, _, _, pool = slots(kb * br)
    first = 3 * (kb * br + 8)
    at_end = jnp.logical_or(where_ref[0] == 0, where_ref[0] == 3)

    def clear(i, carry):
        touched_ref[i] = 0
        return carry

    def add(b, carry):
        place = table_ref[first + b]
        for slab, (b_ref, mask_ref) in enumerate(zip(b_refs, b_masks)):

            @pl.when(place // (kb * br) == slab + 1)
            def _():
                i, k = place % br, (place // br) % kb
                touched_ref[i] = 1
                keep = [mask_ref[k, j].astype(jnp.float32).astype(jnp.bfloat16) for j in range(bc)]
                columns = jnp.concatenate([b_ref[k, j] * keep[j] for j in range(bc)], axis=1)
                acc_ref[pl.ds(pl.multiple_of(i * blk, blk), blk), :] += jnp.dot(
                    late_ref[pl.ds(pl.multiple_of(b * blk, blk), blk), :], columns, preferred_element_type=jnp.float32
                )

        return carry

    def go(i):
        return pltpu.make_async_copy(row_ref.at[i], out_ref.at[i], sems.at[i])

    def send(i, carry):
        @pl.when(touched_ref[i] > 0)
        def _():
            row = pl.multiple_of(i * blk, blk)
            for j in range(bc):
                row_ref[i, j] = filtered(c_ref, i, j, acc_ref[pl.ds(row, blk), j * blk : (j + 1) * blk])
            go(i).start()

        return carry

    def settle(i, carry):
        @pl.when(touched_ref[i] > 0)
        def _():
            go(i).wait()

        return carry

    lax.fori_loop(0, br, clear, 0)
    lax.fori_loop(0, jnp.where(at_end, pool, 0), add, 0)
    lax.fori_loop(0, br, send, 0)
    lax.fori_loop(0, br, settle, 0)


def sparse_product(a_blocks, a_mask, b_blocks, b_mask, c_mask):
    br, kb, blk, _ = a_blocks.shape
    bc = b_blocks.shape[1]
    blocks = br * kb
    head, lead, inner, pool = slots(blocks)
    rows = lax.axis_size("row")
    where = jnp.stack([lax.axis_index("col"), lax.axis_index("row")]).astype(jnp.int32)
    by_column = a_mask.T

    def outward(x):
        return lax.ppermute(x, "col", [(1, 0), (2, 3)])

    def end_swap(x):
        return lax.ppermute(x, "col", [(0, 1), (1, 0), (2, 3), (3, 2)])

    def inward(x):
        return lax.ppermute(x, "col", [(0, 1), (3, 2)])

    def over_middle(x):
        return lax.ppermute(x, "col", [(1, 2), (2, 1)])

    def two_up(x):
        return from_behind(x, "row", -2)

    def odd_up(x):
        return lax.ppermute(x, "row", [((r + 1 + 2 * (r % 2)) % rows, r) for r in range(rows)])

    def core_swap(x):
        return lax.ppermute(x, "row", [(r, r ^ 1) for r in range(rows)])

    def listed(slot_count, note=0):
        return jax.ShapeDtypeStruct((slot_count * blk + note, blk), a_blocks.dtype)

    with jax.named_scope("right_two_up"):
        second = two_up(b_blocks)
    with jax.named_scope("right_odd_up"):
        odd_one = odd_up(b_blocks)
    with jax.named_scope("right_masks"):
        second_mask, odd_mask = two_up(b_mask), odd_up(b_mask)
        b_masks = [b_mask, odd_mask, second_mask, core_swap(second_mask)]

    own_head, own_inner, own_tail, n = pl.pallas_call(
        compact_kernel,
        in_specs=[smem(), whole()],
        out_specs=[whole(), whole(), whole(), smem()],
        out_shape=[
            listed(head, NOTE),
            listed(inner),
            listed(blocks - head),
            jax.ShapeDtypeStruct((1,), jnp.int32),
        ],
        scratch_shapes=[pltpu.VMEM((blocks * blk, blk), a_blocks.dtype)],
        compiler_params=params(),
        cost_estimate=cost(0, 6 * blocks * blk * blk),
        name="compact",
    )(by_column, a_blocks)

    def pooled(skip, more, gate, seen):
        own = blocks - skip
        outs = pl.pallas_call(
            functools.partial(pool_kernel, skip),
            in_specs=[smem(), whole(), whole()] + [anywhere()] * (len(gate) + len(seen)),
            out_specs=[anywhere()] * len(gate) + [whole()],
            out_shape=[jax.ShapeDtypeStruct(g.shape, g.dtype) for g in gate] + [listed(pool)],
            scratch_shapes=[pltpu.VMEM((own * blk + more.shape[0], blk), a_blocks.dtype)],
            input_output_aliases={3 + g: g for g in range(len(gate))},
            compiler_params=params(),
            cost_estimate=cost(0, 6 * pool * blk * blk),
            name="pool",
        )(n, own_tail, more, *gate, *seen)
        return outs[-1], outs[:-1]

    with jax.named_scope("head_over_middle"):
        mid_head = over_middle(own_head)
    with jax.named_scope("head_end_swap"):
        near_head = end_swap(own_head)
    with jax.named_scope("tail_inward"):
        near_tail = inward(own_inner)
    near_head, mid_head = passed([near_head, mid_head])
    with jax.named_scope("second_head_outward"):
        second_head = outward(
            pl.pallas_call(
                extend_kernel,
                in_specs=[whole()] * 2,
                out_specs=whole(),
                out_shape=listed(lead, NOTE),
                compiler_params=params(),
                cost_estimate=cost(0, 0),
                name="extend",
            )(mid_head, own_tail)
        )
    with jax.named_scope("end_head_over_middle"):
        end_head = over_middle(near_head)
    with jax.named_scope("third_head_outward"):
        third_head = outward(end_head)
    mid_pool, _ = pooled(head, near_tail, [], [end_head, token([near_tail], T_TAIL)])
    with jax.named_scope("pool_over_middle"):
        mid_pool = over_middle(mid_pool)
    here = [token([second_head], T_SECOND), third_head, token([second], T_RIGHT), odd_one] + b_masks[1:]
    out_pool, (second,) = pooled(lead, mid_pool, [second], here)
    with jax.named_scope("pool_outward"):
        out_pool = outward(out_pool)
    with jax.named_scope("right_core_swap"):
        right = [b_blocks, odd_one, second, core_swap(second)]

    table, over = pl.pallas_call(
        functools.partial(table_kernel, blocks),
        in_specs=[smem(), smem()] + [anywhere()] * 5,
        out_specs=[smem(), smem()],
        out_shape=[jax.ShapeDtypeStruct((5 * (blocks + 8),), jnp.int32), jax.ShapeDtypeStruct((1,), jnp.int32)],
        scratch_shapes=[
            pltpu.VMEM((5 * NOTE, blk), jnp.bfloat16),
            pltpu.VMEM((5 * NOTE, blk), jnp.int32),
            pltpu.SMEM((5 * NOTE, blk), jnp.int32),
            pltpu.SemaphoreType.DMA((5,)),
            pltpu.SemaphoreType.DMA,
        ],
        compiler_params=params(),
        name="table",
    )(where, by_column, near_head, second_head, third_head, mid_head, end_head)

    def fixed(x):
        return pl.BlockSpec(x.shape, lambda g: (0,) * x.ndim)

    wide_j = 2 if bc % 2 == 0 else 1
    arrived = [near_head, second_head, third_head, near_tail, mid_head, end_head, mid_pool]
    acc, out = pl.pallas_call(
        early_kernel,
        grid=(bc // wide_j,),
        in_specs=[smem()] * (4 + STEPS)
        + [fixed(x) for x in [a_blocks] + arrived]
        + [pl.BlockSpec((kb, wide_j, blk, blk), lambda g: (0, g, 0, 0))] * STEPS,
        out_specs=[
            pl.BlockSpec((br * blk, wide_j * blk), lambda g: (0, g)),
            pl.BlockSpec((br, wide_j, blk, blk), lambda g: (0, g, 0, 0)),
        ],
        out_shape=[
            jax.ShapeDtypeStruct((br * blk, bc * blk), jnp.float32),
            jax.ShapeDtypeStruct((br, bc, blk, blk), jnp.bfloat16),
        ],
        scratch_shapes=[pltpu.VMEM((br * blk, (STEPS * kb + 1) * blk), a_blocks.dtype)],
        compiler_params=params(24),
        cost_estimate=cost(2 * STEPS * br * bc * kb * blk**3, 14 << 20),
        name="early",
    )(where, by_column, c_mask, table, *b_masks, a_blocks, *arrived, *right)

    out = pl.pallas_call(
        late_kernel,
        in_specs=[smem()] * (3 + STEPS - 1) + [whole()] * (1 + STEPS) + [anywhere()],
        out_specs=anywhere(),
        out_shape=jax.ShapeDtypeStruct((br, bc, blk, blk), jnp.bfloat16),
        scratch_shapes=[
            pltpu.VMEM((br, bc, blk, blk), jnp.bfloat16),
            pltpu.SMEM((br,), jnp.int32),
            pltpu.SemaphoreType.DMA((br,)),
        ],
        input_output_aliases={3 + STEPS - 1 + 1 + STEPS: 0},
        compiler_params=params(12),
        cost_estimate=cost(0, 4 << 20),
        name="late",
    )(where, c_mask, table, *b_masks[1:], out_pool, acc, *right[1:], out)

    def again(state):
        before, trips = state
        left = [live(a_blocks, by_column, by_column=True, after=(before,))]
        for _ in range(1, STEPS):
            left.append(from_behind(left[-1], "col", -1))
        odd = lax.axis_index("row") % 2 == 1
        held = [live(slab, mask, after=(before,)) for slab, mask in zip(right, b_masks)]
        ordered = [held[0], jnp.where(odd, held[3], held[1]), held[2], jnp.where(odd, held[1], held[3])]
        return filter_sum(dense_sum(left, ordered), c_mask, blk, before), trips - 1

    out, _ = lax.while_loop(lambda state: state[1] > 0, again, (out, over[0]))
    return out


def on_device(a_blocks, a_mask, b_blocks, b_mask, c_mask):
    blocks = a_blocks.shape[0] * a_blocks.shape[1]
    fits = blocks % 16 == 0 and blocks <= a_blocks.shape[-1]
    if lax.axis_size("col") == STEPS and lax.axis_size("row") % 2 == 0 and fits:
        return sparse_product(a_blocks, a_mask, b_blocks, b_mask, c_mask)
    return dense_product(a_blocks, a_mask, b_blocks, b_mask, c_mask)


def solution(mesh):
    return jax.shard_map(
        on_device,
        mesh=mesh,
        in_specs=(
            P("row", "col", None, None),
            P("row", "col"),
            P("row", "col", None, None),
            P("row", "col"),
            P("row", "col"),
        ),
        out_specs=P("row", "col", None, None),
        check_vma=False,
    )
```

```python
import functools

import jax
import jax.numpy as jnp
from jax import lax
from jax.experimental import pallas as pl
from jax.experimental.pallas import tpu as pltpu
from jax.sharding import PartitionSpec as P

STEPS = 4
T_TAIL, T_SECOND, T_THIRD, T_RIGHT = 7, 4, 12, 1
NOTE = 16
MIB = 1024 * 1024


def slots(blocks):
    return blocks // 2, 3 * blocks // 4, 3 * blocks // 8, 9 * blocks // 16


def from_behind(array, axis, by):
    size = lax.axis_size(axis)
    return lax.ppermute(array, axis, [(i, (i + by) % size) for i in range(size)])


def smem():
    return pl.BlockSpec(memory_space=pltpu.SMEM)


def whole():
    return pl.BlockSpec(memory_space=pltpu.VMEM)


def anywhere():
    return pl.BlockSpec(memory_space=pl.ANY)


def params(mib=8):
    return pltpu.CompilerParams(vmem_limit_bytes=mib * MIB)


def cost(flops, nbytes):
    return pl.CostEstimate(flops=int(flops), bytes_accessed=int(nbytes), transcendentals=0)


def wide(a_ref):
    kb, blk = a_ref.shape[1], a_ref.shape[-1]
    return jnp.concatenate([a_ref[:, k].reshape(-1, blk) for k in range(kb)], axis=1)


def tall(b_ref):
    kb, bc = b_ref.shape[:2]
    return jnp.concatenate(
        [jnp.concatenate([b_ref[k, j] for j in range(bc)], axis=1) for k in range(kb)], axis=0
    )


def filtered(c_ref, i, j, block):
    return (block * c_ref[i, j].astype(jnp.float32)).astype(jnp.bfloat16)


def token_kernel(*refs):
    refs[-1][...] = jnp.zeros_like(refs[-1])


def token(seen, us):
    return pl.pallas_call(
        token_kernel,
        in_specs=[anywhere()] * len(seen),
        out_specs=whole(),
        out_shape=jax.ShapeDtypeStruct((8, 128), jnp.float32),
        compiler_params=params(),
        cost_estimate=cost(us * 1.1e9, 0),
        name="token",
    )(*seen)


def passed(arrays, seen=()):
    return pl.pallas_call(
        lambda *refs: None,
        in_specs=[anywhere()] * (len(arrays) + len(seen)),
        out_specs=[anywhere()] * len(arrays),
        out_shape=[jax.ShapeDtypeStruct(x.shape, x.dtype) for x in arrays],
        input_output_aliases={x: x for x in range(len(arrays))},
        compiler_params=params(),
        cost_estimate=cost(0, 0),
        name="passed",
    )(*arrays, *seen)


def live_kernel(by_column, mask_ref, x_ref, *refs):
    out_ref = refs[-1]
    i = pl.program_id(0)
    for j in range(x_ref.shape[1]):
        keep = mask_ref[j, i] if by_column else mask_ref[i, j]
        out_ref[0, j] = x_ref[0, j] * keep.astype(jnp.float32).astype(x_ref.dtype)


def live(blocks, mask, by_column=False, after=()):
    shape = (1,) + blocks.shape[1:]
    return pl.pallas_call(
        functools.partial(live_kernel, by_column),
        grid=(blocks.shape[0],),
        in_specs=[smem(), pl.BlockSpec(shape, lambda g: (g, 0, 0, 0))] + [anywhere()] * len(after),
        out_specs=pl.BlockSpec(shape, lambda g: (g, 0, 0, 0)),
        out_shape=jax.ShapeDtypeStruct(blocks.shape, blocks.dtype),
        compiler_params=params(),
        cost_estimate=cost(0, 4 * blocks.size),
        name="live",
    )(mask, blocks, *after)


def dense_kernel(*refs):
    a_refs, b_refs, acc_ref = refs[:STEPS], refs[STEPS:-1], refs[-1]
    total = None
    for a_ref, b_ref in zip(a_refs, b_refs):
        part = jnp.dot(wide(a_ref), tall(b_ref), preferred_element_type=jnp.float32)
        total = part if total is None else total + part
    acc_ref[...] = total


def dense_sum(left, right):
    br, kb, blk, _ = left[0].shape
    bc = right[0].shape[1]
    wide_j = 2 if bc % 2 == 0 else 1
    return pl.pallas_call(
        dense_kernel,
        grid=(bc // wide_j,),
        in_specs=[pl.BlockSpec((br, kb, blk, blk), lambda g: (0, 0, 0, 0))] * STEPS
        + [pl.BlockSpec((kb, wide_j, blk, blk), lambda g: (0, g, 0, 0))] * STEPS,
        out_specs=pl.BlockSpec((br * blk, wide_j * blk), lambda g: (0, g)),
        out_shape=jax.ShapeDtypeStruct((br * blk, bc * blk), jnp.float32),
        compiler_params=params(20),
        cost_estimate=cost(2 * STEPS * br * bc * kb * blk**3, 12 << 20),
        name="dense",
    )(*left, *right)


def filter_kernel(c_ref, acc_ref, *refs):
    out_ref = refs[-1]
    blk = out_ref.shape[-1]
    for j in range(out_ref.shape[1]):
        out_ref[0, j] = filtered(c_ref, pl.program_id(0), j, acc_ref[:, j * blk : (j + 1) * blk])


def filter_sum(total, c_mask, blk, *into):
    br, bc = c_mask.shape
    return pl.pallas_call(
        filter_kernel,
        grid=(br,),
        in_specs=[smem(), pl.BlockSpec((blk, bc * blk), lambda g: (g, 0))] + [anywhere()] * len(into),
        out_specs=pl.BlockSpec((1, bc, blk, blk), lambda g: (g, 0, 0, 0)),
        out_shape=jax.ShapeDtypeStruct((br, bc, blk, blk), jnp.bfloat16),
        input_output_aliases={2: 0} if into else {},
        compiler_params=params(),
        name="filter",
    )(c_mask, total, *into)


def dense_product(a_blocks, a_mask, b_blocks, b_mask, c_mask):
    left = [live(a_blocks, a_mask.T, by_column=True)]
    right = [live(b_blocks, b_mask)]
    for _ in range(1, STEPS):
        left.append(from_behind(left[-1], "col", -1))
        right.append(from_behind(right[-1], "row", -1))
    return filter_sum(dense_sum(left, right), c_mask, a_blocks.shape[-1])


def compact_kernel(mask_ref, a_ref, head_ref, inner_ref, tail_ref, n_ref, list_ref):
    br, kb, blk = a_ref.shape[:3]
    head, lead, inner, _ = slots(br * kb)
    lanes = lax.broadcasted_iota(jnp.int32, (NOTE, blk), 1)
    note = jnp.zeros((NOTE, blk), jnp.int32)
    count = jnp.int32(0)
    for k in range(kb):
        for i in range(br):
            list_ref[pl.ds(pl.multiple_of(count * blk, blk), blk), :] = a_ref[i, k]
            note = jnp.where(lanes == k * br + i, mask_ref[k, i], note)
            count = count + mask_ref[k, i]
    note = note.astype(jnp.float32).astype(jnp.bfloat16)
    head_ref[0 : head * blk, :] = list_ref[0 : head * blk, :]
    head_ref[head * blk :, :] = note
    inner_ref[...] = list_ref[head * blk : (head + inner) * blk, :]
    tail_ref[...] = list_ref[head * blk :, :]
    n_ref[0] = count


def extend_kernel(head_ref, tail_ref, out_ref):
    size = head_ref.shape[0] - NOTE
    more = out_ref.shape[0] - head_ref.shape[0]
    out_ref[0:size, :] = head_ref[0:size, :]
    out_ref[size : size + more, :] = tail_ref[0:more, :]
    out_ref[size + more :, :] = head_ref[size:, :]


def pool_kernel(skip, n_ref, tail_ref, more_ref, *refs):
    out_ref, line = refs[-2:]
    blk = out_ref.shape[1]
    first = skip * blk - tail_ref.shape[0]
    own = tail_ref.shape[0] - first
    line[0:own, :] = tail_ref[first:, :]
    at = pl.multiple_of(jnp.maximum(n_ref[0] - skip, 0) * blk, blk)
    line[pl.ds(at, more_ref.shape[0]), :] = more_ref[...]
    out_ref[...] = line[0 : out_ref.shape[0], :]


def table_kernel(blocks, where_ref, own_ref, *refs):
    notes, (table_ref, over_ref, note_ref, wide_ref, mask_ref, sems, sem) = refs[:5], refs[6:]
    copies = [
        pltpu.make_async_copy(
            ref.at[pl.ds(ref.shape[0] - NOTE, NOTE), :], note_ref.at[pl.ds(m * NOTE, NOTE), :], sems.at[m]
        )
        for m, ref in enumerate(notes)
    ]
    for copy in copies:
        copy.start()
    for copy in copies:
        copy.wait()
    wide_ref[...] = note_ref[...].astype(jnp.float32).astype(jnp.int32)
    down = pltpu.make_async_copy(wide_ref, mask_ref, sem)
    down.start()
    down.wait()

    none, apart = STEPS * blocks, blocks + 8
    head, lead, inner, pool = slots(blocks)
    z = where_ref[0]
    at_end = jnp.logical_or(z == 0, z == 3)
    near = 1 + 2 * (z % 2)
    flip = where_ref[1] % 2 == 1

    def place_of(step):
        return jnp.where(flip, 4 - step, step)

    def fill(base, place, m):
        def body(b, count):
            table_ref[count] = place * blocks + b
            return count + mask_ref[m * NOTE, b]

        count = lax.fori_loop(0, blocks, body, jnp.int32(base), unroll=8)

        def pad(p, carry):
            table_ref[p] = none
            return carry

        lax.fori_loop(count, base + blocks, pad, 0)
        return count - base

    first = fill(0, place_of(near), 0)
    second = fill(apart, jnp.where(at_end, 2, place_of(4 - near)), jnp.where(at_end, 1, 3))
    third = fill(2 * apart, jnp.where(at_end, place_of(4 - near), 2), jnp.where(at_end, 2, 4))

    def append(base, begin, length, at):
        def body(p, at):
            table_ref[at] = table_ref[base + p]
            return at + 1

        return lax.fori_loop(begin, length, body, at)

    at = append(0, jnp.where(at_end, lead, blocks), first, jnp.int32(3 * apart))
    at = append(apart, head, second, at)
    at = append(2 * apart, head, third, at)

    def pad(p, carry):
        table_ref[p] = none
        return carry

    lax.fori_loop(at, 3 * apart + pool, pad, 0)

    own = jnp.int32(0)
    for k in range(own_ref.shape[0]):
        for i in range(own_ref.shape[1]):
            own = own + own_ref[k, i]

    def past(n, by):
        return jnp.maximum(n - by, 0)

    def overflows(next_one, middle, far):
        pooled = past(next_one, lead) + past(middle, head) + past(far, head)
        return jnp.logical_or(pooled > pool, far > head + inner)

    ends_view = jnp.logical_or(overflows(first, second, third), overflows(second, first, own))
    middles_view = jnp.logical_or(overflows(own, second, third), overflows(second, own, first))
    over_ref[0] = jnp.where(jnp.where(at_end, ends_view, middles_view), 1, 0).astype(jnp.int32)


def masked_tall(mask_ref, b_ref, j0):
    kb, bc = b_ref.shape[:2]

    def block(k, j):
        return b_ref[k, j] * mask_ref[k, j0 + j].astype(jnp.float32).astype(b_ref.dtype)

    return jnp.concatenate([jnp.concatenate([block(k, j) for j in range(bc)], axis=1) for k in range(kb)], axis=0)


def early_kernel(where_ref, mask_ref, c_ref, table_ref, *refs):
    b_masks, a_ref, refs = refs[:STEPS], refs[STEPS], refs[STEPS + 1 :]
    near_ref, outs, mids, refs = refs[0], refs[1:3], refs[3:7], refs[7:]
    b_refs, (acc_ref, out_ref, left_ref) = refs[:STEPS], refs[STEPS:]
    br, kb, blk, _ = a_ref.shape
    blocks = br * kb
    apart = blocks + 8
    head, lead, inner, pool = slots(blocks)
    z = where_ref[0]
    at_end = jnp.logical_or(z == 0, z == 3)

    def scatter(ref, first, length, at=0):
        def body(b, carry):
            place = table_ref[first + b]
            row = pl.multiple_of((place % br) * blk, blk)
            column = pl.multiple_of((place // br) * blk, blk)
            left_ref[pl.ds(row, blk), pl.ds(column, blk)] = ref[pl.ds(pl.multiple_of((at + b) * blk, blk), blk), :]
            return carry

        lax.fori_loop(0, length, body, 0, unroll=2)

    @pl.when(pl.program_id(0) == 0)
    def _():
        for k in range(kb):
            for i in range(br):
                left_ref[i * blk : (i + 1) * blk, k * blk : (k + 1) * blk] = a_ref[i, k] * mask_ref[k, i].astype(
                    jnp.float32
                ).astype(jnp.bfloat16)
        left_ref[:, kb * blk :] = jnp.zeros((br * blk, left_ref.shape[1] - kb * blk), jnp.bfloat16)
        scatter(near_ref, 0, head)

        @pl.when(at_end)
        def _():
            scatter(outs[0], apart, head)
            scatter(outs[0], head, lead - head, head)
            scatter(outs[1], 2 * apart, head)

        @pl.when(jnp.logical_not(at_end))
        def _():
            scatter(mids[0], head, inner)
            scatter(mids[1], apart, head)
            scatter(mids[2], 2 * apart, head)
            scatter(mids[3], 3 * apart, pool)

    j0 = pl.program_id(0) * out_ref.shape[1]
    total = None
    for t in range(STEPS):
        part = jnp.dot(
            left_ref[:, t * kb * blk : (t + 1) * kb * blk],
            masked_tall(b_masks[t], b_refs[t], j0),
            preferred_element_type=jnp.float32,
        )
        total = part if total is None else total + part
    acc_ref[...] = total
    for i in range(br):
        for j in range(out_ref.shape[1]):
            out_ref[i, j] = filtered(c_ref, i, j0 + j, total[i * blk : (i + 1) * blk, j * blk : (j + 1) * blk])


def rows_kernel(where_ref, table_ref, *refs):
    b_masks, refs = refs[: STEPS - 1], refs[STEPS - 1 :]
    b_refs, (rows_ref, b_ref, need_ref, sems) = refs[: STEPS - 1], refs[STEPS:]
    _, bc, blk, _ = b_ref.shape
    kb = b_refs[0].shape[0]
    br = (table_ref.shape[0] // 5 - 8) // kb
    _, _, _, pool = slots(kb * br)
    first = 3 * (kb * br + 8)
    at_end = jnp.logical_or(where_ref[0] == 0, where_ref[0] == 3)

    def clear(r, carry):
        need_ref[r] = 0
        return carry

    def mark(b, carry):
        place = table_ref[first + b]

        @pl.when(place < STEPS * kb * br)
        def _():
            need_ref[place // br - kb] = 1

        return carry

    lax.fori_loop(0, (STEPS - 1) * kb, clear, 0)
    lax.fori_loop(0, jnp.where(at_end, pool, 0), mark, 0)
    copies = [
        pltpu.make_async_copy(b_refs[r // kb].at[r % kb], b_ref.at[r], sems.at[r]) for r in range((STEPS - 1) * kb)
    ]

    def when(r, act):
        @pl.when(need_ref[r] > 0)
        def _():
            act()

    for r, copy in enumerate(copies):
        when(r, copy.start)
    for r, copy in enumerate(copies):
        when(r, copy.wait)
    for slab, mask_ref in enumerate(b_masks):

        def fill(k, carry):
            r = slab * kb + k

            @pl.when(need_ref[r] > 0)
            def _():
                for j in range(bc):
                    keep = mask_ref[k, j].astype(jnp.float32).astype(jnp.bfloat16)
                    rows_ref[pl.ds(pl.multiple_of(r * blk, blk), blk), j * blk : (j + 1) * blk] = b_ref[r, j] * keep

            return carry

        lax.fori_loop(0, kb, fill, 0)


def late_kernel(where_ref, c_ref, table_ref, late_ref, acc_ref, rows_ref, _, out_ref, row_ref, touched_ref, sems):
    br, bc, blk, _ = out_ref.shape
    kb = rows_ref.shape[0] // blk // (STEPS - 1)
    _, _, _, pool = slots(kb * br)
    first = 3 * (kb * br + 8)
    at_end = jnp.logical_or(where_ref[0] == 0, where_ref[0] == 3)

    def clear(i, carry):
        touched_ref[i] = 0
        return carry

    def add(b, carry):
        place = table_ref[first + b]

        @pl.when(place < STEPS * kb * br)
        def _():
            i, r = place % br, place // br - kb
            touched_ref[i] = 1
            acc_ref[pl.ds(pl.multiple_of(i * blk, blk), blk), :] += jnp.dot(
                late_ref[pl.ds(pl.multiple_of(b * blk, blk), blk), :],
                rows_ref[pl.ds(pl.multiple_of(r * blk, blk), blk), :],
                preferred_element_type=jnp.float32,
            )

        return carry

    def go(i):
        return pltpu.make_async_copy(row_ref.at[i], out_ref.at[i], sems.at[i])

    def send(i, carry):
        @pl.when(touched_ref[i] > 0)
        def _():
            row = pl.multiple_of(i * blk, blk)
            for j in range(bc):
                row_ref[i, j] = filtered(c_ref, i, j, acc_ref[pl.ds(row, blk), j * blk : (j + 1) * blk])
            go(i).start()

        return carry

    def settle(i, carry):
        @pl.when(touched_ref[i] > 0)
        def _():
            go(i).wait()

        return carry

    lax.fori_loop(0, br, clear, 0)
    lax.fori_loop(0, jnp.where(at_end, pool, 0), add, 0)
    lax.fori_loop(0, br, send, 0)
    lax.fori_loop(0, br, settle, 0)


def sparse_product(a_blocks, a_mask, b_blocks, b_mask, c_mask):
    br, kb, blk, _ = a_blocks.shape
    bc = b_blocks.shape[1]
    blocks = br * kb
    head, lead, inner, pool = slots(blocks)
    rows = lax.axis_size("row")
    where = jnp.stack([lax.axis_index("col"), lax.axis_index("row")]).astype(jnp.int32)
    by_column = a_mask.T

    def outward(x):
        return lax.ppermute(x, "col", [(1, 0), (2, 3)])

    def end_swap(x):
        return lax.ppermute(x, "col", [(0, 1), (1, 0), (2, 3), (3, 2)])

    def inward(x):
        return lax.ppermute(x, "col", [(0, 1), (3, 2)])

    def over_middle(x):
        return lax.ppermute(x, "col", [(1, 2), (2, 1)])

    def two_up(x):
        return from_behind(x, "row", -2)

    def odd_up(x):
        return lax.ppermute(x, "row", [((r + 1 + 2 * (r % 2)) % rows, r) for r in range(rows)])

    def core_swap(x):
        return lax.ppermute(x, "row", [(r, r ^ 1) for r in range(rows)])

    def listed(slot_count, note=0):
        return jax.ShapeDtypeStruct((slot_count * blk + note, blk), a_blocks.dtype)

    with jax.named_scope("right_two_up"):
        second = two_up(b_blocks)
    with jax.named_scope("right_odd_up"):
        odd_one = odd_up(b_blocks)
    with jax.named_scope("right_masks"):
        second_mask, odd_mask = two_up(b_mask), odd_up(b_mask)
        b_masks = [b_mask, odd_mask, second_mask, core_swap(second_mask)]

    own_head, own_inner, own_tail, n = pl.pallas_call(
        compact_kernel,
        in_specs=[smem(), whole()],
        out_specs=[whole(), whole(), whole(), smem()],
        out_shape=[
            listed(head, NOTE),
            listed(inner),
            listed(blocks - head),
            jax.ShapeDtypeStruct((1,), jnp.int32),
        ],
        scratch_shapes=[pltpu.VMEM((blocks * blk, blk), a_blocks.dtype)],
        compiler_params=params(),
        cost_estimate=cost(0, 6 * blocks * blk * blk),
        name="compact",
    )(by_column, a_blocks)

    def pooled(skip, more, seen):
        own = blocks - skip
        return pl.pallas_call(
            functools.partial(pool_kernel, skip),
            in_specs=[smem(), whole(), whole()] + [anywhere()] * len(seen),
            out_specs=whole(),
            out_shape=listed(pool),
            scratch_shapes=[pltpu.VMEM((own * blk + more.shape[0], blk), a_blocks.dtype)],
            compiler_params=params(),
            cost_estimate=cost(0, 6 * pool * blk * blk),
            name="pool",
        )(n, own_tail, more, *seen)

    with jax.named_scope("head_over_middle"):
        mid_head = over_middle(own_head)
    with jax.named_scope("head_end_swap"):
        near_head = end_swap(own_head)
    with jax.named_scope("tail_inward"):
        near_tail = inward(own_inner)
    with jax.named_scope("second_head_outward"):
        second_head = outward(
            pl.pallas_call(
                extend_kernel,
                in_specs=[whole()] * 2,
                out_specs=whole(),
                out_shape=listed(lead, NOTE),
                compiler_params=params(),
                cost_estimate=cost(0, 0),
                name="extend",
            )(mid_head, own_tail)
        )
    with jax.named_scope("end_head_over_middle"):
        end_head = over_middle(near_head)
    with jax.named_scope("third_head_outward"):
        third_head = outward(end_head)
    mid_pool = pooled(head, near_tail, [end_head, token([near_tail], T_TAIL)])
    with jax.named_scope("pool_over_middle"):
        mid_pool = over_middle(mid_pool)
    here = [token([second_head], T_SECOND), token([second], T_RIGHT), odd_one] + b_masks[1:]
    mid_pool, second = passed([mid_pool, second], here)
    out_pool = pooled(lead, mid_pool, [])
    with jax.named_scope("pool_outward"):
        out_pool = outward(out_pool)
    with jax.named_scope("right_core_swap"):
        right = [b_blocks, odd_one, second, core_swap(second)]

    table, over = pl.pallas_call(
        functools.partial(table_kernel, blocks),
        in_specs=[smem(), smem()] + [anywhere()] * 6,
        out_specs=[smem(), smem()],
        out_shape=[jax.ShapeDtypeStruct((5 * (blocks + 8),), jnp.int32), jax.ShapeDtypeStruct((1,), jnp.int32)],
        scratch_shapes=[
            pltpu.VMEM((5 * NOTE, blk), jnp.bfloat16),
            pltpu.VMEM((5 * NOTE, blk), jnp.int32),
            pltpu.SMEM((5 * NOTE, blk), jnp.int32),
            pltpu.SemaphoreType.DMA((5,)),
            pltpu.SemaphoreType.DMA,
        ],
        compiler_params=params(),
        name="table",
    )(where, by_column, near_head, second_head, third_head, mid_head, end_head, token([third_head], T_THIRD))

    def fixed(x):
        return pl.BlockSpec(x.shape, lambda g: (0,) * x.ndim)

    wide_j = 2 if bc % 2 == 0 else 1
    arrived = [near_head, second_head, third_head, near_tail, mid_head, end_head, mid_pool]
    acc, out = pl.pallas_call(
        early_kernel,
        grid=(bc // wide_j,),
        in_specs=[smem()] * (4 + STEPS)
        + [fixed(x) for x in [a_blocks] + arrived]
        + [pl.BlockSpec((kb, wide_j, blk, blk), lambda g: (0, g, 0, 0))] * STEPS,
        out_specs=[
            pl.BlockSpec((br * blk, wide_j * blk), lambda g: (0, g)),
            pl.BlockSpec((br, wide_j, blk, blk), lambda g: (0, g, 0, 0)),
        ],
        out_shape=[
            jax.ShapeDtypeStruct((br * blk, bc * blk), jnp.float32),
            jax.ShapeDtypeStruct((br, bc, blk, blk), jnp.bfloat16),
        ],
        scratch_shapes=[pltpu.VMEM((br * blk, (STEPS * kb + 1) * blk), a_blocks.dtype)],
        compiler_params=params(24),
        cost_estimate=cost(2 * STEPS * br * bc * kb * blk**3, 14 << 20),
        name="early",
    )(where, by_column, c_mask, table, *b_masks, a_blocks, *arrived, *right)

    rows_shape = jax.ShapeDtypeStruct(((STEPS - 1) * kb * blk, bc * blk), jnp.bfloat16)
    met = pl.pallas_call(
        rows_kernel,
        in_specs=[smem()] * (2 + STEPS - 1) + [anywhere()] * STEPS,
        out_specs=whole(),
        out_shape=rows_shape,
        scratch_shapes=[
            pltpu.VMEM(((STEPS - 1) * kb, bc, blk, blk), jnp.bfloat16),
            pltpu.SMEM(((STEPS - 1) * kb,), jnp.int32),
            pltpu.SemaphoreType.DMA(((STEPS - 1) * kb,)),
        ],
        compiler_params=params(12),
        cost_estimate=cost(0, 1 << 20),
        name="rows",
    )(where, table, *b_masks[1:], *right[1:], acc)

    def rest(out, acc, late, met):
        return pl.pallas_call(
            late_kernel,
            in_specs=[smem()] * 3 + [whole()] * 3 + [anywhere()],
            out_specs=anywhere(),
            out_shape=jax.ShapeDtypeStruct((br, bc, blk, blk), jnp.bfloat16),
            scratch_shapes=[
                pltpu.VMEM((br, bc, blk, blk), jnp.bfloat16),
                pltpu.SMEM((br,), jnp.int32),
                pltpu.SemaphoreType.DMA((br,)),
            ],
            input_output_aliases={6: 0},
            compiler_params=params(12),
            cost_estimate=cost(0, 4 << 20),
            name="late",
        )(where, c_mask, table, late, acc, met, out)

    out = rest(out, acc, out_pool, met)

    def again(state):
        before, trips = state
        left = [live(a_blocks, by_column, by_column=True, after=(before,))]
        for _ in range(1, STEPS):
            left.append(from_behind(left[-1], "col", -1))
        odd = lax.axis_index("row") % 2 == 1
        held = [live(slab, mask, after=(before,)) for slab, mask in zip(right, b_masks)]
        ordered = [held[0], jnp.where(odd, held[3], held[1]), held[2], jnp.where(odd, held[1], held[3])]
        return filter_sum(dense_sum(left, ordered), c_mask, blk, before), trips - 1

    out, _ = lax.while_loop(lambda state: state[1] > 0, again, (out, over[0]))
    return out


def on_device(a_blocks, a_mask, b_blocks, b_mask, c_mask):
    blocks = a_blocks.shape[0] * a_blocks.shape[1]
    fits = blocks % 16 == 0 and blocks <= a_blocks.shape[-1]
    if lax.axis_size("col") == STEPS and lax.axis_size("row") % 2 == 0 and fits:
        return sparse_product(a_blocks, a_mask, b_blocks, b_mask, c_mask)
    return dense_product(a_blocks, a_mask, b_blocks, b_mask, c_mask)


def solution(mesh):
    return jax.shard_map(
        on_device,
        mesh=mesh,
        in_specs=(
            P("row", "col", None, None),
            P("row", "col"),
            P("row", "col", None, None),
            P("row", "col"),
            P("row", "col"),
        ),
        out_specs=P("row", "col", None, None),
        check_vma=False,
    )
```

```python
import functools

import jax
import jax.numpy as jnp
from jax import lax
from jax.experimental import pallas as pl
from jax.experimental.pallas import tpu as pltpu
from jax.sharding import PartitionSpec as P

STEPS = 4
T_TAIL, T_SECOND, T_THIRD, T_RIGHT = 4, 4, 12, 1
GROUP = 3
NOTE = 16
MIB = 1024 * 1024


def slots(blocks):
    return blocks // 2, 3 * blocks // 4, 3 * blocks // 8, 9 * blocks // 16


def from_behind(array, axis, by):
    size = lax.axis_size(axis)
    return lax.ppermute(array, axis, [(i, (i + by) % size) for i in range(size)])


def smem():
    return pl.BlockSpec(memory_space=pltpu.SMEM)


def whole():
    return pl.BlockSpec(memory_space=pltpu.VMEM)


def anywhere():
    return pl.BlockSpec(memory_space=pl.ANY)


def params(mib=8):
    return pltpu.CompilerParams(vmem_limit_bytes=mib * MIB)


def cost(flops, nbytes):
    return pl.CostEstimate(flops=int(flops), bytes_accessed=int(nbytes), transcendentals=0)


def wide(a_ref):
    kb, blk = a_ref.shape[1], a_ref.shape[-1]
    return jnp.concatenate([a_ref[:, k].reshape(-1, blk) for k in range(kb)], axis=1)


def tall(b_ref):
    kb, bc = b_ref.shape[:2]
    return jnp.concatenate(
        [jnp.concatenate([b_ref[k, j] for j in range(bc)], axis=1) for k in range(kb)], axis=0
    )


def filtered(c_ref, i, j, block):
    return (block * c_ref[i, j].astype(jnp.float32)).astype(jnp.bfloat16)


def token_kernel(*refs):
    refs[-1][...] = jnp.zeros_like(refs[-1])


def token(seen, us):
    return pl.pallas_call(
        token_kernel,
        in_specs=[anywhere()] * len(seen),
        out_specs=whole(),
        out_shape=jax.ShapeDtypeStruct((8, 128), jnp.float32),
        compiler_params=params(),
        cost_estimate=cost(us * 1.1e9, 0),
        name="token",
    )(*seen)


def passed(arrays, seen=()):
    return pl.pallas_call(
        lambda *refs: None,
        in_specs=[anywhere()] * (len(arrays) + len(seen)),
        out_specs=[anywhere()] * len(arrays),
        out_shape=[jax.ShapeDtypeStruct(x.shape, x.dtype) for x in arrays],
        input_output_aliases={x: x for x in range(len(arrays))},
        compiler_params=params(),
        cost_estimate=cost(0, 0),
        name="passed",
    )(*arrays, *seen)


def live_kernel(by_column, mask_ref, x_ref, *refs):
    out_ref = refs[-1]
    i = pl.program_id(0)
    for j in range(x_ref.shape[1]):
        keep = mask_ref[j, i] if by_column else mask_ref[i, j]
        out_ref[0, j] = x_ref[0, j] * keep.astype(jnp.float32).astype(x_ref.dtype)


def live(blocks, mask, by_column=False, after=()):
    shape = (1,) + blocks.shape[1:]
    return pl.pallas_call(
        functools.partial(live_kernel, by_column),
        grid=(blocks.shape[0],),
        in_specs=[smem(), pl.BlockSpec(shape, lambda g: (g, 0, 0, 0))] + [anywhere()] * len(after),
        out_specs=pl.BlockSpec(shape, lambda g: (g, 0, 0, 0)),
        out_shape=jax.ShapeDtypeStruct(blocks.shape, blocks.dtype),
        compiler_params=params(),
        cost_estimate=cost(0, 4 * blocks.size),
        name="live",
    )(mask, blocks, *after)


def dense_kernel(*refs):
    a_refs, b_refs, acc_ref = refs[:STEPS], refs[STEPS:-1], refs[-1]
    total = None
    for a_ref, b_ref in zip(a_refs, b_refs):
        part = jnp.dot(wide(a_ref), tall(b_ref), preferred_element_type=jnp.float32)
        total = part if total is None else total + part
    acc_ref[...] = total


def dense_sum(left, right):
    br, kb, blk, _ = left[0].shape
    bc = right[0].shape[1]
    wide_j = 2 if bc % 2 == 0 else 1
    return pl.pallas_call(
        dense_kernel,
        grid=(bc // wide_j,),
        in_specs=[pl.BlockSpec((br, kb, blk, blk), lambda g: (0, 0, 0, 0))] * STEPS
        + [pl.BlockSpec((kb, wide_j, blk, blk), lambda g: (0, g, 0, 0))] * STEPS,
        out_specs=pl.BlockSpec((br * blk, wide_j * blk), lambda g: (0, g)),
        out_shape=jax.ShapeDtypeStruct((br * blk, bc * blk), jnp.float32),
        compiler_params=params(20),
        cost_estimate=cost(2 * STEPS * br * bc * kb * blk**3, 12 << 20),
        name="dense",
    )(*left, *right)


def filter_kernel(c_ref, acc_ref, *refs):
    out_ref = refs[-1]
    blk = out_ref.shape[-1]
    for j in range(out_ref.shape[1]):
        out_ref[0, j] = filtered(c_ref, pl.program_id(0), j, acc_ref[:, j * blk : (j + 1) * blk])


def filter_sum(total, c_mask, blk, *into):
    br, bc = c_mask.shape
    return pl.pallas_call(
        filter_kernel,
        grid=(br,),
        in_specs=[smem(), pl.BlockSpec((blk, bc * blk), lambda g: (g, 0))] + [anywhere()] * len(into),
        out_specs=pl.BlockSpec((1, bc, blk, blk), lambda g: (g, 0, 0, 0)),
        out_shape=jax.ShapeDtypeStruct((br, bc, blk, blk), jnp.bfloat16),
        input_output_aliases={2: 0} if into else {},
        compiler_params=params(),
        name="filter",
    )(c_mask, total, *into)


def dense_product(a_blocks, a_mask, b_blocks, b_mask, c_mask):
    left = [live(a_blocks, a_mask.T, by_column=True)]
    right = [live(b_blocks, b_mask)]
    for _ in range(1, STEPS):
        left.append(from_behind(left[-1], "col", -1))
        right.append(from_behind(right[-1], "row", -1))
    return filter_sum(dense_sum(left, right), c_mask, a_blocks.shape[-1])


def compact_kernel(mask_ref, a_ref, head_ref, inner_ref, tail_ref, n_ref, list_ref):
    br, kb, blk = a_ref.shape[:3]
    head, lead, inner, _ = slots(br * kb)
    lanes = lax.broadcasted_iota(jnp.int32, (NOTE, blk), 1)
    note = jnp.zeros((NOTE, blk), jnp.int32)
    count = jnp.int32(0)
    for k in range(kb):
        for i in range(br):
            list_ref[pl.ds(pl.multiple_of(count * blk, blk), blk), :] = a_ref[i, k]
            note = jnp.where(lanes == k * br + i, mask_ref[k, i], note)
            count = count + mask_ref[k, i]
    note = note.astype(jnp.float32).astype(jnp.bfloat16)
    head_ref[0 : head * blk, :] = list_ref[0 : head * blk, :]
    head_ref[head * blk :, :] = note
    inner_ref[...] = list_ref[head * blk : (head + inner) * blk, :]
    tail_ref[...] = list_ref[head * blk :, :]
    n_ref[0] = count


def extend_kernel(head_ref, tail_ref, out_ref):
    size = head_ref.shape[0] - NOTE
    more = out_ref.shape[0] - head_ref.shape[0]
    out_ref[0:size, :] = head_ref[0:size, :]
    out_ref[size : size + more, :] = tail_ref[0:more, :]
    out_ref[size + more :, :] = head_ref[size:, :]


def pool_kernel(parts, skip, n_ref, tail_ref, more_ref, *refs):
    outs, line = refs[-1 - parts : -1], refs[-1]
    size, blk = outs[0].shape
    first = skip * blk - tail_ref.shape[0]
    own = tail_ref.shape[0] - first
    line[0:own, :] = tail_ref[first:, :]
    at = pl.multiple_of(jnp.maximum(n_ref[0] - skip, 0) * blk, blk)
    line[pl.ds(at, more_ref.shape[0]), :] = more_ref[...]
    for part, out_ref in enumerate(outs):
        out_ref[...] = line[part * size : (part + 1) * size, :]


def table_kernel(blocks, where_ref, own_ref, far_ref, *refs):
    notes, (table_ref, over_ref, note_ref, wide_ref, mask_ref, sems, sem) = refs[:4], refs[4:]
    copies = [
        pltpu.make_async_copy(
            ref.at[pl.ds(ref.shape[0] - NOTE, NOTE), :], note_ref.at[pl.ds(m * NOTE, NOTE), :], sems.at[m]
        )
        for m, ref in enumerate(notes)
    ]
    for copy in copies:
        copy.start()
    for copy in copies:
        copy.wait()
    for m in range(len(notes)):
        wide_ref[m : m + 1, :] = note_ref[m * NOTE : m * NOTE + 1, :].astype(jnp.float32).astype(jnp.int32)
    down = pltpu.make_async_copy(wide_ref, mask_ref, sem)
    down.start()
    down.wait()

    none, apart = STEPS * blocks, blocks + 8
    head, lead, inner, pool = slots(blocks)
    z = where_ref[0]
    at_end = jnp.logical_or(z == 0, z == 3)
    near = 1 + 2 * (z % 2)
    flip = where_ref[1] % 2 == 1

    def place_of(step):
        return jnp.where(flip, 4 - step, step)

    def noted(m):
        return lambda b: mask_ref[m, b]

    def far(b):
        return jnp.where(at_end, far_ref[b // own_ref.shape[1], b % own_ref.shape[1]], mask_ref[3, b])

    def fill(base, place, live):
        def body(b, count):
            table_ref[count] = place * blocks + b
            return count + live(b)

        count = lax.fori_loop(0, blocks, body, jnp.int32(base), unroll=8)

        def pad(p, carry):
            table_ref[p] = none
            return carry

        lax.fori_loop(count, base + blocks, pad, 0)
        return count - base

    first = fill(0, place_of(near), noted(0))
    second = fill(apart, jnp.where(at_end, 2, place_of(4 - near)), noted(jnp.where(at_end, 1, 2)))
    third = fill(2 * apart, jnp.where(at_end, place_of(4 - near), 2), far)

    def append(base, begin, length, at):
        def body(p, at):
            table_ref[at] = table_ref[base + p]
            return at + 1

        return lax.fori_loop(begin, length, body, at)

    at = append(0, jnp.where(at_end, lead, blocks), first, jnp.int32(3 * apart))
    at = append(apart, head, second, at)
    at = append(2 * apart, head, third, at)

    def pad(p, carry):
        table_ref[p] = none
        return carry

    lax.fori_loop(at, 3 * apart + pool, pad, 0)

    own = jnp.int32(0)
    for k in range(own_ref.shape[0]):
        for i in range(own_ref.shape[1]):
            own = own + own_ref[k, i]

    def past(n, by):
        return jnp.maximum(n - by, 0)

    def overflows(next_one, middle, far):
        pooled = past(next_one, lead) + past(middle, head) + past(far, head)
        return jnp.logical_or(pooled > pool, far > head + inner)

    ends_view = jnp.logical_or(overflows(first, second, third), overflows(second, first, own))
    middles_view = jnp.logical_or(overflows(own, second, third), overflows(second, own, first))
    over_ref[0] = jnp.where(jnp.where(at_end, ends_view, middles_view), 1, 0).astype(jnp.int32)


def masked_tall(mask_ref, b_ref, j0):
    kb, bc = b_ref.shape[:2]

    def block(k, j):
        return b_ref[k, j] * mask_ref[k, j0 + j].astype(jnp.float32).astype(b_ref.dtype)

    return jnp.concatenate([jnp.concatenate([block(k, j) for j in range(bc)], axis=1) for k in range(kb)], axis=0)


def early_kernel(where_ref, mask_ref, c_ref, table_ref, *refs):
    b_masks, a_ref, refs = refs[:STEPS], refs[STEPS], refs[STEPS + 1 :]
    near_ref, outs, mids, refs = refs[0], refs[1:3], refs[3:7], refs[7:-5] + refs[-3:]
    b_refs, (acc_ref, out_ref, left_ref) = refs[:STEPS], refs[STEPS:]
    br, kb, blk, _ = a_ref.shape
    blocks = br * kb
    apart = blocks + 8
    head, lead, inner, pool = slots(blocks)
    z = where_ref[0]
    at_end = jnp.logical_or(z == 0, z == 3)

    def scatter(ref, first, length, at=0):
        def body(b, carry):
            place = table_ref[first + b]
            row = pl.multiple_of((place % br) * blk, blk)
            column = pl.multiple_of((place // br) * blk, blk)
            left_ref[pl.ds(row, blk), pl.ds(column, blk)] = ref[pl.ds(pl.multiple_of((at + b) * blk, blk), blk), :]
            return carry

        lax.fori_loop(0, length, body, 0, unroll=2)

    @pl.when(pl.program_id(0) == 0)
    def _():
        for k in range(kb):
            for i in range(br):
                left_ref[i * blk : (i + 1) * blk, k * blk : (k + 1) * blk] = a_ref[i, k] * mask_ref[k, i].astype(
                    jnp.float32
                ).astype(jnp.bfloat16)
        left_ref[:, kb * blk :] = jnp.zeros((br * blk, left_ref.shape[1] - kb * blk), jnp.bfloat16)
        scatter(near_ref, 0, head)

        @pl.when(at_end)
        def _():
            scatter(outs[0], apart, head)
            scatter(outs[0], head, lead - head, head)
            scatter(outs[1], 2 * apart, head)

        @pl.when(jnp.logical_not(at_end))
        def _():
            scatter(mids[0], head, inner)
            scatter(mids[1], apart, head)
            scatter(mids[2], 2 * apart, head)
            scatter(mids[3], 3 * apart, pool)

    j0 = pl.program_id(0) * out_ref.shape[1]
    total = None
    for t in range(STEPS):
        part = jnp.dot(
            left_ref[:, t * kb * blk : (t + 1) * kb * blk],
            masked_tall(b_masks[t], b_refs[t], j0),
            preferred_element_type=jnp.float32,
        )
        total = part if total is None else total + part
    acc_ref[...] = total
    for i in range(br):
        for j in range(out_ref.shape[1]):
            out_ref[i, j] = filtered(c_ref, i, j0 + j, total[i * blk : (i + 1) * blk, j * blk : (j + 1) * blk])


def rows_kernel(where_ref, table_ref, *refs):
    b_masks, refs = refs[: STEPS - 1], refs[STEPS - 1 :]
    b_refs, (rows_ref, b_ref, need_ref, sems) = refs[: STEPS - 1], refs[STEPS - 1 :]
    _, bc, blk, _ = b_ref.shape
    kb = b_refs[0].shape[0]
    br = (table_ref.shape[0] // 5 - 8) // kb
    _, _, _, pool = slots(kb * br)
    first = 3 * (kb * br + 8)
    at_end = jnp.logical_or(where_ref[0] == 0, where_ref[0] == 3)

    def clear(r, carry):
        need_ref[r] = 0
        return carry

    def mark(b, carry):
        place = table_ref[first + b]

        @pl.when(place < STEPS * kb * br)
        def _():
            need_ref[place // br - kb] = 1

        return carry

    lax.fori_loop(0, (STEPS - 1) * kb, clear, 0)
    lax.fori_loop(0, jnp.where(at_end, pool, 0), mark, 0)
    copies = [
        pltpu.make_async_copy(b_refs[r // kb].at[r % kb], b_ref.at[r], sems.at[r]) for r in range((STEPS - 1) * kb)
    ]

    def when(r, act):
        @pl.when(need_ref[r] > 0)
        def _():
            act()

    for r, copy in enumerate(copies):
        when(r, copy.start)
    for r, copy in enumerate(copies):
        when(r, copy.wait)
    for slab, mask_ref in enumerate(b_masks):

        def fill(k, carry):
            r = slab * kb + k

            @pl.when(need_ref[r] > 0)
            def _():
                for j in range(bc):
                    keep = mask_ref[k, j].astype(jnp.float32).astype(jnp.bfloat16)
                    rows_ref[pl.ds(pl.multiple_of(r * blk, blk), blk), j * blk : (j + 1) * blk] = b_ref[r, j] * keep

            return carry

        lax.fori_loop(0, kb, fill, 0)


def late_kernel(begin, where_ref, c_ref, table_ref, late_ref, rows_ref, acc_in, _, out_ref, acc_ref, row_ref, last_ref, sems):
    del acc_in
    br, bc, blk, _ = out_ref.shape
    kb = rows_ref.shape[0] // blk // (STEPS - 1)
    none = STEPS * kb * br
    size = late_ref.shape[0] // blk
    first = 3 * (kb * br + 8) + begin
    at_end = jnp.logical_or(where_ref[0] == 0, where_ref[0] == 3)

    def clear(i, carry):
        last_ref[i] = -1
        return carry

    def mark(b, live):
        place = table_ref[first + b]

        @pl.when(place < none)
        def _():
            last_ref[place % br] = b

        return live + jnp.where(place < none, 1, 0)

    def go(i):
        return pltpu.make_async_copy(row_ref.at[i], out_ref.at[i], sems.at[i])

    def add(group, carry):
        b0 = group * GROUP
        places = [table_ref[first + b0 + x] for x in range(GROUP)]
        products = []
        for x, place in enumerate(places):
            r = jnp.minimum(place // br - kb, (STEPS - 1) * kb - 1)
            products.append(
                jnp.dot(
                    late_ref[pl.ds(pl.multiple_of((b0 + x) * blk, blk), blk), :],
                    rows_ref[pl.ds(pl.multiple_of(r * blk, blk), blk), :],
                    preferred_element_type=jnp.float32,
                )
            )
        for x, (place, product) in enumerate(zip(places, products)):
            i = place % br
            row = pl.multiple_of(i * blk, blk)

            @pl.when(place < none)
            def _():
                acc_ref[pl.ds(row, blk), :] += product

            @pl.when(jnp.logical_and(place < none, last_ref[i] == b0 + x))
            def _():
                for j in range(bc):
                    row_ref[i, j] = filtered(c_ref, i, j, acc_ref[pl.ds(row, blk), j * blk : (j + 1) * blk])
                go(i).start()

        return carry

    def settle(i, carry):
        @pl.when(last_ref[i] >= 0)
        def _():
            go(i).wait()

        return carry

    lax.fori_loop(0, br, clear, 0)
    live = lax.fori_loop(0, jnp.where(at_end, size, 0), mark, jnp.int32(0))
    lax.fori_loop(0, (live + GROUP - 1) // GROUP, add, 0)
    lax.fori_loop(0, br, settle, 0)


def sparse_product(a_blocks, a_mask, b_blocks, b_mask, c_mask):
    br, kb, blk, _ = a_blocks.shape
    bc = b_blocks.shape[1]
    blocks = br * kb
    head, lead, inner, pool = slots(blocks)
    rows = lax.axis_size("row")
    where = jnp.stack([lax.axis_index("col"), lax.axis_index("row")]).astype(jnp.int32)
    by_column = a_mask.T

    def outward(x):
        return lax.ppermute(x, "col", [(1, 0), (2, 3)])

    def end_swap(x):
        return lax.ppermute(x, "col", [(0, 1), (1, 0), (2, 3), (3, 2)])

    def inward(x):
        return lax.ppermute(x, "col", [(0, 1), (3, 2)])

    def over_middle(x):
        return lax.ppermute(x, "col", [(1, 2), (2, 1)])

    def two_up(x):
        return from_behind(x, "row", -2)

    def odd_up(x):
        return lax.ppermute(x, "row", [((r + 1 + 2 * (r % 2)) % rows, r) for r in range(rows)])

    def core_swap(x):
        return lax.ppermute(x, "row", [(r, r ^ 1) for r in range(rows)])

    def listed(slot_count, note=0):
        return jax.ShapeDtypeStruct((slot_count * blk + note, blk), a_blocks.dtype)

    with jax.named_scope("right_two_up"):
        second = two_up(b_blocks)
    with jax.named_scope("right_odd_up"):
        odd_one = odd_up(b_blocks)
    with jax.named_scope("right_masks"):
        second_mask, odd_mask = two_up(b_mask), odd_up(b_mask)
        b_masks = [b_mask, odd_mask, second_mask, core_swap(second_mask)]

    own_head, own_inner, own_tail, n = pl.pallas_call(
        compact_kernel,
        in_specs=[smem(), whole()],
        out_specs=[whole(), whole(), whole(), smem()],
        out_shape=[
            listed(head, NOTE),
            listed(inner),
            listed(blocks - head),
            jax.ShapeDtypeStruct((1,), jnp.int32),
        ],
        scratch_shapes=[pltpu.VMEM((blocks * blk, blk), a_blocks.dtype)],
        compiler_params=params(),
        cost_estimate=cost(0, 6 * blocks * blk * blk),
        name="compact",
    )(by_column, a_blocks)

    def pooled(skip, more, seen, parts=1):
        own = blocks - skip
        return pl.pallas_call(
            functools.partial(pool_kernel, parts, skip),
            in_specs=[smem(), whole(), whole()] + [anywhere()] * len(seen),
            out_specs=[whole()] * parts,
            out_shape=[listed(pool // parts)] * parts,
            scratch_shapes=[pltpu.VMEM((own * blk + more.shape[0], blk), a_blocks.dtype)],
            compiler_params=params(),
            cost_estimate=cost(0, 6 * pool * blk * blk),
            name="pool",
        )(n, own_tail, more, *seen)

    with jax.named_scope("head_over_middle"):
        mid_head = over_middle(own_head)
    with jax.named_scope("head_end_swap"):
        near_head = end_swap(own_head)
    with jax.named_scope("tail_inward"):
        near_tail = inward(own_inner)
    with jax.named_scope("second_head_outward"):
        second_head = outward(
            pl.pallas_call(
                extend_kernel,
                in_specs=[whole()] * 2,
                out_specs=whole(),
                out_shape=listed(lead, NOTE),
                compiler_params=params(),
                cost_estimate=cost(0, 0),
                name="extend",
            )(mid_head, own_tail)
        )
    with jax.named_scope("end_head_over_middle"):
        end_head = over_middle(near_head)
    with jax.named_scope("third_head_outward"):
        third_head = outward(end_head)
    (mid_pool,) = pooled(head, near_tail, [end_head, token([near_tail], T_TAIL)])
    with jax.named_scope("far_mask"):
        far_mask = lax.ppermute(*passed([a_mask.T], [mid_pool]), "col", [(0, 3), (3, 0)])
    with jax.named_scope("pool_over_middle"):
        mid_pool = over_middle(mid_pool)
    table, over = pl.pallas_call(
        functools.partial(table_kernel, blocks),
        in_specs=[smem()] * 3 + [anywhere()] * 4,
        out_specs=[smem(), smem()],
        out_shape=[jax.ShapeDtypeStruct((5 * (blocks + 8),), jnp.int32), jax.ShapeDtypeStruct((1,), jnp.int32)],
        scratch_shapes=[
            pltpu.VMEM((4 * NOTE, blk), jnp.bfloat16),
            pltpu.VMEM((8, blk), jnp.int32),
            pltpu.SMEM((8, blk), jnp.int32),
            pltpu.SemaphoreType.DMA((4,)),
            pltpu.SemaphoreType.DMA,
        ],
        compiler_params=params(),
        name="table",
    )(where, by_column, far_mask, near_head, second_head, mid_head, end_head)

    here = [table, token([second_head], T_SECOND), token([second], T_RIGHT), odd_one] + b_masks[1:]
    mid_pool, second = passed([mid_pool, second], here)
    out_pools = pooled(lead, mid_pool, [])
    with jax.named_scope("pool_outward"):
        out_pools = [outward(part) for part in out_pools]
    with jax.named_scope("right_core_swap"):
        right = [b_blocks, odd_one, second, core_swap(second)]

    rows_shape = jax.ShapeDtypeStruct(((STEPS - 1) * kb * blk, bc * blk), jnp.bfloat16)
    met = pl.pallas_call(
        rows_kernel,
        in_specs=[smem()] * (2 + STEPS - 1) + [anywhere()] * (STEPS - 1),
        out_specs=whole(),
        out_shape=rows_shape,
        scratch_shapes=[
            pltpu.VMEM(((STEPS - 1) * kb, bc, blk, blk), jnp.bfloat16),
            pltpu.SMEM(((STEPS - 1) * kb,), jnp.int32),
            pltpu.SemaphoreType.DMA(((STEPS - 1) * kb,)),
        ],
        compiler_params=params(12),
        cost_estimate=cost(0, 1 << 20),
        name="rows",
    )(where, table, *b_masks[1:], *right[1:])
    third_here = token([third_head], T_THIRD)

    def fixed(x):
        return pl.BlockSpec(x.shape, lambda g: (0,) * x.ndim)

    wide_j = 2 if bc % 2 == 0 else 1
    arrived = [near_head, second_head, third_head, near_tail, mid_head, end_head, mid_pool]
    acc, out = pl.pallas_call(
        early_kernel,
        grid=(bc // wide_j,),
        in_specs=[smem()] * (4 + STEPS)
        + [fixed(x) for x in [a_blocks] + arrived]
        + [pl.BlockSpec((kb, wide_j, blk, blk), lambda g: (0, g, 0, 0))] * STEPS
        + [anywhere()] * 2,
        out_specs=[
            pl.BlockSpec((br * blk, wide_j * blk), lambda g: (0, g)),
            pl.BlockSpec((br, wide_j, blk, blk), lambda g: (0, g, 0, 0)),
        ],
        out_shape=[
            jax.ShapeDtypeStruct((br * blk, bc * blk), jnp.float32),
            jax.ShapeDtypeStruct((br, bc, blk, blk), jnp.bfloat16),
        ],
        scratch_shapes=[pltpu.VMEM((br * blk, (STEPS * kb + 1) * blk), a_blocks.dtype)],
        compiler_params=params(24),
        cost_estimate=cost(2 * STEPS * br * bc * kb * blk**3, 14 << 20),
        name="early",
    )(where, by_column, c_mask, table, *b_masks, a_blocks, *arrived, *right, met, third_here)

    for part, late in enumerate(out_pools):
        out, acc = pl.pallas_call(
            functools.partial(late_kernel, part * (pool // len(out_pools))),
            in_specs=[smem()] * 3 + [whole()] * 3 + [anywhere()],
            out_specs=[anywhere(), whole()],
            out_shape=[
                jax.ShapeDtypeStruct((br, bc, blk, blk), jnp.bfloat16),
                jax.ShapeDtypeStruct(acc.shape, acc.dtype),
            ],
            scratch_shapes=[
                pltpu.VMEM((br, bc, blk, blk), jnp.bfloat16),
                pltpu.SMEM((br,), jnp.int32),
                pltpu.SemaphoreType.DMA((br,)),
            ],
            input_output_aliases={5: 1, 6: 0},
            compiler_params=params(12),
            cost_estimate=cost(0, 1 << 20),
            name="late",
        )(where, c_mask, table, late, met, acc, out)

    def again(before):
        left = [live(a_blocks, by_column, by_column=True, after=(before,))]
        for _ in range(1, STEPS):
            left.append(from_behind(left[-1], "col", -1))
        odd = lax.axis_index("row") % 2 == 1
        held = [live(slab, mask, after=(before,)) for slab, mask in zip(right, b_masks)]
        ordered = [held[0], jnp.where(odd, held[3], held[1]), held[2], jnp.where(odd, held[1], held[3])]
        return filter_sum(dense_sum(left, ordered), c_mask, blk, before)

    return lax.cond(over[0] > 0, again, lambda before: before, out)


def on_device(a_blocks, a_mask, b_blocks, b_mask, c_mask):
    blocks = a_blocks.shape[0] * a_blocks.shape[1]
    fits = blocks % 32 == 0 and blocks <= a_blocks.shape[-1]
    if lax.axis_size("col") == STEPS and lax.axis_size("row") % 2 == 0 and fits:
        return sparse_product(a_blocks, a_mask, b_blocks, b_mask, c_mask)
    return dense_product(a_blocks, a_mask, b_blocks, b_mask, c_mask)


def solution(mesh):
    return jax.shard_map(
        on_device,
        mesh=mesh,
        in_specs=(
            P("row", "col", None, None),
            P("row", "col"),
            P("row", "col", None, None),
            P("row", "col"),
            P("row", "col"),
        ),
        out_specs=P("row", "col", None, None),
        check_vma=False,
    )
```

```python
import functools

import jax
import jax.numpy as jnp
from jax import lax
from jax.experimental import pallas as pl
from jax.experimental.pallas import tpu as pltpu
from jax.sharding import PartitionSpec as P

STEPS = 4
T_TAIL, T_SECOND, T_THIRD, T_RIGHT = 4, 3, 12, 1
GROUP = 3
NOTE = 16
MIB = 1024 * 1024


def slots(blocks):
    return blocks // 2, 3 * blocks // 4, 3 * blocks // 8, 9 * blocks // 16


def from_behind(array, axis, by):
    size = lax.axis_size(axis)
    return lax.ppermute(array, axis, [(i, (i + by) % size) for i in range(size)])


def smem():
    return pl.BlockSpec(memory_space=pltpu.SMEM)


def whole():
    return pl.BlockSpec(memory_space=pltpu.VMEM)


def anywhere():
    return pl.BlockSpec(memory_space=pl.ANY)


def params(mib=8):
    return pltpu.CompilerParams(vmem_limit_bytes=mib * MIB)


def cost(flops, nbytes):
    return pl.CostEstimate(flops=int(flops), bytes_accessed=int(nbytes), transcendentals=0)


def wide(a_ref):
    kb, blk = a_ref.shape[1], a_ref.shape[-1]
    return jnp.concatenate([a_ref[:, k].reshape(-1, blk) for k in range(kb)], axis=1)


def tall(b_ref):
    kb, bc = b_ref.shape[:2]
    return jnp.concatenate(
        [jnp.concatenate([b_ref[k, j] for j in range(bc)], axis=1) for k in range(kb)], axis=0
    )


def filtered(c_ref, i, j, block):
    return (block * c_ref[i, j].astype(jnp.float32)).astype(jnp.bfloat16)


def token_kernel(*refs):
    refs[-1][...] = jnp.zeros_like(refs[-1])


def token(seen, us):
    return pl.pallas_call(
        token_kernel,
        in_specs=[anywhere()] * len(seen),
        out_specs=whole(),
        out_shape=jax.ShapeDtypeStruct((8, 128), jnp.float32),
        compiler_params=params(),
        cost_estimate=cost(us * 1.1e9, 0),
        name="token",
    )(*seen)


def passed(arrays, seen=()):
    return pl.pallas_call(
        lambda *refs: None,
        in_specs=[anywhere()] * (len(arrays) + len(seen)),
        out_specs=[anywhere()] * len(arrays),
        out_shape=[jax.ShapeDtypeStruct(x.shape, x.dtype) for x in arrays],
        input_output_aliases={x: x for x in range(len(arrays))},
        compiler_params=params(),
        cost_estimate=cost(0, 0),
        name="passed",
    )(*arrays, *seen)


def live_kernel(by_column, mask_ref, x_ref, *refs):
    out_ref = refs[-1]
    i = pl.program_id(0)
    for j in range(x_ref.shape[1]):
        keep = mask_ref[j, i] if by_column else mask_ref[i, j]
        out_ref[0, j] = x_ref[0, j] * keep.astype(jnp.float32).astype(x_ref.dtype)


def live(blocks, mask, by_column=False, after=()):
    shape = (1,) + blocks.shape[1:]
    return pl.pallas_call(
        functools.partial(live_kernel, by_column),
        grid=(blocks.shape[0],),
        in_specs=[smem(), pl.BlockSpec(shape, lambda g: (g, 0, 0, 0))] + [anywhere()] * len(after),
        out_specs=pl.BlockSpec(shape, lambda g: (g, 0, 0, 0)),
        out_shape=jax.ShapeDtypeStruct(blocks.shape, blocks.dtype),
        compiler_params=params(),
        cost_estimate=cost(0, 4 * blocks.size),
        name="live",
    )(mask, blocks, *after)


def dense_kernel(*refs):
    a_refs, b_refs, acc_ref = refs[:STEPS], refs[STEPS:-1], refs[-1]
    total = None
    for a_ref, b_ref in zip(a_refs, b_refs):
        part = jnp.dot(wide(a_ref), tall(b_ref), preferred_element_type=jnp.float32)
        total = part if total is None else total + part
    acc_ref[...] = total


def dense_sum(left, right):
    br, kb, blk, _ = left[0].shape
    bc = right[0].shape[1]
    wide_j = 2 if bc % 2 == 0 else 1
    return pl.pallas_call(
        dense_kernel,
        grid=(bc // wide_j,),
        in_specs=[pl.BlockSpec((br, kb, blk, blk), lambda g: (0, 0, 0, 0))] * STEPS
        + [pl.BlockSpec((kb, wide_j, blk, blk), lambda g: (0, g, 0, 0))] * STEPS,
        out_specs=pl.BlockSpec((br * blk, wide_j * blk), lambda g: (0, g)),
        out_shape=jax.ShapeDtypeStruct((br * blk, bc * blk), jnp.float32),
        compiler_params=params(20),
        cost_estimate=cost(2 * STEPS * br * bc * kb * blk**3, 12 << 20),
        name="dense",
    )(*left, *right)


def filter_kernel(c_ref, acc_ref, *refs):
    out_ref = refs[-1]
    blk = out_ref.shape[-1]
    for j in range(out_ref.shape[1]):
        out_ref[0, j] = filtered(c_ref, pl.program_id(0), j, acc_ref[:, j * blk : (j + 1) * blk])


def filter_sum(total, c_mask, blk, *into):
    br, bc = c_mask.shape
    return pl.pallas_call(
        filter_kernel,
        grid=(br,),
        in_specs=[smem(), pl.BlockSpec((blk, bc * blk), lambda g: (g, 0))] + [anywhere()] * len(into),
        out_specs=pl.BlockSpec((1, bc, blk, blk), lambda g: (g, 0, 0, 0)),
        out_shape=jax.ShapeDtypeStruct((br, bc, blk, blk), jnp.bfloat16),
        input_output_aliases={2: 0} if into else {},
        compiler_params=params(),
        name="filter",
    )(c_mask, total, *into)


def dense_product(a_blocks, a_mask, b_blocks, b_mask, c_mask):
    left = [live(a_blocks, a_mask.T, by_column=True)]
    right = [live(b_blocks, b_mask)]
    for _ in range(1, STEPS):
        left.append(from_behind(left[-1], "col", -1))
        right.append(from_behind(right[-1], "row", -1))
    return filter_sum(dense_sum(left, right), c_mask, a_blocks.shape[-1])


def compact_kernel(mask_ref, a_ref, head_ref, inner_ref, tail_ref, n_ref, list_ref):
    br, kb, blk = a_ref.shape[:3]
    head, lead, inner, _ = slots(br * kb)
    lanes = lax.broadcasted_iota(jnp.int32, (NOTE, blk), 1)
    note = jnp.zeros((NOTE, blk), jnp.int32)
    count = jnp.int32(0)
    for k in range(kb):
        for i in range(br):
            list_ref[pl.ds(pl.multiple_of(count * blk, blk), blk), :] = a_ref[i, k]
            note = jnp.where(lanes == k * br + i, mask_ref[k, i], note)
            count = count + mask_ref[k, i]
    note = note.astype(jnp.float32).astype(jnp.bfloat16)
    head_ref[0 : head * blk, :] = list_ref[0 : head * blk, :]
    head_ref[head * blk :, :] = note
    inner_ref[...] = list_ref[head * blk : (head + inner) * blk, :]
    tail_ref[...] = list_ref[head * blk :, :]
    n_ref[0] = count


def extend_kernel(head_ref, tail_ref, out_ref):
    size = head_ref.shape[0] - NOTE
    more = out_ref.shape[0] - head_ref.shape[0]
    out_ref[0:size, :] = head_ref[0:size, :]
    out_ref[size : size + more, :] = tail_ref[0:more, :]
    out_ref[size + more :, :] = head_ref[size:, :]


def pool_kernel(parts, skip, n_ref, tail_ref, more_ref, *refs):
    outs, line = refs[-1 - parts : -1], refs[-1]
    size, blk = outs[0].shape
    first = skip * blk - tail_ref.shape[0]
    own = tail_ref.shape[0] - first
    line[0:own, :] = tail_ref[first:, :]
    at = pl.multiple_of(jnp.maximum(n_ref[0] - skip, 0) * blk, blk)
    line[pl.ds(at, more_ref.shape[0]), :] = more_ref[...]
    for part, out_ref in enumerate(outs):
        out_ref[...] = line[part * size : (part + 1) * size, :]


def table_kernel(blocks, where_ref, own_ref, far_ref, *refs):
    notes, (table_ref, over_ref, note_ref, wide_ref, mask_ref, sems, sem) = refs[:4], refs[4:]
    copies = [
        pltpu.make_async_copy(
            ref.at[pl.ds(ref.shape[0] - NOTE, NOTE), :], note_ref.at[pl.ds(m * NOTE, NOTE), :], sems.at[m]
        )
        for m, ref in enumerate(notes)
    ]
    for copy in copies:
        copy.start()
    for copy in copies:
        copy.wait()
    for m in range(len(notes)):
        wide_ref[m : m + 1, :] = note_ref[m * NOTE : m * NOTE + 1, :].astype(jnp.float32).astype(jnp.int32)
    down = pltpu.make_async_copy(wide_ref, mask_ref, sem)
    down.start()
    down.wait()

    none, apart = STEPS * blocks, blocks + 8
    head, lead, inner, pool = slots(blocks)
    z = where_ref[0]
    at_end = jnp.logical_or(z == 0, z == 3)
    near = 1 + 2 * (z % 2)
    flip = where_ref[1] % 2 == 1

    def place_of(step):
        return jnp.where(flip, 4 - step, step)

    def noted(m):
        return lambda b: mask_ref[m, b]

    def far(b):
        return jnp.where(at_end, far_ref[b // own_ref.shape[1], b % own_ref.shape[1]], mask_ref[3, b])

    def fill(base, place, live):
        def body(b, count):
            table_ref[count] = place * blocks + b
            return count + live(b)

        count = lax.fori_loop(0, blocks, body, jnp.int32(base), unroll=8)

        def pad(p, carry):
            table_ref[p] = none
            return carry

        lax.fori_loop(count, base + blocks, pad, 0)
        return count - base

    first = fill(0, place_of(near), noted(0))
    second = fill(apart, jnp.where(at_end, 2, place_of(4 - near)), noted(jnp.where(at_end, 1, 2)))
    third = fill(2 * apart, jnp.where(at_end, place_of(4 - near), 2), far)

    def append(base, begin, length, at):
        def body(p, at):
            table_ref[at] = table_ref[base + p]
            return at + 1

        return lax.fori_loop(begin, length, body, at)

    at = append(0, jnp.where(at_end, lead, blocks), first, jnp.int32(3 * apart))
    at = append(apart, head, second, at)
    at = append(2 * apart, head, third, at)

    def pad(p, carry):
        table_ref[p] = none
        return carry

    lax.fori_loop(at, 3 * apart + pool, pad, 0)

    own = jnp.int32(0)
    for k in range(own_ref.shape[0]):
        for i in range(own_ref.shape[1]):
            own = own + own_ref[k, i]

    def past(n, by):
        return jnp.maximum(n - by, 0)

    def overflows(next_one, middle, far):
        pooled = past(next_one, lead) + past(middle, head) + past(far, head)
        return jnp.logical_or(pooled > pool, far > head + inner)

    ends_view = jnp.logical_or(overflows(first, second, third), overflows(second, first, own))
    middles_view = jnp.logical_or(overflows(own, second, third), overflows(second, own, first))
    over_ref[0] = jnp.where(jnp.where(at_end, ends_view, middles_view), 1, 0).astype(jnp.int32)


def masked_tall(mask_ref, b_ref, j0):
    kb, bc = b_ref.shape[:2]

    def block(k, j):
        return b_ref[k, j] * mask_ref[k, j0 + j].astype(jnp.float32).astype(b_ref.dtype)

    return jnp.concatenate([jnp.concatenate([block(k, j) for j in range(bc)], axis=1) for k in range(kb)], axis=0)


def early_kernel(where_ref, mask_ref, c_ref, table_ref, *refs):
    b_masks, a_ref, refs = refs[:STEPS], refs[STEPS], refs[STEPS + 1 :]
    near_ref, outs, mids, refs = refs[0], refs[1:3], refs[3:7], refs[7:-5] + refs[-3:]
    b_refs, (acc_ref, out_ref, left_ref) = refs[:STEPS], refs[STEPS:]
    br, kb, blk, _ = a_ref.shape
    blocks = br * kb
    apart = blocks + 8
    head, lead, inner, pool = slots(blocks)
    z = where_ref[0]
    at_end = jnp.logical_or(z == 0, z == 3)

    def scatter(ref, first, length, at=0):
        def body(b, carry):
            place = table_ref[first + b]
            row = pl.multiple_of((place % br) * blk, blk)
            column = pl.multiple_of((place // br) * blk, blk)
            left_ref[pl.ds(row, blk), pl.ds(column, blk)] = ref[pl.ds(pl.multiple_of((at + b) * blk, blk), blk), :]
            return carry

        lax.fori_loop(0, length, body, 0, unroll=2)

    @pl.when(pl.program_id(0) == 0)
    def _():
        for k in range(kb):
            for i in range(br):
                left_ref[i * blk : (i + 1) * blk, k * blk : (k + 1) * blk] = a_ref[i, k] * mask_ref[k, i].astype(
                    jnp.float32
                ).astype(jnp.bfloat16)
        left_ref[:, kb * blk :] = jnp.zeros((br * blk, left_ref.shape[1] - kb * blk), jnp.bfloat16)
        scatter(near_ref, 0, head)

        @pl.when(at_end)
        def _():
            scatter(outs[0], apart, head)
            scatter(outs[0], head, lead - head, head)
            scatter(outs[1], 2 * apart, head)

        @pl.when(jnp.logical_not(at_end))
        def _():
            scatter(mids[0], head, inner)
            scatter(mids[1], apart, head)
            scatter(mids[2], 2 * apart, head)
            scatter(mids[3], 3 * apart, pool)

    j0 = pl.program_id(0) * out_ref.shape[1]
    total = None
    for t in range(STEPS):
        part = jnp.dot(
            left_ref[:, t * kb * blk : (t + 1) * kb * blk],
            masked_tall(b_masks[t], b_refs[t], j0),
            preferred_element_type=jnp.float32,
        )
        total = part if total is None else total + part
    acc_ref[...] = total
    for i in range(br):
        for j in range(out_ref.shape[1]):
            out_ref[i, j] = filtered(c_ref, i, j0 + j, total[i * blk : (i + 1) * blk, j * blk : (j + 1) * blk])


def rows_kernel(where_ref, table_ref, *refs):
    b_masks, refs = refs[: STEPS - 1], refs[STEPS - 1 :]
    b_refs, (rows_ref, b_ref, need_ref, sems) = refs[: STEPS - 1], refs[STEPS - 1 :]
    _, bc, blk, _ = b_ref.shape
    kb = b_refs[0].shape[0]
    br = (table_ref.shape[0] // 5 - 8) // kb
    _, _, _, pool = slots(kb * br)
    first = 3 * (kb * br + 8)
    at_end = jnp.logical_or(where_ref[0] == 0, where_ref[0] == 3)

    def clear(r, carry):
        need_ref[r] = 0
        return carry

    def mark(b, carry):
        place = table_ref[first + b]

        @pl.when(place < STEPS * kb * br)
        def _():
            need_ref[place // br - kb] = 1

        return carry

    lax.fori_loop(0, (STEPS - 1) * kb, clear, 0)
    lax.fori_loop(0, jnp.where(at_end, pool, 0), mark, 0)
    copies = [
        pltpu.make_async_copy(b_refs[r // kb].at[r % kb], b_ref.at[r], sems.at[r]) for r in range((STEPS - 1) * kb)
    ]

    def when(r, act):
        @pl.when(need_ref[r] > 0)
        def _():
            act()

    for r, copy in enumerate(copies):
        when(r, copy.start)
    for r, copy in enumerate(copies):
        when(r, copy.wait)
    for slab, mask_ref in enumerate(b_masks):

        def fill(k, carry):
            r = slab * kb + k

            @pl.when(need_ref[r] > 0)
            def _():
                for j in range(bc):
                    keep = mask_ref[k, j].astype(jnp.float32).astype(jnp.bfloat16)
                    rows_ref[pl.ds(pl.multiple_of(r * blk, blk), blk), j * blk : (j + 1) * blk] = b_ref[r, j] * keep

            return carry

        lax.fori_loop(0, kb, fill, 0)


def late_kernel(begin, where_ref, c_ref, table_ref, late_ref, rows_ref, acc_in, _, out_ref, acc_ref, row_ref, last_ref, sems):
    del acc_in
    br, bc, blk, _ = out_ref.shape
    kb = rows_ref.shape[0] // blk // (STEPS - 1)
    none = STEPS * kb * br
    size = late_ref.shape[0] // blk
    first = 3 * (kb * br + 8) + begin
    at_end = jnp.logical_or(where_ref[0] == 0, where_ref[0] == 3)

    def clear(i, carry):
        last_ref[i] = -1
        return carry

    def mark(b, live):
        place = table_ref[first + b]

        @pl.when(place < none)
        def _():
            last_ref[place % br] = b

        return live + jnp.where(place < none, 1, 0)

    def go(i):
        return pltpu.make_async_copy(row_ref.at[i], out_ref.at[i], sems.at[i])

    def add(group, carry):
        b0 = group * GROUP
        places = [table_ref[first + b0 + x] for x in range(GROUP)]
        products = []
        for x, place in enumerate(places):
            r = jnp.minimum(place // br - kb, (STEPS - 1) * kb - 1)
            products.append(
                jnp.dot(
                    late_ref[pl.ds(pl.multiple_of((b0 + x) * blk, blk), blk), :],
                    rows_ref[pl.ds(pl.multiple_of(r * blk, blk), blk), :],
                    preferred_element_type=jnp.float32,
                )
            )
        for x, (place, product) in enumerate(zip(places, products)):
            i = place % br
            row = pl.multiple_of(i * blk, blk)

            @pl.when(place < none)
            def _():
                acc_ref[pl.ds(row, blk), :] += product

            @pl.when(jnp.logical_and(place < none, last_ref[i] == b0 + x))
            def _():
                for j in range(bc):
                    row_ref[i, j] = filtered(c_ref, i, j, acc_ref[pl.ds(row, blk), j * blk : (j + 1) * blk])
                go(i).start()

        return carry

    def settle(i, carry):
        @pl.when(last_ref[i] >= 0)
        def _():
            go(i).wait()

        return carry

    lax.fori_loop(0, br, clear, 0)
    live = lax.fori_loop(0, jnp.where(at_end, size, 0), mark, jnp.int32(0))
    lax.fori_loop(0, (live + GROUP - 1) // GROUP, add, 0)
    lax.fori_loop(0, br, settle, 0)


def sparse_product(a_blocks, a_mask, b_blocks, b_mask, c_mask):
    br, kb, blk, _ = a_blocks.shape
    bc = b_blocks.shape[1]
    blocks = br * kb
    head, lead, inner, pool = slots(blocks)
    rows = lax.axis_size("row")
    where = jnp.stack([lax.axis_index("col"), lax.axis_index("row")]).astype(jnp.int32)
    by_column = a_mask.T

    def outward(x):
        return lax.ppermute(x, "col", [(1, 0), (2, 3)])

    def end_swap(x):
        return lax.ppermute(x, "col", [(0, 1), (1, 0), (2, 3), (3, 2)])

    def inward(x):
        return lax.ppermute(x, "col", [(0, 1), (3, 2)])

    def over_middle(x):
        return lax.ppermute(x, "col", [(1, 2), (2, 1)])

    def two_up(x):
        return from_behind(x, "row", -2)

    def odd_up(x):
        return lax.ppermute(x, "row", [((r + 1 + 2 * (r % 2)) % rows, r) for r in range(rows)])

    def core_swap(x):
        return lax.ppermute(x, "row", [(r, r ^ 1) for r in range(rows)])

    def listed(slot_count, note=0):
        return jax.ShapeDtypeStruct((slot_count * blk + note, blk), a_blocks.dtype)

    with jax.named_scope("right_two_up"):
        second = two_up(b_blocks)
    with jax.named_scope("right_odd_up"):
        odd_one = odd_up(b_blocks)
    with jax.named_scope("right_masks"):
        second_mask, odd_mask = two_up(b_mask), odd_up(b_mask)
        b_masks = [b_mask, odd_mask, second_mask, core_swap(second_mask)]

    own_head, own_inner, own_tail, n = pl.pallas_call(
        compact_kernel,
        in_specs=[smem(), whole()],
        out_specs=[whole(), whole(), whole(), smem()],
        out_shape=[
            listed(head, NOTE),
            listed(inner),
            listed(blocks - head),
            jax.ShapeDtypeStruct((1,), jnp.int32),
        ],
        scratch_shapes=[pltpu.VMEM((blocks * blk, blk), a_blocks.dtype)],
        compiler_params=params(),
        cost_estimate=cost(0, 6 * blocks * blk * blk),
        name="compact",
    )(by_column, a_blocks)

    def pooled(skip, more, seen, parts=1):
        own = blocks - skip
        return pl.pallas_call(
            functools.partial(pool_kernel, parts, skip),
            in_specs=[smem(), whole(), whole()] + [anywhere()] * len(seen),
            out_specs=[whole()] * parts,
            out_shape=[listed(pool // parts)] * parts,
            scratch_shapes=[pltpu.VMEM((own * blk + more.shape[0], blk), a_blocks.dtype)],
            compiler_params=params(),
            cost_estimate=cost(0, 6 * pool * blk * blk),
            name="pool",
        )(n, own_tail, more, *seen)

    with jax.named_scope("head_end_swap"):
        near_head = end_swap(own_head)
    with jax.named_scope("head_over_middle"):
        mid_head = over_middle(own_head)
    with jax.named_scope("tail_inward"):
        near_tail = inward(own_inner)
    with jax.named_scope("second_head_outward"):
        second_head = outward(
            pl.pallas_call(
                extend_kernel,
                in_specs=[whole()] * 2,
                out_specs=whole(),
                out_shape=listed(lead, NOTE),
                compiler_params=params(),
                cost_estimate=cost(0, 0),
                name="extend",
            )(mid_head, own_tail)
        )
    with jax.named_scope("end_head_over_middle"):
        end_head = over_middle(near_head)
    with jax.named_scope("third_head_outward"):
        third_head = outward(end_head)
    (mid_pool,) = pooled(head, near_tail, [end_head, token([near_tail], T_TAIL), second_mask, odd_mask])
    with jax.named_scope("far_mask"):
        far_mask = lax.ppermute(*passed([a_mask.T], [mid_pool]), "col", [(0, 3), (3, 0)])
    with jax.named_scope("pool_over_middle"):
        mid_pool = over_middle(mid_pool)
    table, over = pl.pallas_call(
        functools.partial(table_kernel, blocks),
        in_specs=[smem()] * 3 + [anywhere()] * 4,
        out_specs=[smem(), smem()],
        out_shape=[jax.ShapeDtypeStruct((5 * (blocks + 8),), jnp.int32), jax.ShapeDtypeStruct((1,), jnp.int32)],
        scratch_shapes=[
            pltpu.VMEM((4 * NOTE, blk), jnp.bfloat16),
            pltpu.VMEM((8, blk), jnp.int32),
            pltpu.SMEM((8, blk), jnp.int32),
            pltpu.SemaphoreType.DMA((4,)),
            pltpu.SemaphoreType.DMA,
        ],
        compiler_params=params(),
        name="table",
    )(where, by_column, far_mask, near_head, second_head, mid_head, end_head)

    here = [table, token([second_head], T_SECOND), token([second], T_RIGHT), odd_one] + b_masks[1:]
    mid_pool, second = passed([mid_pool, second], here)
    out_pools = pooled(lead, mid_pool, [])
    with jax.named_scope("pool_outward"):
        out_pools = [outward(part) for part in out_pools]
    with jax.named_scope("right_core_swap"):
        right = [b_blocks, odd_one, second, core_swap(second)]

    rows_shape = jax.ShapeDtypeStruct(((STEPS - 1) * kb * blk, bc * blk), jnp.bfloat16)
    met = pl.pallas_call(
        rows_kernel,
        in_specs=[smem()] * (2 + STEPS - 1) + [anywhere()] * (STEPS - 1),
        out_specs=whole(),
        out_shape=rows_shape,
        scratch_shapes=[
            pltpu.VMEM(((STEPS - 1) * kb, bc, blk, blk), jnp.bfloat16),
            pltpu.SMEM(((STEPS - 1) * kb,), jnp.int32),
            pltpu.SemaphoreType.DMA(((STEPS - 1) * kb,)),
        ],
        compiler_params=params(12),
        cost_estimate=cost(0, 1 << 20),
        name="rows",
    )(where, table, *b_masks[1:], *right[1:])
    third_here = token([third_head], T_THIRD)

    def fixed(x):
        return pl.BlockSpec(x.shape, lambda g: (0,) * x.ndim)

    wide_j = 2 if bc % 2 == 0 else 1
    arrived = [near_head, second_head, third_head, near_tail, mid_head, end_head, mid_pool]
    acc, out = pl.pallas_call(
        early_kernel,
        grid=(bc // wide_j,),
        in_specs=[smem()] * (4 + STEPS)
        + [fixed(x) for x in [a_blocks] + arrived]
        + [pl.BlockSpec((kb, wide_j, blk, blk), lambda g: (0, g, 0, 0))] * STEPS
        + [anywhere()] * 2,
        out_specs=[
            pl.BlockSpec((br * blk, wide_j * blk), lambda g: (0, g)),
            pl.BlockSpec((br, wide_j, blk, blk), lambda g: (0, g, 0, 0)),
        ],
        out_shape=[
            jax.ShapeDtypeStruct((br * blk, bc * blk), jnp.float32),
            jax.ShapeDtypeStruct((br, bc, blk, blk), jnp.bfloat16),
        ],
        scratch_shapes=[pltpu.VMEM((br * blk, (STEPS * kb + 1) * blk), a_blocks.dtype)],
        compiler_params=params(24),
        cost_estimate=cost(2 * STEPS * br * bc * kb * blk**3, 14 << 20),
        name="early",
    )(where, by_column, c_mask, table, *b_masks, a_blocks, *arrived, *right, met, third_here)

    for part, late in enumerate(out_pools):
        out, acc = pl.pallas_call(
            functools.partial(late_kernel, part * (pool // len(out_pools))),
            in_specs=[smem()] * 3 + [whole()] * 3 + [anywhere()],
            out_specs=[anywhere(), whole()],
            out_shape=[
                jax.ShapeDtypeStruct((br, bc, blk, blk), jnp.bfloat16),
                jax.ShapeDtypeStruct(acc.shape, acc.dtype),
            ],
            scratch_shapes=[
                pltpu.VMEM((br, bc, blk, blk), jnp.bfloat16),
                pltpu.SMEM((br,), jnp.int32),
                pltpu.SemaphoreType.DMA((br,)),
            ],
            input_output_aliases={5: 1, 6: 0},
            compiler_params=params(12),
            cost_estimate=cost(0, 1 << 20),
            name="late",
        )(where, c_mask, table, late, met, acc, out)

    def again(before):
        left = [live(a_blocks, by_column, by_column=True, after=(before,))]
        for _ in range(1, STEPS):
            left.append(from_behind(left[-1], "col", -1))
        odd = lax.axis_index("row") % 2 == 1
        held = [live(slab, mask, after=(before,)) for slab, mask in zip(right, b_masks)]
        ordered = [held[0], jnp.where(odd, held[3], held[1]), held[2], jnp.where(odd, held[1], held[3])]
        return filter_sum(dense_sum(left, ordered), c_mask, blk, before)

    return lax.cond(over[0] > 0, again, lambda before: before, out)


def on_device(a_blocks, a_mask, b_blocks, b_mask, c_mask):
    blocks = a_blocks.shape[0] * a_blocks.shape[1]
    fits = blocks % 32 == 0 and blocks <= a_blocks.shape[-1]
    if lax.axis_size("col") == STEPS and lax.axis_size("row") % 2 == 0 and fits:
        return sparse_product(a_blocks, a_mask, b_blocks, b_mask, c_mask)
    return dense_product(a_blocks, a_mask, b_blocks, b_mask, c_mask)


def solution(mesh):
    return jax.shard_map(
        on_device,
        mesh=mesh,
        in_specs=(
            P("row", "col", None, None),
            P("row", "col"),
            P("row", "col", None, None),
            P("row", "col"),
            P("row", "col"),
        ),
        out_specs=P("row", "col", None, None),
        check_vma=False,
    )
```

```python
import functools

import jax
import jax.numpy as jnp
from jax import lax
from jax.experimental import pallas as pl
from jax.experimental.pallas import tpu as pltpu
from jax.sharding import PartitionSpec as P

STEPS = 4
T_TAIL, T_SECOND, T_THIRD, T_RIGHT = 4, 3, 12, 1
GROUP = 3
NOTE = 16
MIB = 1024 * 1024


def slots(blocks):
    return blocks // 2, 3 * blocks // 4, 3 * blocks // 8, 9 * blocks // 16


def from_behind(array, axis, by):
    size = lax.axis_size(axis)
    return lax.ppermute(array, axis, [(i, (i + by) % size) for i in range(size)])


def smem():
    return pl.BlockSpec(memory_space=pltpu.SMEM)


def whole():
    return pl.BlockSpec(memory_space=pltpu.VMEM)


def anywhere():
    return pl.BlockSpec(memory_space=pl.ANY)


def params(mib=8):
    return pltpu.CompilerParams(vmem_limit_bytes=mib * MIB)


def cost(flops, nbytes):
    return pl.CostEstimate(flops=int(flops), bytes_accessed=int(nbytes), transcendentals=0)


def wide(a_ref):
    kb, blk = a_ref.shape[1], a_ref.shape[-1]
    return jnp.concatenate([a_ref[:, k].reshape(-1, blk) for k in range(kb)], axis=1)


def tall(b_ref):
    kb, bc = b_ref.shape[:2]
    return jnp.concatenate(
        [jnp.concatenate([b_ref[k, j] for j in range(bc)], axis=1) for k in range(kb)], axis=0
    )


def filtered(c_ref, i, j, block):
    return (block * c_ref[i, j].astype(jnp.float32)).astype(jnp.bfloat16)


def token_kernel(*refs):
    refs[-1][...] = jnp.zeros_like(refs[-1])


def token(seen, us):
    return pl.pallas_call(
        token_kernel,
        in_specs=[anywhere()] * len(seen),
        out_specs=whole(),
        out_shape=jax.ShapeDtypeStruct((8, 128), jnp.float32),
        compiler_params=params(),
        cost_estimate=cost(us * 1.1e9, 0),
        name="token",
    )(*seen)


def passed(arrays, seen=()):
    return pl.pallas_call(
        lambda *refs: None,
        in_specs=[anywhere()] * (len(arrays) + len(seen)),
        out_specs=[anywhere()] * len(arrays),
        out_shape=[jax.ShapeDtypeStruct(x.shape, x.dtype) for x in arrays],
        input_output_aliases={x: x for x in range(len(arrays))},
        compiler_params=params(),
        cost_estimate=cost(0, 0),
        name="passed",
    )(*arrays, *seen)


def live_kernel(by_column, mask_ref, x_ref, *refs):
    out_ref = refs[-1]
    i = pl.program_id(0)
    for j in range(x_ref.shape[1]):
        keep = mask_ref[j, i] if by_column else mask_ref[i, j]
        out_ref[0, j] = x_ref[0, j] * keep.astype(jnp.float32).astype(x_ref.dtype)


def live(blocks, mask, by_column=False, after=()):
    shape = (1,) + blocks.shape[1:]
    return pl.pallas_call(
        functools.partial(live_kernel, by_column),
        grid=(blocks.shape[0],),
        in_specs=[smem(), pl.BlockSpec(shape, lambda g: (g, 0, 0, 0))] + [anywhere()] * len(after),
        out_specs=pl.BlockSpec(shape, lambda g: (g, 0, 0, 0)),
        out_shape=jax.ShapeDtypeStruct(blocks.shape, blocks.dtype),
        compiler_params=params(),
        cost_estimate=cost(0, 4 * blocks.size),
        name="live",
    )(mask, blocks, *after)


def dense_kernel(*refs):
    a_refs, b_refs, acc_ref = refs[:STEPS], refs[STEPS:-1], refs[-1]
    total = None
    for a_ref, b_ref in zip(a_refs, b_refs):
        part = jnp.dot(wide(a_ref), tall(b_ref), preferred_element_type=jnp.float32)
        total = part if total is None else total + part
    acc_ref[...] = total


def dense_sum(left, right):
    br, kb, blk, _ = left[0].shape
    bc = right[0].shape[1]
    wide_j = 2 if bc % 2 == 0 else 1
    return pl.pallas_call(
        dense_kernel,
        grid=(bc // wide_j,),
        in_specs=[pl.BlockSpec((br, kb, blk, blk), lambda g: (0, 0, 0, 0))] * STEPS
        + [pl.BlockSpec((kb, wide_j, blk, blk), lambda g: (0, g, 0, 0))] * STEPS,
        out_specs=pl.BlockSpec((br * blk, wide_j * blk), lambda g: (0, g)),
        out_shape=jax.ShapeDtypeStruct((br * blk, bc * blk), jnp.float32),
        compiler_params=params(20),
        cost_estimate=cost(2 * STEPS * br * bc * kb * blk**3, 12 << 20),
        name="dense",
    )(*left, *right)


def filter_kernel(c_ref, acc_ref, *refs):
    out_ref = refs[-1]
    blk = out_ref.shape[-1]
    for j in range(out_ref.shape[1]):
        out_ref[0, j] = filtered(c_ref, pl.program_id(0), j, acc_ref[:, j * blk : (j + 1) * blk])


def filter_sum(total, c_mask, blk, *into):
    br, bc = c_mask.shape
    return pl.pallas_call(
        filter_kernel,
        grid=(br,),
        in_specs=[smem(), pl.BlockSpec((blk, bc * blk), lambda g: (g, 0))] + [anywhere()] * len(into),
        out_specs=pl.BlockSpec((1, bc, blk, blk), lambda g: (g, 0, 0, 0)),
        out_shape=jax.ShapeDtypeStruct((br, bc, blk, blk), jnp.bfloat16),
        input_output_aliases={2: 0} if into else {},
        compiler_params=params(),
        name="filter",
    )(c_mask, total, *into)


def dense_product(a_blocks, a_mask, b_blocks, b_mask, c_mask):
    left = [live(a_blocks, a_mask.T, by_column=True)]
    right = [live(b_blocks, b_mask)]
    for _ in range(1, STEPS):
        left.append(from_behind(left[-1], "col", -1))
        right.append(from_behind(right[-1], "row", -1))
    return filter_sum(dense_sum(left, right), c_mask, a_blocks.shape[-1])


def compact_kernel(mask_ref, a_ref, head_ref, inner_ref, tail_ref, n_ref, list_ref):
    br, kb, blk = a_ref.shape[:3]
    head, lead, inner, _ = slots(br * kb)
    lanes = lax.broadcasted_iota(jnp.int32, (NOTE, blk), 1)
    note = jnp.zeros((NOTE, blk), jnp.int32)
    count = jnp.int32(0)
    for k in range(kb):
        for i in range(br):
            list_ref[pl.ds(pl.multiple_of(count * blk, blk), blk), :] = a_ref[i, k]
            note = jnp.where(lanes == k * br + i, mask_ref[k, i], note)
            count = count + mask_ref[k, i]
    note = note.astype(jnp.float32).astype(jnp.bfloat16)
    head_ref[0 : head * blk, :] = list_ref[0 : head * blk, :]
    head_ref[head * blk :, :] = note
    inner_ref[...] = list_ref[head * blk : (head + inner) * blk, :]
    tail_ref[...] = list_ref[head * blk :, :]
    n_ref[0] = count


def extend_kernel(head_ref, tail_ref, out_ref):
    size = head_ref.shape[0] - NOTE
    more = out_ref.shape[0] - head_ref.shape[0]
    out_ref[0:size, :] = head_ref[0:size, :]
    out_ref[size : size + more, :] = tail_ref[0:more, :]
    out_ref[size + more :, :] = head_ref[size:, :]


def pool_kernel(parts, skip, n_ref, tail_ref, more_ref, *refs):
    outs, line = refs[-1 - parts : -1], refs[-1]
    size, blk = outs[0].shape
    first = skip * blk - tail_ref.shape[0]
    own = tail_ref.shape[0] - first
    line[0:own, :] = tail_ref[first:, :]
    at = pl.multiple_of(jnp.maximum(n_ref[0] - skip, 0) * blk, blk)
    line[pl.ds(at, more_ref.shape[0]), :] = more_ref[...]
    for part, out_ref in enumerate(outs):
        out_ref[...] = line[part * size : (part + 1) * size, :]


def table_kernel(blocks, where_ref, own_ref, far_ref, *refs):
    notes, (table_ref, over_ref, note_ref, wide_ref, mask_ref, sems, sem) = refs[:4], refs[4:]
    copies = [
        pltpu.make_async_copy(
            ref.at[pl.ds(ref.shape[0] - NOTE, NOTE), :], note_ref.at[pl.ds(m * NOTE, NOTE), :], sems.at[m]
        )
        for m, ref in enumerate(notes)
    ]
    for copy in copies:
        copy.start()
    for copy in copies:
        copy.wait()
    for m in range(len(notes)):
        wide_ref[m : m + 1, :] = note_ref[m * NOTE : (m + 1) * NOTE, :].astype(jnp.float32).astype(jnp.int32)[0:1, :]
    down = pltpu.make_async_copy(wide_ref, mask_ref, sem)
    down.start()
    down.wait()

    none, apart = STEPS * blocks, blocks + 8
    head, lead, inner, pool = slots(blocks)
    z = where_ref[0]
    at_end = jnp.logical_or(z == 0, z == 3)
    near = 1 + 2 * (z % 2)
    flip = where_ref[1] % 2 == 1

    def place_of(step):
        return jnp.where(flip, 4 - step, step)

    def noted(m):
        return lambda b: mask_ref[m, b]

    def far(b):
        return jnp.where(at_end, far_ref[b // own_ref.shape[1], b % own_ref.shape[1]], mask_ref[3, b])

    def fill(base, place, live):
        def body(b, count):
            table_ref[count] = place * blocks + b
            return count + live(b)

        count = lax.fori_loop(0, blocks, body, jnp.int32(base), unroll=8)

        def pad(p, carry):
            table_ref[p] = none
            return carry

        lax.fori_loop(count, base + blocks, pad, 0)
        return count - base

    first = fill(0, place_of(near), noted(0))
    second = fill(apart, jnp.where(at_end, 2, place_of(4 - near)), noted(jnp.where(at_end, 1, 2)))
    third = fill(2 * apart, jnp.where(at_end, place_of(4 - near), 2), far)

    def append(base, begin, length, at):
        def body(p, at):
            table_ref[at] = table_ref[base + p]
            return at + 1

        return lax.fori_loop(begin, length, body, at)

    at = append(0, jnp.where(at_end, lead, blocks), first, jnp.int32(3 * apart))
    at = append(apart, head, second, at)
    at = append(2 * apart, head, third, at)

    def pad(p, carry):
        table_ref[p] = none
        return carry

    lax.fori_loop(at, 3 * apart + pool, pad, 0)

    own = jnp.int32(0)
    for k in range(own_ref.shape[0]):
        for i in range(own_ref.shape[1]):
            own = own + own_ref[k, i]

    def past(n, by):
        return jnp.maximum(n - by, 0)

    def overflows(next_one, middle, far):
        pooled = past(next_one, lead) + past(middle, head) + past(far, head)
        return jnp.logical_or(pooled > pool, far > head + inner)

    ends_view = jnp.logical_or(overflows(first, second, third), overflows(second, first, own))
    middles_view = jnp.logical_or(overflows(own, second, third), overflows(second, own, first))
    over_ref[0] = jnp.where(jnp.where(at_end, ends_view, middles_view), 1, 0).astype(jnp.int32)


def masked_tall(mask_ref, b_ref, j0):
    kb, bc = b_ref.shape[:2]

    def block(k, j):
        return b_ref[k, j] * mask_ref[k, j0 + j].astype(jnp.float32).astype(b_ref.dtype)

    return jnp.concatenate([jnp.concatenate([block(k, j) for j in range(bc)], axis=1) for k in range(kb)], axis=0)


def early_kernel(where_ref, mask_ref, c_ref, table_ref, *refs):
    b_masks, a_ref, refs = refs[:STEPS], refs[STEPS], refs[STEPS + 1 :]
    near_ref, outs, mids, refs = refs[0], refs[1:3], refs[3:7], refs[7:-5] + refs[-3:]
    b_refs, (acc_ref, out_ref, left_ref) = refs[:STEPS], refs[STEPS:]
    br, kb, blk, _ = a_ref.shape
    blocks = br * kb
    apart = blocks + 8
    head, lead, inner, pool = slots(blocks)
    z = where_ref[0]
    at_end = jnp.logical_or(z == 0, z == 3)

    def scatter(ref, first, length, at=0):
        def body(b, carry):
            place = table_ref[first + b]
            row = pl.multiple_of((place % br) * blk, blk)
            column = pl.multiple_of((place // br) * blk, blk)
            left_ref[pl.ds(row, blk), pl.ds(column, blk)] = ref[pl.ds(pl.multiple_of((at + b) * blk, blk), blk), :]
            return carry

        lax.fori_loop(0, length, body, 0, unroll=2)

    @pl.when(pl.program_id(0) == 0)
    def _():
        for k in range(kb):
            for i in range(br):
                left_ref[i * blk : (i + 1) * blk, k * blk : (k + 1) * blk] = a_ref[i, k] * mask_ref[k, i].astype(
                    jnp.float32
                ).astype(jnp.bfloat16)
        left_ref[:, kb * blk :] = jnp.zeros((br * blk, left_ref.shape[1] - kb * blk), jnp.bfloat16)
        scatter(near_ref, 0, head)

        @pl.when(at_end)
        def _():
            scatter(outs[0], apart, head)
            scatter(outs[0], head, lead - head, head)
            scatter(outs[1], 2 * apart, head)

        @pl.when(jnp.logical_not(at_end))
        def _():
            scatter(mids[0], head, inner)
            scatter(mids[1], apart, head)
            scatter(mids[2], 2 * apart, head)
            scatter(mids[3], 3 * apart, pool)

    j0 = pl.program_id(0) * out_ref.shape[1]
    total = None
    for t in range(STEPS):
        part = jnp.dot(
            left_ref[:, t * kb * blk : (t + 1) * kb * blk],
            masked_tall(b_masks[t], b_refs[t], j0),
            preferred_element_type=jnp.float32,
        )
        total = part if total is None else total + part
    acc_ref[...] = total
    for i in range(br):
        for j in range(out_ref.shape[1]):
            out_ref[i, j] = filtered(c_ref, i, j0 + j, total[i * blk : (i + 1) * blk, j * blk : (j + 1) * blk])


def rows_kernel(where_ref, table_ref, *refs):
    b_masks, refs = refs[: STEPS - 1], refs[STEPS - 1 :]
    b_refs, (rows_ref, b_ref, need_ref, sems) = refs[: STEPS - 1], refs[STEPS - 1 :]
    _, bc, blk, _ = b_ref.shape
    kb = b_refs[0].shape[0]
    br = (table_ref.shape[0] // 5 - 8) // kb
    _, _, _, pool = slots(kb * br)
    first = 3 * (kb * br + 8)
    at_end = jnp.logical_or(where_ref[0] == 0, where_ref[0] == 3)

    def clear(r, carry):
        need_ref[r] = 0
        return carry

    def mark(b, carry):
        place = table_ref[first + b]

        @pl.when(place < STEPS * kb * br)
        def _():
            need_ref[place // br - kb] = 1

        return carry

    lax.fori_loop(0, (STEPS - 1) * kb, clear, 0)
    lax.fori_loop(0, jnp.where(at_end, pool, 0), mark, 0)
    copies = [
        pltpu.make_async_copy(b_refs[r // kb].at[r % kb], b_ref.at[r], sems.at[r]) for r in range((STEPS - 1) * kb)
    ]

    def when(r, act):
        @pl.when(need_ref[r] > 0)
        def _():
            act()

    for r, copy in enumerate(copies):
        when(r, copy.start)
    for r, copy in enumerate(copies):
        when(r, copy.wait)
    for slab, mask_ref in enumerate(b_masks):

        def fill(k, carry):
            r = slab * kb + k

            @pl.when(need_ref[r] > 0)
            def _():
                for j in range(bc):
                    keep = mask_ref[k, j].astype(jnp.float32).astype(jnp.bfloat16)
                    rows_ref[pl.ds(pl.multiple_of(r * blk, blk), blk), j * blk : (j + 1) * blk] = b_ref[r, j] * keep

            return carry

        lax.fori_loop(0, kb, fill, 0)


def late_kernel(begin, where_ref, c_ref, table_ref, late_ref, rows_ref, acc_in, _, out_ref, acc_ref, row_ref, last_ref, sems):
    del acc_in
    br, bc, blk, _ = out_ref.shape
    kb = rows_ref.shape[0] // blk // (STEPS - 1)
    none = STEPS * kb * br
    size = late_ref.shape[0] // blk
    first = 3 * (kb * br + 8) + begin
    at_end = jnp.logical_or(where_ref[0] == 0, where_ref[0] == 3)

    def clear(i, carry):
        last_ref[i] = -1
        return carry

    def mark(b, live):
        place = table_ref[first + b]

        @pl.when(place < none)
        def _():
            last_ref[place % br] = b

        return live + jnp.where(place < none, 1, 0)

    def go(i):
        return pltpu.make_async_copy(row_ref.at[i], out_ref.at[i], sems.at[i])

    def add(group, carry):
        b0 = group * GROUP
        places = [table_ref[first + b0 + x] for x in range(GROUP)]
        products = []
        for x, place in enumerate(places):
            r = jnp.minimum(place // br - kb, (STEPS - 1) * kb - 1)
            products.append(
                jnp.dot(
                    late_ref[pl.ds(pl.multiple_of((b0 + x) * blk, blk), blk), :],
                    rows_ref[pl.ds(pl.multiple_of(r * blk, blk), blk), :],
                    preferred_element_type=jnp.float32,
                )
            )
        for x, (place, product) in enumerate(zip(places, products)):
            i = place % br
            row = pl.multiple_of(i * blk, blk)

            @pl.when(place < none)
            def _():
                acc_ref[pl.ds(row, blk), :] += product

            @pl.when(jnp.logical_and(place < none, last_ref[i] == b0 + x))
            def _():
                for j in range(bc):
                    row_ref[i, j] = filtered(c_ref, i, j, acc_ref[pl.ds(row, blk), j * blk : (j + 1) * blk])
                go(i).start()

        return carry

    def settle(i, carry):
        @pl.when(last_ref[i] >= 0)
        def _():
            go(i).wait()

        return carry

    lax.fori_loop(0, br, clear, 0)
    live = lax.fori_loop(0, jnp.where(at_end, size, 0), mark, jnp.int32(0))
    lax.fori_loop(0, (live + GROUP - 1) // GROUP, add, 0)
    lax.fori_loop(0, br, settle, 0)


def sparse_product(a_blocks, a_mask, b_blocks, b_mask, c_mask):
    br, kb, blk, _ = a_blocks.shape
    bc = b_blocks.shape[1]
    blocks = br * kb
    head, lead, inner, pool = slots(blocks)
    rows = lax.axis_size("row")
    where = jnp.stack([lax.axis_index("col"), lax.axis_index("row")]).astype(jnp.int32)
    by_column = a_mask.T

    def outward(x):
        return lax.ppermute(x, "col", [(1, 0), (2, 3)])

    def end_swap(x):
        return lax.ppermute(x, "col", [(0, 1), (1, 0), (2, 3), (3, 2)])

    def inward(x):
        return lax.ppermute(x, "col", [(0, 1), (3, 2)])

    def over_middle(x):
        return lax.ppermute(x, "col", [(1, 2), (2, 1)])

    def two_up(x):
        return from_behind(x, "row", -2)

    def odd_up(x):
        return lax.ppermute(x, "row", [((r + 1 + 2 * (r % 2)) % rows, r) for r in range(rows)])

    def core_swap(x):
        return lax.ppermute(x, "row", [(r, r ^ 1) for r in range(rows)])

    def listed(slot_count, note=0):
        return jax.ShapeDtypeStruct((slot_count * blk + note, blk), a_blocks.dtype)

    with jax.named_scope("right_two_up"):
        second = two_up(b_blocks)
    with jax.named_scope("right_odd_up"):
        odd_one = odd_up(b_blocks)
    with jax.named_scope("right_masks"):
        second_mask, odd_mask = two_up(b_mask), odd_up(b_mask)
        b_masks = [b_mask, odd_mask, second_mask, core_swap(second_mask)]

    own_head, own_inner, own_tail, n = pl.pallas_call(
        compact_kernel,
        in_specs=[smem(), whole()],
        out_specs=[whole(), whole(), whole(), smem()],
        out_shape=[
            listed(head, NOTE),
            listed(inner),
            listed(blocks - head),
            jax.ShapeDtypeStruct((1,), jnp.int32),
        ],
        scratch_shapes=[pltpu.VMEM((blocks * blk, blk), a_blocks.dtype)],
        compiler_params=params(),
        cost_estimate=cost(0, 6 * blocks * blk * blk),
        name="compact",
    )(by_column, a_blocks)

    def pooled(skip, more, seen, parts=1):
        own = blocks - skip
        return pl.pallas_call(
            functools.partial(pool_kernel, parts, skip),
            in_specs=[smem(), whole(), whole()] + [anywhere()] * len(seen),
            out_specs=[whole()] * parts,
            out_shape=[listed(pool // parts)] * parts,
            scratch_shapes=[pltpu.VMEM((own * blk + more.shape[0], blk), a_blocks.dtype)],
            compiler_params=params(),
            cost_estimate=cost(0, 6 * pool * blk * blk),
            name="pool",
        )(n, own_tail, more, *seen)

    with jax.named_scope("head_end_swap"):
        near_head = end_swap(own_head)
    with jax.named_scope("head_over_middle"):
        mid_head = over_middle(own_head)
    with jax.named_scope("tail_inward"):
        near_tail = inward(own_inner)
    with jax.named_scope("second_head_outward"):
        second_head = outward(
            pl.pallas_call(
                extend_kernel,
                in_specs=[whole()] * 2,
                out_specs=whole(),
                out_shape=listed(lead, NOTE),
                compiler_params=params(),
                cost_estimate=cost(0, 0),
                name="extend",
            )(mid_head, own_tail)
        )
    with jax.named_scope("end_head_over_middle"):
        end_head = over_middle(near_head)
    with jax.named_scope("third_head_outward"):
        third_head = outward(end_head)
    (mid_pool,) = pooled(head, near_tail, [end_head, token([near_tail], T_TAIL), second_mask, odd_mask])
    with jax.named_scope("far_mask"):
        far_mask = lax.ppermute(*passed([a_mask.T], [mid_pool]), "col", [(0, 3), (3, 0)])
    with jax.named_scope("pool_over_middle"):
        mid_pool = over_middle(mid_pool)
    table, over = pl.pallas_call(
        functools.partial(table_kernel, blocks),
        in_specs=[smem()] * 3 + [anywhere()] * 4,
        out_specs=[smem(), smem()],
        out_shape=[jax.ShapeDtypeStruct((5 * (blocks + 8),), jnp.int32), jax.ShapeDtypeStruct((1,), jnp.int32)],
        scratch_shapes=[
            pltpu.VMEM((4 * NOTE, blk), jnp.bfloat16),
            pltpu.VMEM((8, blk), jnp.int32),
            pltpu.SMEM((8, blk), jnp.int32),
            pltpu.SemaphoreType.DMA((4,)),
            pltpu.SemaphoreType.DMA,
        ],
        compiler_params=params(),
        name="table",
    )(where, by_column, far_mask, near_head, second_head, mid_head, end_head)

    here = [table, token([second_head], T_SECOND), token([second], T_RIGHT), odd_one] + b_masks[1:]
    mid_pool, second = passed([mid_pool, second], here)
    out_pools = pooled(lead, mid_pool, [])
    with jax.named_scope("pool_outward"):
        out_pools = [outward(part) for part in out_pools]
    with jax.named_scope("right_core_swap"):
        right = [b_blocks, odd_one, second, core_swap(second)]

    rows_shape = jax.ShapeDtypeStruct(((STEPS - 1) * kb * blk, bc * blk), jnp.bfloat16)
    met = pl.pallas_call(
        rows_kernel,
        in_specs=[smem()] * (2 + STEPS - 1) + [anywhere()] * (STEPS - 1),
        out_specs=whole(),
        out_shape=rows_shape,
        scratch_shapes=[
            pltpu.VMEM(((STEPS - 1) * kb, bc, blk, blk), jnp.bfloat16),
            pltpu.SMEM(((STEPS - 1) * kb,), jnp.int32),
            pltpu.SemaphoreType.DMA(((STEPS - 1) * kb,)),
        ],
        compiler_params=params(12),
        cost_estimate=cost(0, 1 << 20),
        name="rows",
    )(where, table, *b_masks[1:], *right[1:])
    third_here = token([third_head], T_THIRD)

    def fixed(x):
        return pl.BlockSpec(x.shape, lambda g: (0,) * x.ndim)

    wide_j = 2 if bc % 2 == 0 else 1
    arrived = [near_head, second_head, third_head, near_tail, mid_head, end_head, mid_pool]
    acc, out = pl.pallas_call(
        early_kernel,
        grid=(bc // wide_j,),
        in_specs=[smem()] * (4 + STEPS)
        + [fixed(x) for x in [a_blocks] + arrived]
        + [pl.BlockSpec((kb, wide_j, blk, blk), lambda g: (0, g, 0, 0))] * STEPS
        + [anywhere()] * 2,
        out_specs=[
            pl.BlockSpec((br * blk, wide_j * blk), lambda g: (0, g)),
            pl.BlockSpec((br, wide_j, blk, blk), lambda g: (0, g, 0, 0)),
        ],
        out_shape=[
            jax.ShapeDtypeStruct((br * blk, bc * blk), jnp.float32),
            jax.ShapeDtypeStruct((br, bc, blk, blk), jnp.bfloat16),
        ],
        scratch_shapes=[pltpu.VMEM((br * blk, (STEPS * kb + 1) * blk), a_blocks.dtype)],
        compiler_params=params(24),
        cost_estimate=cost(2 * STEPS * br * bc * kb * blk**3, 14 << 20),
        name="early",
    )(where, by_column, c_mask, table, *b_masks, a_blocks, *arrived, *right, met, third_here)

    for part, late in enumerate(out_pools):
        out, acc = pl.pallas_call(
            functools.partial(late_kernel, part * (pool // len(out_pools))),
            in_specs=[smem()] * 3 + [whole()] * 3 + [anywhere()],
            out_specs=[anywhere(), whole()],
            out_shape=[
                jax.ShapeDtypeStruct((br, bc, blk, blk), jnp.bfloat16),
                jax.ShapeDtypeStruct(acc.shape, acc.dtype),
            ],
            scratch_shapes=[
                pltpu.VMEM((br, bc, blk, blk), jnp.bfloat16),
                pltpu.SMEM((br,), jnp.int32),
                pltpu.SemaphoreType.DMA((br,)),
            ],
            input_output_aliases={5: 1, 6: 0},
            compiler_params=params(12),
            cost_estimate=cost(0, 1 << 20),
            name="late",
        )(where, c_mask, table, late, met, acc, out)

    def again(before):
        left = [live(a_blocks, by_column, by_column=True, after=(before,))]
        for _ in range(1, STEPS):
            left.append(from_behind(left[-1], "col", -1))
        odd = lax.axis_index("row") % 2 == 1
        held = [live(slab, mask, after=(before,)) for slab, mask in zip(right, b_masks)]
        ordered = [held[0], jnp.where(odd, held[3], held[1]), held[2], jnp.where(odd, held[1], held[3])]
        return filter_sum(dense_sum(left, ordered), c_mask, blk, before)

    return lax.cond(over[0] > 0, again, lambda before: before, out)


def on_device(a_blocks, a_mask, b_blocks, b_mask, c_mask):
    blocks = a_blocks.shape[0] * a_blocks.shape[1]
    fits = blocks % 32 == 0 and blocks <= a_blocks.shape[-1]
    if lax.axis_size("col") == STEPS and lax.axis_size("row") % 2 == 0 and fits:
        return sparse_product(a_blocks, a_mask, b_blocks, b_mask, c_mask)
    return dense_product(a_blocks, a_mask, b_blocks, b_mask, c_mask)


def solution(mesh):
    return jax.shard_map(
        on_device,
        mesh=mesh,
        in_specs=(
            P("row", "col", None, None),
            P("row", "col"),
            P("row", "col", None, None),
            P("row", "col"),
            P("row", "col"),
        ),
        out_specs=P("row", "col", None, None),
        check_vma=False,
    )
```

```python
import functools

import jax
import jax.numpy as jnp
from jax import lax
from jax.experimental import pallas as pl
from jax.experimental.pallas import tpu as pltpu
from jax.sharding import PartitionSpec as P

STEPS = 4
T_TAIL, T_SECOND, T_THIRD, T_RIGHT = 4, 3, 12, 1
GROUP = 3
NOTE = 16
MIB = 1024 * 1024


def slots(blocks):
    return blocks // 2, 3 * blocks // 4, 3 * blocks // 8, 9 * blocks // 16


def from_behind(array, axis, by):
    size = lax.axis_size(axis)
    return lax.ppermute(array, axis, [(i, (i + by) % size) for i in range(size)])


def smem():
    return pl.BlockSpec(memory_space=pltpu.SMEM)


def whole():
    return pl.BlockSpec(memory_space=pltpu.VMEM)


def anywhere():
    return pl.BlockSpec(memory_space=pl.ANY)


def params(mib=8):
    return pltpu.CompilerParams(vmem_limit_bytes=mib * MIB)


def cost(flops, nbytes):
    return pl.CostEstimate(flops=int(flops), bytes_accessed=int(nbytes), transcendentals=0)


def wide(a_ref):
    kb, blk = a_ref.shape[1], a_ref.shape[-1]
    return jnp.concatenate([a_ref[:, k].reshape(-1, blk) for k in range(kb)], axis=1)


def tall(b_ref):
    kb, bc = b_ref.shape[:2]
    return jnp.concatenate(
        [jnp.concatenate([b_ref[k, j] for j in range(bc)], axis=1) for k in range(kb)], axis=0
    )


def filtered(c_ref, i, j, block):
    return (block * c_ref[i, j].astype(jnp.float32)).astype(jnp.bfloat16)


def token_kernel(*refs):
    refs[-1][...] = jnp.zeros_like(refs[-1])


def token(seen, us):
    return pl.pallas_call(
        token_kernel,
        in_specs=[anywhere()] * len(seen),
        out_specs=whole(),
        out_shape=jax.ShapeDtypeStruct((8, 128), jnp.float32),
        compiler_params=params(),
        cost_estimate=cost(us * 1.1e9, 0),
        name="token",
    )(*seen)


def passed(arrays, seen=()):
    return pl.pallas_call(
        lambda *refs: None,
        in_specs=[anywhere()] * (len(arrays) + len(seen)),
        out_specs=[anywhere()] * len(arrays),
        out_shape=[jax.ShapeDtypeStruct(x.shape, x.dtype) for x in arrays],
        input_output_aliases={x: x for x in range(len(arrays))},
        compiler_params=params(),
        cost_estimate=cost(0, 0),
        name="passed",
    )(*arrays, *seen)


def live_kernel(by_column, mask_ref, x_ref, *refs):
    out_ref = refs[-1]
    i = pl.program_id(0)
    for j in range(x_ref.shape[1]):
        keep = mask_ref[j, i] if by_column else mask_ref[i, j]
        out_ref[0, j] = x_ref[0, j] * keep.astype(jnp.float32).astype(x_ref.dtype)


def live(blocks, mask, by_column=False, after=()):
    shape = (1,) + blocks.shape[1:]
    return pl.pallas_call(
        functools.partial(live_kernel, by_column),
        grid=(blocks.shape[0],),
        in_specs=[smem(), pl.BlockSpec(shape, lambda g: (g, 0, 0, 0))] + [anywhere()] * len(after),
        out_specs=pl.BlockSpec(shape, lambda g: (g, 0, 0, 0)),
        out_shape=jax.ShapeDtypeStruct(blocks.shape, blocks.dtype),
        compiler_params=params(),
        cost_estimate=cost(0, 4 * blocks.size),
        name="live",
    )(mask, blocks, *after)


def dense_kernel(*refs):
    a_refs, b_refs, acc_ref = refs[:STEPS], refs[STEPS:-1], refs[-1]
    total = None
    for a_ref, b_ref in zip(a_refs, b_refs):
        part = jnp.dot(wide(a_ref), tall(b_ref), preferred_element_type=jnp.float32)
        total = part if total is None else total + part
    acc_ref[...] = total


def dense_sum(left, right):
    br, kb, blk, _ = left[0].shape
    bc = right[0].shape[1]
    wide_j = 2 if bc % 2 == 0 else 1
    return pl.pallas_call(
        dense_kernel,
        grid=(bc // wide_j,),
        in_specs=[pl.BlockSpec((br, kb, blk, blk), lambda g: (0, 0, 0, 0))] * STEPS
        + [pl.BlockSpec((kb, wide_j, blk, blk), lambda g: (0, g, 0, 0))] * STEPS,
        out_specs=pl.BlockSpec((br * blk, wide_j * blk), lambda g: (0, g)),
        out_shape=jax.ShapeDtypeStruct((br * blk, bc * blk), jnp.float32),
        compiler_params=params(20),
        cost_estimate=cost(2 * STEPS * br * bc * kb * blk**3, 12 << 20),
        name="dense",
    )(*left, *right)


def filter_kernel(c_ref, acc_ref, *refs):
    out_ref = refs[-1]
    blk = out_ref.shape[-1]
    for j in range(out_ref.shape[1]):
        out_ref[0, j] = filtered(c_ref, pl.program_id(0), j, acc_ref[:, j * blk : (j + 1) * blk])


def filter_sum(total, c_mask, blk, *into):
    br, bc = c_mask.shape
    return pl.pallas_call(
        filter_kernel,
        grid=(br,),
        in_specs=[smem(), pl.BlockSpec((blk, bc * blk), lambda g: (g, 0))] + [anywhere()] * len(into),
        out_specs=pl.BlockSpec((1, bc, blk, blk), lambda g: (g, 0, 0, 0)),
        out_shape=jax.ShapeDtypeStruct((br, bc, blk, blk), jnp.bfloat16),
        input_output_aliases={2: 0} if into else {},
        compiler_params=params(),
        name="filter",
    )(c_mask, total, *into)


def dense_product(a_blocks, a_mask, b_blocks, b_mask, c_mask):
    left = [live(a_blocks, a_mask.T, by_column=True)]
    right = [live(b_blocks, b_mask)]
    for _ in range(1, STEPS):
        left.append(from_behind(left[-1], "col", -1))
        right.append(from_behind(right[-1], "row", -1))
    return filter_sum(dense_sum(left, right), c_mask, a_blocks.shape[-1])


def compact_kernel(mask_ref, a_ref, head_ref, inner_ref, tail_ref, n_ref, list_ref):
    br, kb, blk = a_ref.shape[:3]
    head, lead, inner, _ = slots(br * kb)
    lanes = lax.broadcasted_iota(jnp.int32, (NOTE, blk), 1)
    note = jnp.zeros((NOTE, blk), jnp.int32)
    count = jnp.int32(0)
    for k in range(kb):
        for i in range(br):
            list_ref[pl.ds(pl.multiple_of(count * blk, blk), blk), :] = a_ref[i, k]
            note = jnp.where(lanes == k * br + i, mask_ref[k, i], note)
            count = count + mask_ref[k, i]
    note = note.astype(jnp.float32).astype(jnp.bfloat16)
    head_ref[0 : head * blk, :] = list_ref[0 : head * blk, :]
    head_ref[head * blk :, :] = note
    inner_ref[...] = list_ref[head * blk : (head + inner) * blk, :]
    tail_ref[...] = list_ref[head * blk :, :]
    n_ref[0] = count


def extend_kernel(head_ref, tail_ref, out_ref):
    size = head_ref.shape[0] - NOTE
    more = out_ref.shape[0] - head_ref.shape[0]
    out_ref[0:size, :] = head_ref[0:size, :]
    out_ref[size : size + more, :] = tail_ref[0:more, :]
    out_ref[size + more :, :] = head_ref[size:, :]


def pool_kernel(parts, skip, n_ref, tail_ref, more_ref, *refs):
    outs, line = refs[-1 - parts : -1], refs[-1]
    size, blk = outs[0].shape
    first = skip * blk - tail_ref.shape[0]
    own = tail_ref.shape[0] - first
    line[0:own, :] = tail_ref[first:, :]
    at = pl.multiple_of(jnp.maximum(n_ref[0] - skip, 0) * blk, blk)
    line[pl.ds(at, more_ref.shape[0]), :] = more_ref[...]
    for part, out_ref in enumerate(outs):
        out_ref[...] = line[part * size : (part + 1) * size, :]


def table_kernel(blocks, where_ref, own_ref, far_ref, *refs):
    notes, (table_ref, over_ref, note_ref, wide_ref, mask_ref, sems, sem) = refs[:4], refs[4:]
    copies = [
        pltpu.make_async_copy(
            ref.at[pl.ds(ref.shape[0] - NOTE, NOTE), :], note_ref.at[pl.ds(m * NOTE, NOTE), :], sems.at[m]
        )
        for m, ref in enumerate(notes)
    ]
    for copy in copies:
        copy.start()
    for copy in copies:
        copy.wait()
    for m in range(len(notes)):
        wide_ref[m : m + 1, :] = note_ref[m * NOTE : (m + 1) * NOTE, :].astype(jnp.float32).astype(jnp.int32)[0:1, :]
    down = pltpu.make_async_copy(wide_ref, mask_ref, sem)
    down.start()
    down.wait()

    none, apart = STEPS * blocks, blocks + 8
    head, lead, inner, pool = slots(blocks)
    z = where_ref[0]
    at_end = jnp.logical_or(z == 0, z == 3)
    near = 1 + 2 * (z % 2)
    flip = where_ref[1] % 2 == 1

    def place_of(step):
        return jnp.where(flip, 4 - step, step)

    def noted(m):
        return lambda b: mask_ref[m, b]

    def far(b):
        return jnp.where(at_end, far_ref[b // own_ref.shape[1], b % own_ref.shape[1]], mask_ref[3, b])

    def fill(base, place, live):
        def body(b, count):
            table_ref[count] = place * blocks + b
            return count + live(b)

        count = lax.fori_loop(0, blocks, body, jnp.int32(base), unroll=8)

        def pad(p, carry):
            table_ref[p] = none
            return carry

        lax.fori_loop(count, base + blocks, pad, 0)
        return count - base

    first = fill(0, place_of(near), noted(0))
    second = fill(apart, jnp.where(at_end, 2, place_of(4 - near)), noted(jnp.where(at_end, 1, 2)))
    third = fill(2 * apart, jnp.where(at_end, place_of(4 - near), 2), far)

    def append(base, begin, length, at):
        def body(p, at):
            table_ref[at] = table_ref[base + p]
            return at + 1

        return lax.fori_loop(begin, length, body, at)

    at = append(0, jnp.where(at_end, lead, blocks), first, jnp.int32(3 * apart))
    at = append(apart, head, second, at)
    at = append(2 * apart, head, third, at)

    def pad(p, carry):
        table_ref[p] = none
        return carry

    lax.fori_loop(at, 3 * apart + pool, pad, 0)

    own = jnp.int32(0)
    for k in range(own_ref.shape[0]):
        for i in range(own_ref.shape[1]):
            own = own + own_ref[k, i]

    def past(n, by):
        return jnp.maximum(n - by, 0)

    def overflows(next_one, middle, far):
        pooled = past(next_one, lead) + past(middle, head) + past(far, head)
        return jnp.logical_or(pooled > pool, far > head + inner)

    ends_view = jnp.logical_or(overflows(first, second, third), overflows(second, first, own))
    middles_view = jnp.logical_or(overflows(own, second, third), overflows(second, own, first))
    over_ref[0] = jnp.where(jnp.where(at_end, ends_view, middles_view), 1, 0).astype(jnp.int32)


def masked_tall(mask_ref, b_ref, j0):
    kb, bc = b_ref.shape[:2]

    def block(k, j):
        return b_ref[k, j] * mask_ref[k, j0 + j].astype(jnp.float32).astype(b_ref.dtype)

    return jnp.concatenate([jnp.concatenate([block(k, j) for j in range(bc)], axis=1) for k in range(kb)], axis=0)


def early_kernel(where_ref, mask_ref, c_ref, table_ref, *refs):
    b_masks, a_ref, refs = refs[:STEPS], refs[STEPS], refs[STEPS + 1 :]
    near_ref, outs, mids, refs = refs[0], refs[1:3], refs[3:7], refs[7:-5] + refs[-3:]
    b_refs, (acc_ref, out_ref, left_ref) = refs[:STEPS], refs[STEPS:]
    br, kb, blk, _ = a_ref.shape
    blocks = br * kb
    apart = blocks + 8
    head, lead, inner, pool = slots(blocks)
    z = where_ref[0]
    at_end = jnp.logical_or(z == 0, z == 3)

    def scatter(ref, first, length, at=0):
        def body(b, carry):
            place = table_ref[first + b]
            row = pl.multiple_of((place % br) * blk, blk)
            column = pl.multiple_of((place // br) * blk, blk)
            left_ref[pl.ds(row, blk), pl.ds(column, blk)] = ref[pl.ds(pl.multiple_of((at + b) * blk, blk), blk), :]
            return carry

        lax.fori_loop(0, length, body, 0, unroll=2)

    @pl.when(pl.program_id(0) == 0)
    def _():
        for k in range(kb):
            for i in range(br):
                left_ref[i * blk : (i + 1) * blk, k * blk : (k + 1) * blk] = a_ref[i, k] * mask_ref[k, i].astype(
                    jnp.float32
                ).astype(jnp.bfloat16)
        left_ref[:, kb * blk :] = jnp.zeros((br * blk, left_ref.shape[1] - kb * blk), jnp.bfloat16)
        scatter(near_ref, 0, head)

        @pl.when(at_end)
        def _():
            scatter(outs[0], apart, head)
            scatter(outs[0], head, lead - head, head)
            scatter(outs[1], 2 * apart, head)

        @pl.when(jnp.logical_not(at_end))
        def _():
            scatter(mids[0], head, inner)
            scatter(mids[1], apart, head)
            scatter(mids[2], 2 * apart, head)
            scatter(mids[3], 3 * apart, pool)

    j0 = pl.program_id(0) * out_ref.shape[1]
    total = None
    for t in range(STEPS):
        part = jnp.dot(
            left_ref[:, t * kb * blk : (t + 1) * kb * blk],
            masked_tall(b_masks[t], b_refs[t], j0),
            preferred_element_type=jnp.float32,
        )
        total = part if total is None else total + part
    acc_ref[...] = total
    for i in range(br):
        for j in range(out_ref.shape[1]):
            out_ref[i, j] = filtered(c_ref, i, j0 + j, total[i * blk : (i + 1) * blk, j * blk : (j + 1) * blk])


def rows_kernel(where_ref, table_ref, *refs):
    b_masks, refs = refs[: STEPS - 1], refs[STEPS - 1 :]
    b_refs, (rows_ref, b_ref, need_ref, sems) = refs[: STEPS - 1], refs[STEPS - 1 :]
    _, bc, blk, _ = b_ref.shape
    kb = b_refs[0].shape[0]
    br = (table_ref.shape[0] // 5 - 8) // kb
    _, _, _, pool = slots(kb * br)
    first = 3 * (kb * br + 8)
    at_end = jnp.logical_or(where_ref[0] == 0, where_ref[0] == 3)

    def clear(r, carry):
        need_ref[r] = 0
        return carry

    def mark(b, carry):
        place = table_ref[first + b]

        @pl.when(place < STEPS * kb * br)
        def _():
            need_ref[place // br - kb] = 1

        return carry

    lax.fori_loop(0, (STEPS - 1) * kb, clear, 0)
    lax.fori_loop(0, jnp.where(at_end, pool, 0), mark, 0)
    copies = [
        pltpu.make_async_copy(b_refs[r // kb].at[r % kb], b_ref.at[r], sems.at[r]) for r in range((STEPS - 1) * kb)
    ]

    def when(r, act):
        @pl.when(need_ref[r] > 0)
        def _():
            act()

    for r, copy in enumerate(copies):
        when(r, copy.start)
    for r, copy in enumerate(copies):
        when(r, copy.wait)
    for slab, mask_ref in enumerate(b_masks):

        def fill(k, carry):
            r = slab * kb + k

            @pl.when(need_ref[r] > 0)
            def _():
                for j in range(bc):
                    keep = mask_ref[k, j].astype(jnp.float32).astype(jnp.bfloat16)
                    rows_ref[pl.ds(pl.multiple_of(r * blk, blk), blk), j * blk : (j + 1) * blk] = b_ref[r, j] * keep

            return carry

        lax.fori_loop(0, kb, fill, 0)


def late_kernel(begin, where_ref, c_ref, table_ref, late_ref, rows_ref, acc_in, _, out_ref, acc_ref, row_ref, last_ref, sems):
    del acc_in
    br, bc, blk, _ = out_ref.shape
    kb = rows_ref.shape[0] // blk // (STEPS - 1)
    none = STEPS * kb * br
    size = late_ref.shape[0] // blk
    first = 3 * (kb * br + 8) + begin
    at_end = jnp.logical_or(where_ref[0] == 0, where_ref[0] == 3)

    def clear(i, carry):
        last_ref[i] = -1
        return carry

    def mark(b, live):
        place = table_ref[first + b]

        @pl.when(place < none)
        def _():
            last_ref[place % br] = b

        return live + jnp.where(place < none, 1, 0)

    def go(i):
        return pltpu.make_async_copy(row_ref.at[i], out_ref.at[i], sems.at[i])

    def add(group, carry):
        b0 = group * GROUP
        places = [table_ref[first + b0 + x] for x in range(GROUP)]
        products = []
        for x, place in enumerate(places):
            r = jnp.minimum(place // br - kb, (STEPS - 1) * kb - 1)
            products.append(
                jnp.dot(
                    late_ref[pl.ds(pl.multiple_of((b0 + x) * blk, blk), blk), :],
                    rows_ref[pl.ds(pl.multiple_of(r * blk, blk), blk), :],
                    preferred_element_type=jnp.float32,
                )
            )
        for x, (place, product) in enumerate(zip(places, products)):
            i = place % br
            row = pl.multiple_of(i * blk, blk)

            @pl.when(place < none)
            def _():
                acc_ref[pl.ds(row, blk), :] += product

            @pl.when(jnp.logical_and(place < none, last_ref[i] == b0 + x))
            def _():
                for j in range(bc):
                    row_ref[i, j] = filtered(c_ref, i, j, acc_ref[pl.ds(row, blk), j * blk : (j + 1) * blk])
                go(i).start()

        return carry

    def settle(i, carry):
        @pl.when(last_ref[i] >= 0)
        def _():
            go(i).wait()

        return carry

    lax.fori_loop(0, br, clear, 0)
    live = lax.fori_loop(0, jnp.where(at_end, size, 0), mark, jnp.int32(0))
    lax.fori_loop(0, (live + GROUP - 1) // GROUP, add, 0)
    lax.fori_loop(0, br, settle, 0)


def sparse_product(a_blocks, a_mask, b_blocks, b_mask, c_mask):
    br, kb, blk, _ = a_blocks.shape
    bc = b_blocks.shape[1]
    blocks = br * kb
    head, lead, inner, pool = slots(blocks)
    rows = lax.axis_size("row")
    where = jnp.stack([lax.axis_index("col"), lax.axis_index("row")]).astype(jnp.int32)
    by_column = a_mask.T

    def outward(x):
        return lax.ppermute(x, "col", [(1, 0), (2, 3)])

    def end_swap(x):
        return lax.ppermute(x, "col", [(0, 1), (1, 0), (2, 3), (3, 2)])

    def inward(x):
        return lax.ppermute(x, "col", [(0, 1), (3, 2)])

    def over_middle(x):
        return lax.ppermute(x, "col", [(1, 2), (2, 1)])

    def two_up(x):
        return from_behind(x, "row", -2)

    def odd_up(x):
        return lax.ppermute(x, "row", [((r + 1 + 2 * (r % 2)) % rows, r) for r in range(rows)])

    def core_swap(x):
        return lax.ppermute(x, "row", [(r, r ^ 1) for r in range(rows)])

    def listed(slot_count, note=0):
        return jax.ShapeDtypeStruct((slot_count * blk + note, blk), a_blocks.dtype)

    with jax.named_scope("right_two_up"):
        second = two_up(b_blocks)
    with jax.named_scope("right_odd_up"):
        odd_one = odd_up(b_blocks)
    with jax.named_scope("right_masks"):
        second_mask, odd_mask = two_up(b_mask), odd_up(b_mask)
        b_masks = [b_mask, odd_mask, second_mask, core_swap(second_mask)]

    own_head, own_inner, own_tail, n = pl.pallas_call(
        compact_kernel,
        in_specs=[smem(), whole()],
        out_specs=[whole(), whole(), whole(), smem()],
        out_shape=[
            listed(head, NOTE),
            listed(inner),
            listed(blocks - head),
            jax.ShapeDtypeStruct((1,), jnp.int32),
        ],
        scratch_shapes=[pltpu.VMEM((blocks * blk, blk), a_blocks.dtype)],
        compiler_params=params(),
        cost_estimate=cost(0, 6 * blocks * blk * blk),
        name="compact",
    )(by_column, a_blocks)

    def pooled(skip, more, seen, parts=1):
        own = blocks - skip
        return pl.pallas_call(
            functools.partial(pool_kernel, parts, skip),
            in_specs=[smem(), whole(), whole()] + [anywhere()] * len(seen),
            out_specs=[whole()] * parts,
            out_shape=[listed(pool // parts)] * parts,
            scratch_shapes=[pltpu.VMEM((own * blk + more.shape[0], blk), a_blocks.dtype)],
            compiler_params=params(),
            cost_estimate=cost(0, 6 * pool * blk * blk),
            name="pool",
        )(n, own_tail, more, *seen)

    with jax.named_scope("head_end_swap"):
        near_head = end_swap(own_head)
    with jax.named_scope("head_over_middle"):
        mid_head = over_middle(own_head)
    with jax.named_scope("tail_inward"):
        near_tail = inward(own_inner)
    with jax.named_scope("second_head_outward"):
        second_head = outward(
            pl.pallas_call(
                extend_kernel,
                in_specs=[whole()] * 2,
                out_specs=whole(),
                out_shape=listed(lead, NOTE),
                compiler_params=params(),
                cost_estimate=cost(0, 0),
                name="extend",
            )(mid_head, own_tail)
        )
    with jax.named_scope("end_head_over_middle"):
        end_head = over_middle(near_head)
    with jax.named_scope("third_head_outward"):
        third_head = outward(end_head)
    (mid_pool,) = pooled(head, near_tail, [token([near_tail], T_TAIL), second_mask, odd_mask])
    (mid_pool,) = passed([mid_pool], [end_head])
    with jax.named_scope("far_mask"):
        far_mask = lax.ppermute(*passed([a_mask.T], [mid_pool]), "col", [(0, 3), (3, 0)])
    with jax.named_scope("pool_over_middle"):
        mid_pool = over_middle(mid_pool)
    table, over = pl.pallas_call(
        functools.partial(table_kernel, blocks),
        in_specs=[smem()] * 3 + [anywhere()] * 4,
        out_specs=[smem(), smem()],
        out_shape=[jax.ShapeDtypeStruct((5 * (blocks + 8),), jnp.int32), jax.ShapeDtypeStruct((1,), jnp.int32)],
        scratch_shapes=[
            pltpu.VMEM((4 * NOTE, blk), jnp.bfloat16),
            pltpu.VMEM((8, blk), jnp.int32),
            pltpu.SMEM((8, blk), jnp.int32),
            pltpu.SemaphoreType.DMA((4,)),
            pltpu.SemaphoreType.DMA,
        ],
        compiler_params=params(),
        name="table",
    )(where, by_column, far_mask, near_head, second_head, mid_head, end_head)

    here = [table, token([second_head], T_SECOND), token([second], T_RIGHT), odd_one] + b_masks[1:]
    mid_pool, second = passed([mid_pool, second], here)
    out_pools = pooled(lead, mid_pool, [])
    with jax.named_scope("pool_outward"):
        out_pools = [outward(part) for part in out_pools]
    with jax.named_scope("right_core_swap"):
        right = [b_blocks, odd_one, second, core_swap(second)]

    rows_shape = jax.ShapeDtypeStruct(((STEPS - 1) * kb * blk, bc * blk), jnp.bfloat16)
    met = pl.pallas_call(
        rows_kernel,
        in_specs=[smem()] * (2 + STEPS - 1) + [anywhere()] * (STEPS - 1),
        out_specs=whole(),
        out_shape=rows_shape,
        scratch_shapes=[
            pltpu.VMEM(((STEPS - 1) * kb, bc, blk, blk), jnp.bfloat16),
            pltpu.SMEM(((STEPS - 1) * kb,), jnp.int32),
            pltpu.SemaphoreType.DMA(((STEPS - 1) * kb,)),
        ],
        compiler_params=params(12),
        cost_estimate=cost(0, 1 << 20),
        name="rows",
    )(where, table, *b_masks[1:], *right[1:])
    third_here = token([third_head], T_THIRD)

    def fixed(x):
        return pl.BlockSpec(x.shape, lambda g: (0,) * x.ndim)

    wide_j = 2 if bc % 2 == 0 else 1
    arrived = [near_head, second_head, third_head, near_tail, mid_head, end_head, mid_pool]
    acc, out = pl.pallas_call(
        early_kernel,
        grid=(bc // wide_j,),
        in_specs=[smem()] * (4 + STEPS)
        + [fixed(x) for x in [a_blocks] + arrived]
        + [pl.BlockSpec((kb, wide_j, blk, blk), lambda g: (0, g, 0, 0))] * STEPS
        + [anywhere()] * 2,
        out_specs=[
            pl.BlockSpec((br * blk, wide_j * blk), lambda g: (0, g)),
            pl.BlockSpec((br, wide_j, blk, blk), lambda g: (0, g, 0, 0)),
        ],
        out_shape=[
            jax.ShapeDtypeStruct((br * blk, bc * blk), jnp.float32),
            jax.ShapeDtypeStruct((br, bc, blk, blk), jnp.bfloat16),
        ],
        scratch_shapes=[pltpu.VMEM((br * blk, (STEPS * kb + 1) * blk), a_blocks.dtype)],
        compiler_params=params(24),
        cost_estimate=cost(2 * STEPS * br * bc * kb * blk**3, 14 << 20),
        name="early",
    )(where, by_column, c_mask, table, *b_masks, a_blocks, *arrived, *right, met, third_here)

    for part, late in enumerate(out_pools):
        out, acc = pl.pallas_call(
            functools.partial(late_kernel, part * (pool // len(out_pools))),
            in_specs=[smem()] * 3 + [whole()] * 3 + [anywhere()],
            out_specs=[anywhere(), whole()],
            out_shape=[
                jax.ShapeDtypeStruct((br, bc, blk, blk), jnp.bfloat16),
                jax.ShapeDtypeStruct(acc.shape, acc.dtype),
            ],
            scratch_shapes=[
                pltpu.VMEM((br, bc, blk, blk), jnp.bfloat16),
                pltpu.SMEM((br,), jnp.int32),
                pltpu.SemaphoreType.DMA((br,)),
            ],
            input_output_aliases={5: 1, 6: 0},
            compiler_params=params(12),
            cost_estimate=cost(0, 1 << 20),
            name="late",
        )(where, c_mask, table, late, met, acc, out)

    def again(before):
        left = [live(a_blocks, by_column, by_column=True, after=(before,))]
        for _ in range(1, STEPS):
            left.append(from_behind(left[-1], "col", -1))
        odd = lax.axis_index("row") % 2 == 1
        held = [live(slab, mask, after=(before,)) for slab, mask in zip(right, b_masks)]
        ordered = [held[0], jnp.where(odd, held[3], held[1]), held[2], jnp.where(odd, held[1], held[3])]
        return filter_sum(dense_sum(left, ordered), c_mask, blk, before)

    return lax.cond(over[0] > 0, again, lambda before: before, out)


def on_device(a_blocks, a_mask, b_blocks, b_mask, c_mask):
    blocks = a_blocks.shape[0] * a_blocks.shape[1]
    fits = blocks % 32 == 0 and blocks <= a_blocks.shape[-1]
    if lax.axis_size("col") == STEPS and lax.axis_size("row") % 2 == 0 and fits:
        return sparse_product(a_blocks, a_mask, b_blocks, b_mask, c_mask)
    return dense_product(a_blocks, a_mask, b_blocks, b_mask, c_mask)


def solution(mesh):
    return jax.shard_map(
        on_device,
        mesh=mesh,
        in_specs=(
            P("row", "col", None, None),
            P("row", "col"),
            P("row", "col", None, None),
            P("row", "col"),
            P("row", "col"),
        ),
        out_specs=P("row", "col", None, None),
        check_vma=False,
    )
```
